128 devices in a mesh: section: 2 (over x_lo), fsdp: 16 (over z, y), rep: 4 (over x_hi, core).
Axes of the slice: x: 4 (x_hi: 2, x_lo: 2; x = x_hi * 2 + x_lo), y: 4, z: 4, core: 2. Of those that a mesh axis runs over, the one named last changes fastest.
Arguments:
- patch_tokens: bfloat16 [16, 1024, 1024], P('rep', 'fsdp'), may hold values from -6 to 6
- out_grad: bfloat16 [16, 1024, 1024], P('rep', 'fsdp'), may hold values from -6 to 6
- batch_counts: int32 [4, 2], P('rep'), may hold values from 1 to 2, as said below
- norm_gain: bfloat16 [2, 2, 1024], P('section', None, 'fsdp'), may hold values from 0.25 to 1.75
- norm_bias: bfloat16 [2, 2, 1024], P('section', None, 'fsdp'), may hold values from -1.75 to 1.75
- qkv_weight: bfloat16 [2, 1024, 3072], P('section', 'fsdp'), may hold values from -0.1875 to 0.1875
- qv_bias: bfloat16 [2, 2, 1024], P('section', None, 'fsdp'), may hold values from -1.75 to 1.75
- proj_weight: bfloat16 [2, 1024, 1024], P('section', 'fsdp'), may hold values from -3 to 3
- fc1_weight: bfloat16 [2, 1024, 4096], P('section', 'fsdp'), may hold values from -0.1875 to 0.1875
- fc1_bias: bfloat16 [2, 4096], P('section', 'fsdp'), may hold values from -3 to 3
- fc2_weight: bfloat16 [2, 4096, 1024], P('section', 'fsdp'), may hold values from -0.09375 to 0.09375
- out_bias: bfloat16 [2, 2, 1024], P('section', None, 'fsdp'), may hold values from -1.75 to 1.75
- layer_scale: bfloat16 [2, 2, 1024], P('section', None, 'fsdp'), may hold values from 0.29882812 to 1.1953125
Outputs:
- block_out: bfloat16 [2, 16, 1024, 1024], P('section', 'rep', 'fsdp')
- in_grad: bfloat16 [2, 16, 1024, 1024], P('section', 'rep', 'fsdp')
- norm_gain_grad: float32 [2, 2, 1024], P('section', None, 'fsdp')
- norm_bias_grad: float32 [2, 2, 1024], P('section', None, 'fsdp')
- qkv_weight_grad: float32 [2, 1024, 3072], P('section', 'fsdp')
- qv_bias_grad: float32 [2, 2, 1024], P('section', None, 'fsdp')
- proj_weight_grad: float32 [2, 1024, 1024], P('section', 'fsdp')
- fc1_weight_grad: float32 [2, 1024, 4096], P('section', 'fsdp')
- fc1_bias_grad: float32 [2, 4096], P('section', 'fsdp')
- fc2_weight_grad: float32 [2, 4096, 1024], P('section', 'fsdp')
- out_bias_grad: float32 [2, 2, 1024], P('section', None, 'fsdp')
- layer_scale_grad: float32 [2, 2, 1024], P('section', None, 'fsdp')
The draws below stay inside these ranges and needn't reach their ends.
Inputs may be any that keep to these rules, and one draw needn't show every extreme that they name: Micro-batch m of replica r holds batch_counts[r, m] live images in its first slots; the first micro-batch of every replica is full, and the last micro-batch of one replica holds a single live image.
All inputs are finite; a program needn't handle non-finite values.
Results may differ from the reference program's by a relative error of at most 0.019.
Values may be sent and summed in bfloat16 or wider, within the bound.
No kernel may reach another device: no remote copies, remote signals or barrier semaphores. Data moves between devices by JAX's collectives and lax.ppermute only.
A program may use at most 192 MiB of HBM per device.

```python
import math
import jax
import jax.numpy as jnp
from jax import lax

D = 1024
HEADS = 16
HEAD_DIM = 64
FF = 4096
SEQ = 1024
MB = 2
IMG_MB = 2
IMAGES = 16
N_REP = 4


def draw_batch_counts(key, part):
    key = jax.random.fold_in(key, 7)
    count_key = jax.random.fold_in(key, 1)
    pick_key = jax.random.fold_in(key, 2)
    drawn = jax.random.randint(count_key, (N_REP, MB), 1, IMG_MB + 1)
    chosen = jax.random.randint(pick_key, (), 0, N_REP)
    leading = jnp.arange(MB)[None, :] == 0
    trailing = (jnp.arange(MB)[None, :] == MB - 1) & (jnp.arange(N_REP)[:, None] == chosen)
    return jnp.where(leading, IMG_MB, jnp.where(trailing, 1, drawn)).astype(jnp.int32)


def block_scale(key, dims, pieces, smallest, top_value):
    factor_of, own = 1.0, jax.random.fold_in(key, 6)
    for position, blocks in pieces:
        steps = jnp.exp(jax.random.uniform(jax.random.fold_in(own, position), (blocks,), jnp.float32, smallest / len(pieces), top_value / len(pieces)))
        factor_of = factor_of * jnp.repeat(steps, dims[position] // blocks).reshape([-1 if axis == position else 1 for axis in range(len(dims))])
    return factor_of


def noise(stream_key, extent, width, most, split=(), held_as=jnp.bfloat16):
    values = width * jax.random.normal(stream_key, extent, jnp.float32)
    if split:
        values = values * block_scale(stream_key, extent, split, -0.22, 0.18)
    return jnp.clip(values, -most, most).astype(held_as)


def setup_inputs(seed: int = 0) -> dict:
    arg_keys = jax.random.split(jax.random.key(seed), 14)
    return {
        "patch_tokens": noise(arg_keys[0], (IMAGES, SEQ, D), 1.0, 6.0, ((0, 4), (1, 16))),
        "out_grad": noise(arg_keys[1], (IMAGES, SEQ, D), 1.0, 6.0, ((0, 4), (1, 16))),
        "batch_counts": draw_batch_counts(jax.random.fold_in(arg_keys[13], 71), 0),
        "norm_gain": jnp.clip(1.0 + 0.15 * jax.random.normal(arg_keys[3], (2, 2, D), jnp.float32), 0.25, 1.75).astype(jnp.bfloat16),
        "norm_bias": noise(arg_keys[4], (2, 2, D), 0.3, 1.75, ((0, 2), (2, 16))),
        "qkv_weight": noise(arg_keys[5], (2, D, 3 * D), D ** -0.5, 0.1875, ((0, 2), (1, 16))),
        "qv_bias": noise(arg_keys[6], (2, 2, D), 0.3, 1.75, ((0, 2), (2, 16))),
        "proj_weight": noise(arg_keys[7], (2, D, D), (max(D // 256, 1)) ** -0.5, 3.0, ((0, 2), (1, 16))),
        "fc1_weight": noise(arg_keys[8], (2, D, FF), D ** -0.5, 0.1875, ((0, 2), (1, 16))),
        "fc1_bias": noise(arg_keys[9], (2, FF), 0.5, 3.0, ((0, 2), (1, 16))),
        "fc2_weight": noise(arg_keys[10], (2, FF, D), FF ** -0.5, 0.09375, ((0, 2), (1, 16))),
        "out_bias": noise(arg_keys[11], (2, 2, D), 0.3, 1.75, ((0, 2), (2, 16))),
        "layer_scale": jnp.clip(jnp.exp(math.log(1.1953125) - 1.3862944 * jax.random.uniform(arg_keys[12], (2, 2, D), jnp.float32) ** block_scale(arg_keys[12], (2, 2, D), ((0, 2), (2, 16)), -0.2, 0.2)), 0.29882812, 1.1953125).astype(jnp.bfloat16),
    }


epsilon = 1e-06
highest = lax.Precision.HIGHEST

@jax.custom_vjp
def low(v):
    return lax.optimization_barrier(v.astype(jnp.bfloat16)).astype(jnp.float32)

@jax.custom_vjp
def low_back(v):
    return v

def low_keep(v):
    return (low(v), None)

def low_pass(kept, grad):
    return (grad,)

def back_keep(v):
    return (v, None)

def back_low(kept, grad):
    return (low(grad),)
low.defvjp(low_keep, low_pass)
low_back.defvjp(back_keep, back_low)

def normalize(values, scale_vec, shift_vec):
    row_mean = lax.optimization_barrier(jnp.mean(values, axis=-1, keepdims=True))
    centred = values - row_mean
    spread = lax.optimization_barrier(jnp.mean(centred * centred, axis=-1, keepdims=True))
    return centred * lax.rsqrt(spread + epsilon) * scale_vec + shift_vec

def layer(inputs, params):
    norm_gains, norm_shifts, qkv_matrix, in_biases, proj_matrix, up_matrix, hidden_bias, down_matrix, out_biases, scales = params
    length = inputs.shape[0]
    normed_one = low(normalize(inputs, norm_gains[0], norm_shifts[0]))
    joined = jnp.dot(normed_one, qkv_matrix, precision=highest)
    queries = low_back(low(joined[:, :D] + in_biases[0]))
    key_block = low_back(low(joined[:, D:2 * D]))
    value_block = low_back(low(joined[:, 2 * D:] + in_biases[1]))
    query_heads = queries.reshape(length, HEADS, HEAD_DIM)
    key_heads = key_block.reshape(length, HEADS, HEAD_DIM)
    value_heads = value_block.reshape(length, HEADS, HEAD_DIM)
    scores = low_back(jnp.einsum('qhe,khe->hqk', query_heads, key_heads, precision=highest) * HEAD_DIM ** (-0.5))
    weighting = low(jax.nn.softmax(scores, axis=-1))
    attended = jnp.einsum('hqk,khe->qhe', weighting, value_heads, precision=highest).reshape(length, D)
    attended = low_back(low(attended))
    branch = low_back(jnp.dot(attended, proj_matrix, precision=highest) + out_biases[0])
    middle = inputs + scales[0] * branch
    normed_two = low(normalize(middle, norm_gains[1], norm_shifts[1]))
    before = low_back(jnp.dot(normed_two, up_matrix, precision=highest) + hidden_bias)
    activated = low(jax.nn.gelu(before, approximate=False))
    branch_two = low_back(jnp.dot(activated, down_matrix, precision=highest) + out_biases[1])
    return middle + scales[1] * branch_two

def reference(patch_tokens, out_grad, batch_counts, norm_gain, norm_bias, qkv_weight, qv_bias, proj_weight, fc1_weight, fc1_bias, fc2_weight, out_bias, layer_scale):
    stacks = (norm_gain, norm_bias, qkv_weight, qv_bias, proj_weight, fc1_weight, fc1_bias, fc2_weight, out_bias, layer_scale)
    first_layer = tuple((stacked[0].astype(jnp.float32) for stacked in stacks))
    second_layer = tuple((stacked[1].astype(jnp.float32) for stacked in stacks))
    image_ids = jnp.arange(IMAGES, dtype=jnp.int32)
    slot_counts = batch_counts.reshape(-1)[image_ids // IMG_MB]
    live_mask = (image_ids % IMG_MB < slot_counts).astype(jnp.float32)

    def one_image(running, record):
        tokens, grad_tokens, live_flag = record
        inputs = tokens.astype(jnp.float32)
        handed_raw, back_first = jax.vjp(layer, inputs, first_layer)
        handed = low(handed_raw)
        result, back_second = jax.vjp(layer, handed, second_layer)
        grad_mid, grads_second = back_second(grad_tokens.astype(jnp.float32) * live_flag)
        grad_sent = low(grad_mid)
        grad_inputs, grads_first = back_first(grad_sent)
        running = (jax.tree.map(jnp.add, running[0], grads_first), jax.tree.map(jnp.add, running[1], grads_second))
        outputs = (handed.astype(jnp.bfloat16), result.astype(jnp.bfloat16), grad_inputs.astype(jnp.bfloat16), grad_sent.astype(jnp.bfloat16))
        return (running, outputs)
    start = (jax.tree.map(jnp.zeros_like, first_layer), jax.tree.map(jnp.zeros_like, second_layer))
    totals, outputs = lax.scan(one_image, start, (patch_tokens, out_grad, live_mask))
    block_out = jnp.stack([outputs[0], outputs[1]])
    in_grad = jnp.stack([outputs[2], outputs[3]])
    grads = tuple((jnp.stack([totals[0][k], totals[1][k]]) for k in range(10)))
    return (block_out, in_grad, grads[0], grads[1], grads[2], grads[3], grads[4], grads[5], grads[6], grads[7], grads[8], grads[9])
```

```python
import jax
import jax.numpy as jnp
from jax import lax
from jax.experimental import pallas as pl
from jax.experimental.pallas import tpu as pltpu
from jax.sharding import Mesh, PartitionSpec as P

HEAD_DIM = 64
IMG_MB = 2
PAIR = 2 * HEAD_DIM
EPSILON = 1e-06

FSDP = ("z", "yh", "yl")
REP = ("xhi", "core")
bf16 = jnp.bfloat16
f32 = jnp.float32


def dot(a, b, dims):
    return lax.dot_general(a, b, (dims, ((), ())), preferred_element_type=f32)


def mm(a, b):
    return dot(a, b, ((1,), (0,)))


def mm_t(a, b):
    return dot(a, b, ((1,), (1,)))


def t_mm(a, b):
    return dot(a, b, ((0,), (0,)))


def swap(value, axis):
    return lax.ppermute(value, axis, [(0, 1), (1, 0)])


def attend_kernel(q_ref, own_ref, mate_ref, near_ref, far_ref, out_ref, log_ref):
    rows = q_ref.shape[0]
    both = [r[...] for r in (own_ref, mate_ref, near_ref, far_ref)]
    keys = jnp.concatenate([b[:, :PAIR] for b in both], axis=0)
    values = jnp.concatenate([b[:, PAIR:] for b in both], axis=0)
    queries = q_ref[...] * jnp.asarray(HEAD_DIM**-0.5, bf16)
    lane = lax.broadcasted_iota(jnp.int32, (rows, PAIR), 1)
    outs = []
    for head in range(2):
        mine = (lane >= head * HEAD_DIM) & (lane < (head + 1) * HEAD_DIM)
        picked = jnp.where(mine, queries, jnp.zeros_like(queries))
        scores = mm_t(keys, picked)
        top = jnp.max(scores, axis=0, keepdims=True)
        raised = jnp.exp(scores - top)
        total = jnp.sum(raised, axis=0, keepdims=True)
        out = t_mm(values, raised.astype(bf16))
        outs.append(out * (1.0 / total))
        log_ref[0, head : head + 1, :] = top + jnp.log(total)
    row = lax.broadcasted_iota(jnp.int32, (PAIR, rows), 0)
    joined = jnp.where(row < HEAD_DIM, outs[0], outs[1])
    out_ref[...] = joined.T.astype(bf16)


def attend_back_kernel(
    q_ref, own_ref, mate_ref, near_ref, far_ref, grad_ref, log_ref, dq_ref, *dkv_refs
):
    rows = q_ref.shape[0]
    both = [r[...] for r in (own_ref, mate_ref, near_ref, far_ref)]
    keys = jnp.concatenate([b[:, :PAIR] for b in both], axis=0)
    values = jnp.concatenate([b[:, PAIR:] for b in both], axis=0)
    queries = q_ref[...] * jnp.asarray(HEAD_DIM**-0.5, bf16)
    grads = grad_ref[...]
    lane = lax.broadcasted_iota(jnp.int32, (rows, PAIR), 1)
    dqs, dk, dv = [], None, None
    for head in range(2):
        mine = (lane >= head * HEAD_DIM) & (lane < (head + 1) * HEAD_DIM)
        picked = jnp.where(mine, queries, jnp.zeros_like(queries))
        grad = jnp.where(mine, grads, jnp.zeros_like(grads))
        scores = mm_t(keys, picked)
        weighting = jnp.exp(scores - log_ref[0, head : head + 1, :])
        grad_weighting = mm_t(values, grad)
        row_term = jnp.sum(grad_weighting * weighting, axis=0, keepdims=True)
        grad_scores = (weighting * (grad_weighting - row_term)).astype(bf16)
        dqs.append(t_mm(keys, grad_scores))
        k_part = mm(grad_scores, picked)
        v_part = mm(weighting.astype(bf16), grad)
        dk = k_part if dk is None else dk + k_part
        dv = v_part if dv is None else dv + v_part
    row = lax.broadcasted_iota(jnp.int32, (PAIR, rows), 0)
    joined = jnp.where(row < HEAD_DIM, dqs[0], dqs[1]) * (HEAD_DIM**-0.5)
    dq_ref[...] = joined.T.astype(bf16)
    for i, ref in enumerate(dkv_refs):
        ref[:, :PAIR] = dk[i * rows : (i + 1) * rows].astype(bf16)
        ref[:, PAIR:] = dv[i * rows : (i + 1) * rows].astype(bf16)


def pair_specs(rows, pairs):
    half = pairs // 2
    q_spec = pl.BlockSpec((rows, PAIR), lambda i: (0, i))
    kv_spec = pl.BlockSpec((rows, 2 * PAIR), lambda i: (0, i))
    kv_swapped = pl.BlockSpec((rows, 2 * PAIR), lambda i: (0, (i + half) % pairs))
    log_spec = pl.BlockSpec((1, 2, rows), lambda i: (i, 0, 0))
    return q_spec, [kv_spec, kv_swapped, kv_spec, kv_swapped], log_spec


def attend(queries, blocks):
    rows, width = queries.shape
    pairs = width // PAIR
    q_spec, kv_specs, log_spec = pair_specs(rows, pairs)
    return pl.pallas_call(
        attend_kernel,
        grid=(pairs,),
        in_specs=[q_spec] + kv_specs,
        out_specs=[q_spec, log_spec],
        out_shape=[
            jax.ShapeDtypeStruct((rows, width), bf16),
            jax.ShapeDtypeStruct((pairs, 2, rows), f32),
        ],
        compiler_params=pltpu.CompilerParams(vmem_limit_bytes=40 * 2**20),
        name="attend",
    )(queries, *blocks)


def attend_back(queries, blocks, grad, log_total):
    rows, width = queries.shape
    pairs = width // PAIR
    q_spec, kv_specs, log_spec = pair_specs(rows, pairs)
    return pl.pallas_call(
        attend_back_kernel,
        grid=(pairs,),
        in_specs=[q_spec] + kv_specs + [q_spec, log_spec],
        out_specs=[q_spec] + kv_specs,
        out_shape=[jax.ShapeDtypeStruct((rows, width), bf16)]
        + [jax.ShapeDtypeStruct((rows, 2 * width), bf16)] * 4,
        compiler_params=pltpu.CompilerParams(vmem_limit_bytes=40 * 2**20),
        name="attend_back",
    )(queries, *blocks, grad, log_total)


def to_images(tokens):
    count, rows, width = tokens.shape
    mixed = lax.all_to_all(tokens, "z", split_axis=0, concat_axis=0, tiled=True)
    mixed = mixed.reshape(count * rows, width)
    return lax.ppermute(mixed, ("yh", "core"), [(0, 0), (1, 2), (2, 1), (3, 3)])


def from_images(tokens, count):
    rows, width = tokens.shape
    mixed = lax.ppermute(tokens, ("yh", "core"), [(0, 0), (1, 2), (2, 1), (3, 3)])
    mixed = mixed.reshape(count, rows // count, width)
    return lax.all_to_all(mixed, "z", split_axis=0, concat_axis=0, tiled=True)


def group_blocks(key_value):
    mate = swap(key_value, "core")
    near = swap(key_value, "yl")
    far = swap(near, "core")
    return (key_value, mate, near, far)


def group_sum(own, mate, near, far):
    mate, far = swap(mate, "core"), swap(far, "core")
    sent = (near.astype(f32) + far.astype(f32)).astype(bf16)
    kept = own.astype(f32) + mate.astype(f32)
    return (kept + swap(sent, "yl").astype(f32)).astype(bf16)


def normal_part(values):
    mean = jnp.mean(values, axis=-1, keepdims=True)
    centred = values - mean
    factor = lax.rsqrt(jnp.mean(centred * centred, axis=-1, keepdims=True) + EPSILON)
    return centred * factor, factor


def norm_back(grad, normal, factor, gain):
    e = grad * gain
    inner = jnp.mean(e * normal, axis=-1, keepdims=True)
    return factor * (e - jnp.mean(e, axis=-1, keepdims=True) - normal * inner)


def forward(tokens, w):
    inputs = tokens.astype(f32)
    normed_one = (normal_part(inputs)[0] * w["gain"][0] + w["shift"][0]).astype(bf16)
    width = tokens.shape[1]
    half = width // 2
    joined = [
        (mm(normed_one, part) + bias).astype(bf16) for part, bias in zip(w["qkv"], w["qkv_bias"])
    ]
    queries = jnp.concatenate([j[:, :half] for j in joined], axis=1)
    blocks = group_blocks(jnp.concatenate([j[:, half:] for j in joined], axis=1))
    attended, log_total = attend(queries, blocks)
    branch = mm(attended, w["proj"]) + w["out_bias"][0]
    middle = inputs + w["scale"][0] * branch
    normed_two = (normal_part(middle)[0] * w["gain"][1] + w["shift"][1]).astype(bf16)
    activated, slope, branch_two = [], [], w["out_bias"][1]
    for up, bias, down in zip(w["fc1"], w["fc1_bias"], w["fc2"]):
        before = mm(normed_two, up) + bias
        phi = 0.5 * (1.0 + lax.erf(before * (0.5**0.5)))
        density = jnp.exp(-0.5 * before * before) * 0.3989422804014327
        active = (before * phi).astype(bf16)
        activated.append(active)
        slope.append((phi + before * density).astype(bf16))
        branch_two = branch_two + mm(active, down)
    result = (middle + w["scale"][1] * branch_two).astype(bf16)
    kept = dict(
        inputs=inputs,
        normed_one=normed_one,
        queries=queries,
        blocks=blocks,
        attended=attended,
        log_total=log_total,
        branch=branch,
        middle=middle,
        normed_two=normed_two,
        activated=activated,
        slope=slope,
        branch_two=branch_two,
    )
    return result, kept


def backward(grad_out, kept, w):
    grad_branch_two = (w["scale"][1] * grad_out).astype(bf16)
    grad_before = []
    grad_normed_two = 0.0
    for up, down, slope in zip(w["fc1"], w["fc2"], kept["slope"]):
        part = (mm_t(grad_branch_two, down) * slope.astype(f32)).astype(bf16)
        grad_before.append(part)
        grad_normed_two = grad_normed_two + mm_t(part, up)
    normal_two, factor_two = normal_part(kept["middle"])
    grad_middle = grad_out + norm_back(grad_normed_two, normal_two, factor_two, w["gain"][1])
    grad_branch = (w["scale"][0] * grad_middle).astype(bf16)
    grad_attended = mm_t(grad_branch, w["proj"]).astype(bf16)
    parts = attend_back(kept["queries"], kept["blocks"], grad_attended, kept["log_total"])
    grad_queries = parts[0]
    grad_key_value = group_sum(*parts[1:])
    width = grad_queries.shape[1]
    half = width // 2
    grad_joined = [
        jnp.concatenate(
            [
                grad_queries[:, i * half : (i + 1) * half],
                grad_key_value[:, i * width : (i + 1) * width],
            ],
            axis=1,
        )
        for i in range(2)
    ]
    grad_normed_one = sum(mm_t(g, part) for g, part in zip(grad_joined, w["qkv"]))
    normal_one, factor_one = normal_part(kept["inputs"])
    grad_inputs = grad_middle + norm_back(grad_normed_one, normal_one, factor_one, w["gain"][0])
    total = lambda a: jnp.sum(a.astype(f32), axis=0)
    joined_sums = [total(g) for g in grad_joined]
    vectors = dict(
        gain=(total(grad_normed_one * normal_one), total(grad_normed_two * normal_two)),
        shift=(total(grad_normed_one), total(grad_normed_two)),
        out_bias=(total(grad_branch), total(grad_branch_two)),
        scale=(total(grad_middle * kept["branch"]), total(grad_out * kept["branch_two"])),
        joined=joined_sums,
        fc1_bias=[total(g) for g in grad_before],
    )
    outer = dict(
        qkv=(kept["normed_one"], grad_joined),
        proj=(kept["attended"], grad_branch),
        fc1=(kept["normed_two"], grad_before),
        fc2=(kept["activated"], grad_branch_two),
    )
    return grad_inputs.astype(bf16), vectors, outer


def ordered(core, mine, other):
    return jnp.where(core == 0, mine, other), jnp.where(core == 0, other, mine)


def per_device(
    patch_tokens,
    out_grad,
    batch_counts,
    norm_gain,
    norm_bias,
    qkv_weight,
    qv_bias,
    proj_weight,
    fc1_weight,
    fc1_bias,
    fc2_weight,
    out_bias,
    layer_scale,
):
    section = lax.axis_index("section")
    core = lax.axis_index("core")
    shards = lax.axis_size(FSDP)
    images, rows, width = patch_tokens.shape
    half = width // 2
    own = width // shards
    hidden = fc2_weight.shape[1]
    mid = hidden // 2
    groups = half // PAIR
    pick = lambda a, i, axis: lax.dynamic_index_in_dim(a, i, axis, keepdims=False)
    gather = lambda a: lax.all_gather(a, FSDP, axis=0, tiled=True)

    q, k, v = (qkv_weight[0][:, i * width : (i + 1) * width] for i in range(3))
    q_mine = pick(q.reshape(own, 2, half), core, 1)
    kv = jnp.stack([k.reshape(own, 2, groups, PAIR), v.reshape(own, 2, groups, PAIR)], axis=3)
    kv_mine = pick(kv, core, 1).reshape(own, width)
    vectors = jnp.concatenate(
        [a[0] for a in (norm_gain, norm_bias, qv_bias, out_bias, layer_scale)]
        + [fc1_bias[0].reshape(own, hidden // own).T],
        axis=0,
    ).T
    count = vectors.shape[1]
    vectors = jnp.pad(vectors, ((0, 0), (0, 128 - count)))
    first = gather(jnp.concatenate([q_mine, kv_mine, vectors], axis=1))
    qkv_mine = first[:, : half + width]
    vectors = first[:, half + width : half + width + count].T.astype(f32)
    fc1_b = vectors[10:].T.reshape(shards, 2, mid // 1)
    fc1_mine = pick(fc1_weight[0].reshape(own, shards, 2, mid), core, 2).reshape(own, shards * mid)
    fc2_mine = pick(fc2_weight[0].reshape(2, mid, width), core, 0)
    proj_mine = pick(proj_weight[0].reshape(2, own // 2, width), core, 0)
    proj_half = gather(proj_mine)
    fc1_half = gather(fc1_mine)
    fc2_half = gather(fc2_mine)
    lower, upper = ordered(core, proj_half, swap(proj_half, "core"))
    proj = jnp.stack(
        [lower.reshape(shards, own // 2, width), upper.reshape(shards, own // 2, width)], axis=1
    ).reshape(2, half, width)
    proj = jnp.concatenate([pick(proj, core, 0), pick(proj, 1 - core, 0)], axis=0)

    def halves(vector):
        pair = vector.reshape(2, half)
        return pick(pair, core, 0), pick(pair, 1 - core, 0)

    def qkv_bias(q_half, v_half):
        v_part = v_half.reshape(groups, 1, PAIR)
        kv_part = jnp.concatenate([jnp.zeros_like(v_part), v_part], axis=1).reshape(width)
        return jnp.concatenate([q_half, kv_part])

    w = dict(
        gain=vectors[0:2],
        shift=vectors[2:4],
        out_bias=vectors[6:8],
        scale=vectors[8:10],
        qkv=(qkv_mine, swap(qkv_mine, "core")),
        qkv_bias=[qkv_bias(a, b) for a, b in zip(halves(vectors[4]), halves(vectors[5]))],
        proj=proj,
        fc1=(fc1_half, swap(fc1_half, "core")),
        fc1_bias=(pick(fc1_b, core, 1).reshape(-1), pick(fc1_b, 1 - core, 1).reshape(-1)),
        fc2=(fc2_half, swap(fc2_half, "core")),
    )

    live = (
        jnp.arange(images) % IMG_MB < jnp.repeat(batch_counts[0], IMG_MB)
    ).astype(bf16)
    first_tokens = to_images(patch_tokens)
    last_grad = to_images(out_grad * live[:, None, None])

    sent, _ = forward(first_tokens, w)
    passed = lax.ppermute(sent, "section", [(0, 1)])
    tokens = jnp.where(section == 0, first_tokens, passed)
    result, kept = forward(tokens, w)
    block_out = from_images(result, images)

    sent, _, _ = backward(last_grad.astype(f32), kept, w)
    passed = lax.ppermute(sent, "section", [(1, 0)])
    grad_out = jnp.where(section == 1, last_grad, passed).astype(f32)
    grad_inputs, sums, outer = backward(grad_out, kept, w)
    in_grad = from_images(grad_inputs, images)

    def core_sum(mine, other):
        return (mine + swap(other.astype(bf16), "core").astype(f32)).astype(bf16)

    def scatter(a):
        return lax.psum_scatter(a, FSDP, scatter_dimension=0, tiled=True)

    def natural(pair):
        return jnp.concatenate(ordered(core, *pair))

    joined = sums["joined"]
    v_sum = lambda a: a[half:].reshape(groups, 2, PAIR)[:, 1].reshape(half)
    fc1_sum = jnp.stack(
        ordered(core, *(s.reshape(shards, mid) for s in sums["fc1_bias"])), axis=1
    ).reshape(width, hidden // own)
    vector_grads = jnp.concatenate(
        [
            jnp.stack(
                [
                    *sums["gain"],
                    *sums["shift"],
                    natural([j[:half] for j in joined]),
                    natural([v_sum(j) for j in joined]),
                    *sums["out_bias"],
                    *sums["scale"],
                ],
                axis=1,
            ),
            fc1_sum,
        ],
        axis=1,
    )
    vector_grads = jnp.pad(vector_grads, ((0, 0), (0, 128 - count)))

    a2, du = outer["fc1"]
    z, e2 = outer["fc2"]
    fc2_grad = scatter(core_sum(t_mm(z[0], e2), t_mm(z[1], e2)))
    fc1_grad = scatter(core_sum(t_mm(a2, du[0]), t_mm(a2, du[1])))
    o, e1 = outer["proj"]
    proj_full = t_mm(o, e1).astype(bf16).reshape(2, half, width)
    proj_full = jnp.concatenate(ordered(core, proj_full[0], proj_full[1]))
    proj_full = proj_full.reshape(shards, 2, own // 2, width)
    proj_grad = scatter(
        core_sum(pick(proj_full, core, 1).astype(f32), pick(proj_full, 1 - core, 1)).reshape(
            half, width
        )
    )
    a1, dj = outer["qkv"]
    vec = [vector_grads, vector_grads]
    qkv_grad = scatter(
        core_sum(*(jnp.concatenate([t_mm(a1, d), g], axis=1) for d, g in zip(dj, vec)))
    )

    parts = [qkv_grad, fc1_grad, proj_grad, fc2_grad]
    parts = [
        (a.astype(f32) + swap(a, "xhi").astype(f32)).astype(bf16) for a in parts
    ]
    others = [swap(a, "core") for a in parts]
    qkv_pair, fc1_pair, proj_pair, fc2_pair = (
        ordered(core, a.astype(f32), b.astype(f32)) for a, b in zip(parts, others)
    )
    vec_grad = parts[0][:, half + width : half + width + count].T.astype(f32)
    q_grad = jnp.concatenate([p[:, :half] for p in qkv_pair], axis=1)
    kv_grads = [p[:, half : half + width].reshape(own, groups, 2, PAIR) for p in qkv_pair]
    k_grad, v_grad = (
        jnp.concatenate([p[:, :, i].reshape(own, half) for p in kv_grads], axis=1)
        for i in range(2)
    )
    qkv_out = jnp.concatenate([q_grad, k_grad, v_grad], axis=1)
    fc1_out = jnp.stack([p.reshape(own, shards, mid) for p in fc1_pair], axis=2).reshape(
        own, 2 * shards * mid
    )
    fc2_out = jnp.concatenate(fc2_pair, axis=0)
    proj_out = jnp.concatenate(proj_pair, axis=0)
    return (
        block_out[None],
        in_grad[None],
        vec_grad[0:2][None],
        vec_grad[2:4][None],
        qkv_out[None],
        vec_grad[4:6][None],
        proj_out[None],
        fc1_out[None],
        vec_grad[10:].T.reshape(1, hidden),
        fc2_out[None],
        vec_grad[6:8][None],
        vec_grad[8:10][None],
    )


def solution(mesh):
    sections, fsdp, rep = mesh.devices.shape
    inner = Mesh(
        mesh.devices.reshape(sections, fsdp // 4, 2, 2, rep // 2, 2),
        ("section",) + FSDP + REP,
    )
    weight = P("section", FSDP, None)
    vector = P("section", None, FSDP)
    tokens = P(REP, FSDP, None)
    both = P("section", REP, FSDP, None)
    return jax.shard_map(
        per_device,
        mesh=inner,
        in_specs=(
            tokens,
            tokens,
            P(REP, None),
            vector,
            vector,
            weight,
            vector,
            weight,
            weight,
            P("section", FSDP),
            weight,
            vector,
            vector,
        ),
        out_specs=(
            both,
            both,
            vector,
            vector,
            weight,
            vector,
            weight,
            weight,
            P("section", FSDP),
            weight,
            vector,
            vector,
        ),
        check_vma=False,
    )
```

```python
import jax
import jax.numpy as jnp
from jax import lax
from jax.experimental import pallas as pl
from jax.experimental.pallas import tpu as pltpu
from jax.sharding import Mesh, PartitionSpec as P

HEAD_DIM = 64
IMG_MB = 2
PAIR = 2 * HEAD_DIM
EPSILON = 1e-06

FSDP = ("z", "yh", "yl")
REP = ("xhi", "core")
bf16 = jnp.bfloat16
f32 = jnp.float32


def dot(a, b, dims):
    return lax.dot_general(a, b, (dims, ((), ())), preferred_element_type=f32)


def mm(a, b):
    return dot(a, b, ((1,), (0,)))


def mm_t(a, b):
    return dot(a, b, ((1,), (1,)))


def t_mm(a, b):
    return dot(a, b, ((0,), (0,)))


def swap(value, axis):
    return lax.ppermute(value, axis, [(0, 1), (1, 0)])


def attend_kernel(q_ref, own_ref, mate_ref, near_ref, far_ref, out_ref, log_ref):
    rows = q_ref.shape[0]
    both = [r[...] for r in (own_ref, mate_ref, near_ref, far_ref)]
    keys = jnp.concatenate([b[:, :PAIR] for b in both], axis=0)
    values = jnp.concatenate([b[:, PAIR:] for b in both], axis=0)
    queries = q_ref[...] * jnp.asarray(HEAD_DIM**-0.5, bf16)
    lane = lax.broadcasted_iota(jnp.int32, (rows, PAIR), 1)
    outs = []
    for head in range(2):
        mine = (lane >= head * HEAD_DIM) & (lane < (head + 1) * HEAD_DIM)
        picked = jnp.where(mine, queries, jnp.zeros_like(queries))
        scores = mm_t(keys, picked)
        top = jnp.max(scores, axis=0, keepdims=True)
        raised = jnp.exp(scores - top)
        total = jnp.sum(raised, axis=0, keepdims=True)
        out = t_mm(values, raised.astype(bf16))
        outs.append(out * (1.0 / total))
        log_ref[0, head : head + 1, :] = top + jnp.log(total)
    row = lax.broadcasted_iota(jnp.int32, (PAIR, rows), 0)
    joined = jnp.where(row < HEAD_DIM, outs[0], outs[1])
    out_ref[...] = joined.T.astype(bf16)


def attend_back_kernel(
    q_ref, own_ref, mate_ref, near_ref, far_ref, grad_ref, log_ref, dq_ref, *dkv_refs
):
    rows = q_ref.shape[0]
    both = [r[...] for r in (own_ref, mate_ref, near_ref, far_ref)]
    keys = jnp.concatenate([b[:, :PAIR] for b in both], axis=0)
    values = jnp.concatenate([b[:, PAIR:] for b in both], axis=0)
    queries = q_ref[...] * jnp.asarray(HEAD_DIM**-0.5, bf16)
    grads = grad_ref[...]
    lane = lax.broadcasted_iota(jnp.int32, (rows, PAIR), 1)
    dqs, dk, dv = [], None, None
    for head in range(2):
        mine = (lane >= head * HEAD_DIM) & (lane < (head + 1) * HEAD_DIM)
        picked = jnp.where(mine, queries, jnp.zeros_like(queries))
        grad = jnp.where(mine, grads, jnp.zeros_like(grads))
        scores = mm_t(keys, picked)
        weighting = jnp.exp(scores - log_ref[0, head : head + 1, :])
        grad_weighting = mm_t(values, grad)
        row_term = jnp.sum(grad_weighting * weighting, axis=0, keepdims=True)
        grad_scores = (weighting * (grad_weighting - row_term)).astype(bf16)
        dqs.append(t_mm(keys, grad_scores))
        k_part = mm(grad_scores, picked)
        v_part = mm(weighting.astype(bf16), grad)
        dk = k_part if dk is None else dk + k_part
        dv = v_part if dv is None else dv + v_part
    row = lax.broadcasted_iota(jnp.int32, (PAIR, rows), 0)
    joined = jnp.where(row < HEAD_DIM, dqs[0], dqs[1]) * (HEAD_DIM**-0.5)
    dq_ref[...] = joined.T.astype(bf16)
    for i, ref in enumerate(dkv_refs):
        ref[:, :PAIR] = dk[i * rows : (i + 1) * rows].astype(bf16)
        ref[:, PAIR:] = dv[i * rows : (i + 1) * rows].astype(bf16)


def pair_specs(rows, pairs):
    half = pairs // 2
    q_spec = pl.BlockSpec((rows, PAIR), lambda i: (0, i))
    kv_spec = pl.BlockSpec((rows, 2 * PAIR), lambda i: (0, i))
    kv_swapped = pl.BlockSpec((rows, 2 * PAIR), lambda i: (0, (i + half) % pairs))
    log_spec = pl.BlockSpec((1, 2, rows), lambda i: (i, 0, 0))
    return q_spec, [kv_spec, kv_swapped, kv_spec, kv_swapped], log_spec


def attend(queries, blocks):
    rows, width = queries.shape
    pairs = width // PAIR
    q_spec, kv_specs, log_spec = pair_specs(rows, pairs)
    return pl.pallas_call(
        attend_kernel,
        grid=(pairs,),
        in_specs=[q_spec] + kv_specs,
        out_specs=[q_spec, log_spec],
        out_shape=[
            jax.ShapeDtypeStruct((rows, width), bf16),
            jax.ShapeDtypeStruct((pairs, 2, rows), f32),
        ],
        compiler_params=pltpu.CompilerParams(vmem_limit_bytes=40 * 2**20),
        name="attend",
    )(queries, *blocks)


def attend_back(queries, blocks, grad, log_total):
    rows, width = queries.shape
    pairs = width // PAIR
    q_spec, kv_specs, log_spec = pair_specs(rows, pairs)
    return pl.pallas_call(
        attend_back_kernel,
        grid=(pairs,),
        in_specs=[q_spec] + kv_specs + [q_spec, log_spec],
        out_specs=[q_spec] + kv_specs,
        out_shape=[jax.ShapeDtypeStruct((rows, width), bf16)]
        + [jax.ShapeDtypeStruct((rows, 2 * width), bf16)] * 4,
        compiler_params=pltpu.CompilerParams(vmem_limit_bytes=40 * 2**20),
        name="attend_back",
    )(queries, *blocks, grad, log_total)


FLIP = [(0, 0), (1, 2), (2, 1), (3, 3)]


def to_images(arrays):
    count, rows, width = arrays[0].shape
    mixed = jnp.stack(arrays, axis=1)
    mixed = lax.all_to_all(mixed, "z", split_axis=0, concat_axis=0, tiled=True)
    mixed = [mixed[:, i].reshape(count * rows, width) for i in range(len(arrays))]
    return [lax.ppermute(m, ("yh", "core"), FLIP) for m in mixed]


def from_images(arrays, count):
    rows, width = arrays[0].shape
    mixed = [lax.ppermute(a, ("yh", "core"), FLIP) for a in arrays]
    mixed = jnp.stack([m.reshape(count, rows // count, width) for m in mixed], axis=1)
    mixed = lax.all_to_all(mixed, "z", split_axis=0, concat_axis=0, tiled=True)
    return [mixed[:, i] for i in range(len(arrays))]


RING_Z, RING_Y = "z", ("yh", "yl")
AHEAD = [(i, (i + 1) % 4) for i in range(4)]
BACK = [(i, (i - 1) % 4) for i in range(4)]


def ring_place(value, axis, out_shapes, views):
    half = value.shape[0] // 2
    ahead = lax.ppermute(value, axis, AHEAD)
    back = lax.ppermute(value, axis, BACK)
    far_a = lax.ppermute(ahead[:half], axis, AHEAD)
    far_b = lax.ppermute(back[half:], axis, BACK)
    pieces = [(value, 0, 0), (ahead, 3, 0), (back, 1, 0), (far_a, 2, 0), (far_b, 2, half)]
    n_outs = len(out_shapes)

    def kernel(index_ref, *refs):
        sources, outs, sems = refs[:5], refs[5 : 5 + n_outs], refs[5 + n_outs]
        copies = []
        for source, (_, step, start) in zip(sources, pieces):
            place = lax.rem(index_ref[0] + step, 4)
            for src, dst in views(outs, source, place, start):
                copies.append(pltpu.make_async_copy(src, dst, sems.at[len(copies)]))
        for copy in copies:
            copy.start()
        for copy in copies:
            copy.wait()

    size = 2 * sum(2 * value.size * 4 for _ in range(1))
    return pl.pallas_call(
        kernel,
        in_specs=[pl.BlockSpec(memory_space=pltpu.SMEM)] + [pl.BlockSpec(memory_space=pl.ANY)] * 5,
        out_specs=[pl.BlockSpec(memory_space=pl.ANY)] * n_outs,
        out_shape=[jax.ShapeDtypeStruct(shape, value.dtype) for shape in out_shapes],
        scratch_shapes=[pltpu.SemaphoreType.DMA((5 * max(n_outs, 1),))],
        cost_estimate=pl.CostEstimate(flops=0, bytes_accessed=size, transcendentals=0),
        name="ring_place",
    )(lax.axis_index(axis).reshape(1), *(p[0] for p in pieces))


def in_order(outs, piece, place, start):
    return [(piece, outs[0].at[place, pl.ds(start, piece.shape[0])])]


def ring_sum(blocks, axis):
    index = lax.axis_index(axis)
    block = lambda k: lax.dynamic_index_in_dim(blocks, (index + k) % 4, 0, keepdims=False)
    add = lambda *parts: sum(p.astype(f32) for p in parts).astype(bf16)
    far, after, before = block(2), block(1), block(3)
    half = far.shape[0] // 2
    low = lax.ppermute(far[:half], axis, AHEAD)
    high = lax.ppermute(far[half:], axis, BACK)
    after = jnp.concatenate([add(after[:half], low), after[half:]])
    before = jnp.concatenate([before[:half], add(before[half:], high)])
    after = lax.ppermute(after, axis, AHEAD)
    before = lax.ppermute(before, axis, BACK)
    return add(block(0), after, before)


def group_blocks(key_value):
    mate = swap(key_value, "core")
    near = swap(key_value, "yl")
    far = swap(near, "core")
    return (key_value, mate, near, far)


def group_sum(own, mate, near, far):
    mate, far = swap(mate, "core"), swap(far, "core")
    sent = (near.astype(f32) + far.astype(f32)).astype(bf16)
    kept = own.astype(f32) + mate.astype(f32)
    return (kept + swap(sent, "yl").astype(f32)).astype(bf16)


def normal_part(values):
    mean = jnp.mean(values, axis=-1, keepdims=True)
    centred = values - mean
    factor = lax.rsqrt(jnp.mean(centred * centred, axis=-1, keepdims=True) + EPSILON)
    return centred * factor, factor


def norm_back(grad, normal, factor, gain):
    e = grad * gain
    inner = jnp.mean(e * normal, axis=-1, keepdims=True)
    return factor * (e - jnp.mean(e, axis=-1, keepdims=True) - normal * inner)


def flip_halves(core, value):
    half = value.shape[-1] // 2
    turned = jnp.concatenate([value[..., half:], value[..., :half]], axis=-1)
    return jnp.where(core == 0, value, turned)


def forward(tokens, w):
    inputs = tokens.astype(f32)
    normed_one = (normal_part(inputs)[0] * w["gain"][0] + w["shift"][0]).astype(bf16)
    project = lambda name: jnp.concatenate(
        [
            (mm(normed_one, part) + bias).astype(bf16)
            for part, bias in zip(w[name], w[name + "_bias"])
        ],
        axis=1,
    )
    blocks = group_blocks(project("kv"))
    queries = project("q")
    attended, log_total = attend(queries, blocks)
    attended = flip_halves(w["core"], attended)
    branch = flip_halves(w["core"], jnp.concatenate([mm(attended, p) for p in w["proj"]], axis=1))
    branch = branch + w["out_bias"][0]
    middle = inputs + w["scale"][0] * branch
    normed_two = (normal_part(middle)[0] * w["gain"][1] + w["shift"][1]).astype(bf16)
    activated, slope, branch_two = [], [], w["out_bias"][1]
    for up, bias, down in zip(w["fc1"], w["fc1_bias"], w["fc2"]):
        before = mm(normed_two, up) + bias
        phi = 0.5 * (1.0 + lax.erf(before * (0.5**0.5)))
        density = jnp.exp(-0.5 * before * before) * 0.3989422804014327
        active = (before * phi).astype(bf16)
        activated.append(active)
        slope.append((phi + before * density).astype(bf16))
        for i, part in enumerate(down):
            rows = part.shape[0]
            branch_two = branch_two + mm(active[:, i * rows : (i + 1) * rows], part)
    result = (middle + w["scale"][1] * branch_two).astype(bf16)
    kept = dict(
        inputs=inputs,
        normed_one=normed_one,
        queries=queries,
        blocks=blocks,
        attended=attended,
        log_total=log_total,
        branch=branch,
        middle=middle,
        normed_two=normed_two,
        activated=activated,
        slope=slope,
        branch_two=branch_two,
    )
    return result, kept


def backward(grad_out, kept, w):
    grad_branch_two = (w["scale"][1] * grad_out).astype(bf16)
    grad_before = []
    grad_normed_two = 0.0
    for up, down, slope in zip(w["fc1"], w["fc2"], kept["slope"]):
        part = jnp.concatenate([mm_t(grad_branch_two, d) for d in down], axis=1)
        part = (part * slope.astype(f32)).astype(bf16)
        grad_before.append(part)
        grad_normed_two = grad_normed_two + mm_t(part, up)
    normal_two, factor_two = normal_part(kept["middle"])
    grad_middle = grad_out + norm_back(grad_normed_two, normal_two, factor_two, w["gain"][1])
    grad_branch = (w["scale"][0] * grad_middle).astype(bf16)
    width = grad_branch.shape[1]
    half = width // 2
    grad_halves = flip_halves(w["core"], grad_branch)
    grad_halves = [grad_halves[:, :half], grad_halves[:, half:]]
    grad_attended = sum(mm_t(g, p) for g, p in zip(grad_halves, w["proj"])).astype(bf16)
    grad_attended = flip_halves(w["core"], grad_attended)
    parts = attend_back(kept["queries"], kept["blocks"], grad_attended, kept["log_total"])
    grad_queries = parts[0]
    grad_key_value = group_sum(*parts[1:])
    grad_q = [grad_queries[:, i * half : (i + 1) * half] for i in range(2)]
    grad_kv = [grad_key_value[:, i * width : (i + 1) * width] for i in range(2)]
    grad_normed_one = sum(
        mm_t(g, part) for g, part in zip(grad_q + grad_kv, w["q"] + w["kv"])
    )
    normal_one, factor_one = normal_part(kept["inputs"])
    grad_inputs = grad_middle + norm_back(grad_normed_one, normal_one, factor_one, w["gain"][0])
    total = lambda a: jnp.sum(a.astype(f32), axis=0)
    vectors = dict(
        gain=(total(grad_normed_one * normal_one), total(grad_normed_two * normal_two)),
        shift=(total(grad_normed_one), total(grad_normed_two)),
        out_bias=(total(grad_branch), total(grad_branch_two)),
        scale=(total(grad_middle * kept["branch"]), total(grad_out * kept["branch_two"])),
        q=[total(g) for g in grad_q],
        kv=[total(g) for g in grad_kv],
        fc1_bias=[total(g) for g in grad_before],
    )
    outer = dict(
        q=(kept["normed_one"], grad_q),
        kv=(kept["normed_one"], grad_kv),
        proj=(kept["attended"], grad_halves),
        fc1=(kept["normed_two"], grad_before),
        fc2=(kept["activated"], grad_branch_two),
    )
    return grad_inputs.astype(bf16), vectors, outer


def ordered(core, mine, other):
    return jnp.where(core == 0, mine, other), jnp.where(core == 0, other, mine)


def per_device(
    patch_tokens,
    out_grad,
    batch_counts,
    norm_gain,
    norm_bias,
    qkv_weight,
    qv_bias,
    proj_weight,
    fc1_weight,
    fc1_bias,
    fc2_weight,
    out_bias,
    layer_scale,
):
    section = lax.axis_index("section")
    core = lax.axis_index("core")
    shards = lax.axis_size(FSDP)
    images, rows, width = patch_tokens.shape
    half = width // 2
    own = width // shards
    hidden = fc2_weight.shape[1]
    mid = hidden // 2
    groups = half // PAIR
    pick = lambda a, i, axis: lax.dynamic_index_in_dim(a, i, axis, keepdims=False)

    part = mid // 2
    q, k, v = (qkv_weight[0][:, i * width : (i + 1) * width] for i in range(3))
    q_mine = pick(q.reshape(own, 2, half), core, 1)
    kv = jnp.stack([k.reshape(own, 2, groups, PAIR), v.reshape(own, 2, groups, PAIR)], axis=3)
    kv_mine = pick(kv, core, 1).reshape(own, width)
    proj_mine = pick(proj_weight[0].reshape(own, 2, half), core, 1)
    vectors = jnp.concatenate(
        [a[0] for a in (norm_gain, norm_bias, qv_bias, out_bias, layer_scale)]
        + [fc1_bias[0].reshape(own, hidden // own).T],
        axis=0,
    ).T
    count = vectors.shape[1]
    vectors = jnp.pad(vectors, ((0, 0), (0, 128 - count)))
    fc1_mine = pick(fc1_weight[0].reshape(own, shards, 2, 2, part), core, 2)
    fc1_mine = jnp.swapaxes(fc1_mine, 1, 2).reshape(own, shards * mid)
    fc2_mine = pick(fc2_weight[0].reshape(2, 2, part, width), core, 0)
    fc_mine = jnp.concatenate([fc1_mine, fc2_mine[0], fc2_mine[1]], axis=1)
    fc_half = lax.all_gather(fc_mine, FSDP, axis=0, tiled=True)

    a_mine = jnp.concatenate([q_mine, proj_mine, vectors], axis=1)
    a_row = ring_place(a_mine, RING_Y, [(4, own, a_mine.shape[1])], in_order)[0]
    a_row = a_row.reshape(4 * own, a_mine.shape[1])
    b_row = ring_place(kv_mine, RING_Z, [(4, own, width)], in_order)[0]

    def a_views(outs, piece, place, start):
        rows = pl.ds(start, piece.shape[0])
        columns = [pl.ds(0, half), pl.ds(half, half), pl.ds(width, 128)]
        return [(piece.at[:, c], out.at[place, rows]) for c, out in zip(columns, outs)]

    def b_views(outs, piece, place, start):
        return [(piece, outs[0].at[pl.ds(start, piece.shape[0]), place])]

    q_half, proj_half, vectors = (
        o.reshape(width, -1)
        for o in ring_place(
            a_row, RING_Z, [(4, 4 * own, half), (4, 4 * own, half), (4, 4 * own, 128)], a_views
        )
    )
    kv_half = ring_place(b_row, RING_Y, [(4, 4, own, width)], b_views)[0].reshape(width, width)
    vectors = vectors[:, :count].T.astype(f32)
    fc1_b = vectors[10:].T.reshape(shards, 2, 2, part)

    def halves(vector):
        pair = vector.reshape(2, half)
        return pick(pair, core, 0), pick(pair, 1 - core, 0)

    def kv_bias(v_half):
        v_part = v_half.reshape(groups, 1, PAIR)
        return jnp.concatenate([jnp.zeros_like(v_part), v_part], axis=1).reshape(width)

    wide = shards * mid
    fc_pair = (fc_half, swap(fc_half, "core"))
    w = dict(
        core=core,
        gain=vectors[0:2],
        shift=vectors[2:4],
        out_bias=vectors[6:8],
        scale=vectors[8:10],
        q=[q_half, swap(q_half, "core")],
        q_bias=halves(vectors[4]),
        kv=[kv_half, swap(kv_half, "core")],
        kv_bias=[kv_bias(b) for b in halves(vectors[5])],
        proj=(proj_half, swap(proj_half, "core")),
        fc1=[f[:, :wide] for f in fc_pair],
        fc1_bias=[
            jnp.swapaxes(pick(fc1_b, c, 1), 0, 1).reshape(-1) for c in (core, 1 - core)
        ],
        fc2=[(f[:, wide : wide + width], f[:, wide + width :]) for f in fc_pair],
    )

    live = (
        jnp.arange(images) % IMG_MB < jnp.repeat(batch_counts[0], IMG_MB)
    ).astype(bf16)
    first_tokens, last_grad = to_images([patch_tokens, out_grad * live[:, None, None]])

    sent, _ = forward(first_tokens, w)
    passed = lax.ppermute(sent, "section", [(0, 1)])
    tokens = jnp.where(section == 0, first_tokens, passed)
    result, kept = forward(tokens, w)

    sent, _, _ = backward(last_grad.astype(f32), kept, w)
    passed = lax.ppermute(sent, "section", [(1, 0)])
    grad_out = jnp.where(section == 1, last_grad, passed).astype(f32)
    grad_inputs, sums, outer = backward(grad_out, kept, w)
    result, grad_inputs = lax.optimization_barrier((result, grad_inputs))
    block_out, in_grad = from_images([result, grad_inputs], images)

    def core_sum(mine, other):
        return (mine + swap(other.astype(bf16), "core").astype(f32)).astype(bf16)

    def natural(pair):
        return jnp.concatenate(ordered(core, *pair))

    v_sum = lambda a: a.reshape(groups, 2, PAIR)[:, 1].reshape(half)
    fc1_sum = jnp.stack(
        ordered(
            core, *(jnp.swapaxes(s.reshape(2, shards, part), 0, 1) for s in sums["fc1_bias"])
        ),
        axis=1,
    ).reshape(width, hidden // own)
    vector_grads = jnp.concatenate(
        [
            jnp.stack(
                [
                    *sums["gain"],
                    *sums["shift"],
                    natural(sums["q"]),
                    natural([v_sum(g) for g in sums["kv"]]),
                    *sums["out_bias"],
                    *sums["scale"],
                ],
                axis=1,
            ),
            fc1_sum,
        ],
        axis=1,
    )
    vector_grads = jnp.pad(vector_grads, ((0, 0), (0, 128 - count)))

    a2, du = outer["fc1"]
    z, e2 = outer["fc2"]
    fc_parts = [
        jnp.concatenate([t_mm(a2, du[i]), t_mm(z[i][:, :width], e2), t_mm(z[i][:, width:], e2)], 1)
        for i in range(2)
    ]
    fc_grad = lax.psum_scatter(core_sum(*fc_parts), FSDP, scatter_dimension=0, tiled=True)
    a1, dq = outer["q"]
    dkv = outer["kv"][1]
    o, e1 = outer["proj"]
    a_parts = [
        jnp.concatenate([t_mm(a1, dq[i]), t_mm(o, e1[i]), vector_grads], axis=1) for i in range(2)
    ]
    b_parts = [t_mm(a1, dkv[i]) for i in range(2)]
    b_sum = ring_sum(core_sum(*b_parts).reshape(4, 4, own, width), RING_Z)
    b_grad = ring_sum(b_sum, RING_Y)
    a_blocks = core_sum(*a_parts).reshape(4, 4, own, width + 128)
    a_sum = ring_sum(jnp.swapaxes(a_blocks, 0, 1), RING_Y)
    a_grad = ring_sum(a_sum, RING_Z)

    parts = [a_grad, b_grad, fc_grad]
    parts = [(a.astype(f32) + swap(a, "xhi").astype(f32)).astype(bf16) for a in parts]
    vec_grad = parts[0][:, width : width + count].T.astype(f32)
    others = [swap(a, "core") for a in parts]
    a_pair, b_pair, fc_pair = (
        ordered(core, a.astype(f32), b.astype(f32)) for a, b in zip(parts, others)
    )
    q_grad = jnp.concatenate([p[:, :half] for p in a_pair], axis=1)
    proj_out = jnp.concatenate([p[:, half:width] for p in a_pair], axis=1)
    kv_grads = [p.reshape(own, groups, 2, PAIR) for p in b_pair]
    k_grad, v_grad = (
        jnp.concatenate([p[:, :, i].reshape(own, half) for p in kv_grads], axis=1)
        for i in range(2)
    )
    qkv_out = jnp.concatenate([q_grad, k_grad, v_grad], axis=1)
    fc1_out = jnp.stack(
        [jnp.swapaxes(p[:, :wide].reshape(own, 2, shards, part), 1, 2) for p in fc_pair], axis=2
    ).reshape(own, 2 * wide)
    fc2_out = jnp.concatenate(
        [p[:, wide + i * width : wide + (i + 1) * width] for p in fc_pair for i in range(2)], axis=0
    )
    return (
        block_out[None],
        in_grad[None],
        vec_grad[0:2][None],
        vec_grad[2:4][None],
        qkv_out[None],
        vec_grad[4:6][None],
        proj_out[None],
        fc1_out[None],
        vec_grad[10:].T.reshape(1, hidden),
        fc2_out[None],
        vec_grad[6:8][None],
        vec_grad[8:10][None],
    )


def solution(mesh):
    sections, fsdp, rep = mesh.devices.shape
    inner = Mesh(
        mesh.devices.reshape(sections, fsdp // 4, 2, 2, rep // 2, 2),
        ("section",) + FSDP + REP,
    )
    weight = P("section", FSDP, None)
    vector = P("section", None, FSDP)
    tokens = P(REP, FSDP, None)
    both = P("section", REP, FSDP, None)
    return jax.shard_map(
        per_device,
        mesh=inner,
        in_specs=(
            tokens,
            tokens,
            P(REP, None),
            vector,
            vector,
            weight,
            vector,
            weight,
            weight,
            P("section", FSDP),
            weight,
            vector,
            vector,
        ),
        out_specs=(
            both,
            both,
            vector,
            vector,
            weight,
            vector,
            weight,
            weight,
            P("section", FSDP),
            weight,
            vector,
            vector,
        ),
        check_vma=False,
    )
```

```python
import jax
import jax.numpy as jnp
from jax import lax
from jax.experimental import pallas as pl
from jax.experimental.pallas import tpu as pltpu
from jax.sharding import Mesh, PartitionSpec as P

HEAD_DIM = 64
IMG_MB = 2
PAIR = 2 * HEAD_DIM
EPSILON = 1e-06

FSDP = ("z", "yh", "yl")
REP = ("xhi", "core")
bf16 = jnp.bfloat16
f32 = jnp.float32


def dot(a, b, dims):
    return lax.dot_general(a, b, (dims, ((), ())), preferred_element_type=f32)


def mm(a, b):
    return dot(a, b, ((1,), (0,)))


def mm_t(a, b):
    return dot(a, b, ((1,), (1,)))


def t_mm(a, b):
    return dot(a, b, ((0,), (0,)))


def swap(value, axis):
    return lax.ppermute(value, axis, [(0, 1), (1, 0)])


def attend_kernel(q_ref, own_ref, mate_ref, near_ref, far_ref, out_ref, log_ref):
    rows = q_ref.shape[0]
    both = [r[...] for r in (own_ref, mate_ref, near_ref, far_ref)]
    keys = jnp.concatenate([b[:, :PAIR] for b in both], axis=0)
    values = jnp.concatenate([b[:, PAIR:] for b in both], axis=0)
    queries = q_ref[...] * jnp.asarray(HEAD_DIM**-0.5, bf16)
    lane = lax.broadcasted_iota(jnp.int32, (rows, PAIR), 1)
    outs = []
    for head in range(2):
        mine = (lane >= head * HEAD_DIM) & (lane < (head + 1) * HEAD_DIM)
        picked = jnp.where(mine, queries, jnp.zeros_like(queries))
        scores = mm_t(keys, picked)
        top = jnp.max(scores, axis=0, keepdims=True)
        raised = jnp.exp(scores - top)
        total = jnp.sum(raised, axis=0, keepdims=True)
        out = t_mm(values, raised.astype(bf16))
        outs.append(out * (1.0 / total))
        log_ref[0, head : head + 1, :] = top + jnp.log(total)
    row = lax.broadcasted_iota(jnp.int32, (PAIR, rows), 0)
    joined = jnp.where(row < HEAD_DIM, outs[0], outs[1])
    out_ref[...] = joined.T.astype(bf16)


def attend_back_kernel(
    q_ref, own_ref, mate_ref, near_ref, far_ref, grad_ref, log_ref, dq_ref, *dkv_refs
):
    rows = q_ref.shape[0]
    both = [r[...] for r in (own_ref, mate_ref, near_ref, far_ref)]
    keys = jnp.concatenate([b[:, :PAIR] for b in both], axis=0)
    values = jnp.concatenate([b[:, PAIR:] for b in both], axis=0)
    queries = q_ref[...] * jnp.asarray(HEAD_DIM**-0.5, bf16)
    grads = grad_ref[...]
    lane = lax.broadcasted_iota(jnp.int32, (rows, PAIR), 1)
    dqs, dk, dv = [], None, None
    for head in range(2):
        mine = (lane >= head * HEAD_DIM) & (lane < (head + 1) * HEAD_DIM)
        picked = jnp.where(mine, queries, jnp.zeros_like(queries))
        grad = jnp.where(mine, grads, jnp.zeros_like(grads))
        scores = mm_t(keys, picked)
        weighting = jnp.exp(scores - log_ref[0, head : head + 1, :])
        grad_weighting = mm_t(values, grad)
        row_term = jnp.sum(grad_weighting * weighting, axis=0, keepdims=True)
        grad_scores = (weighting * (grad_weighting - row_term)).astype(bf16)
        dqs.append(t_mm(keys, grad_scores))
        k_part = mm(grad_scores, picked)
        v_part = mm(weighting.astype(bf16), grad)
        dk = k_part if dk is None else dk + k_part
        dv = v_part if dv is None else dv + v_part
    row = lax.broadcasted_iota(jnp.int32, (PAIR, rows), 0)
    joined = jnp.where(row < HEAD_DIM, dqs[0], dqs[1]) * (HEAD_DIM**-0.5)
    dq_ref[...] = joined.T.astype(bf16)
    for i, ref in enumerate(dkv_refs):
        ref[:, :PAIR] = dk[i * rows : (i + 1) * rows].astype(bf16)
        ref[:, PAIR:] = dv[i * rows : (i + 1) * rows].astype(bf16)


def pair_specs(rows, pairs):
    half = pairs // 2
    q_spec = pl.BlockSpec((rows, PAIR), lambda i: (0, i))
    kv_spec = pl.BlockSpec((rows, 2 * PAIR), lambda i: (0, i))
    kv_swapped = pl.BlockSpec((rows, 2 * PAIR), lambda i: (0, (i + half) % pairs))
    log_spec = pl.BlockSpec((1, 2, rows), lambda i: (i, 0, 0))
    return q_spec, [kv_spec, kv_swapped, kv_spec, kv_swapped], log_spec


def attend(queries, blocks):
    rows, width = queries.shape
    pairs = width // PAIR
    q_spec, kv_specs, log_spec = pair_specs(rows, pairs)
    return pl.pallas_call(
        attend_kernel,
        grid=(pairs,),
        in_specs=[q_spec] + kv_specs,
        out_specs=[q_spec, log_spec],
        out_shape=[
            jax.ShapeDtypeStruct((rows, width), bf16),
            jax.ShapeDtypeStruct((pairs, 2, rows), f32),
        ],
        compiler_params=pltpu.CompilerParams(vmem_limit_bytes=40 * 2**20),
        name="attend",
    )(queries, *blocks)


def attend_back(queries, blocks, grad, log_total):
    rows, width = queries.shape
    pairs = width // PAIR
    q_spec, kv_specs, log_spec = pair_specs(rows, pairs)
    return pl.pallas_call(
        attend_back_kernel,
        grid=(pairs,),
        in_specs=[q_spec] + kv_specs + [q_spec, log_spec],
        out_specs=[q_spec] + kv_specs,
        out_shape=[jax.ShapeDtypeStruct((rows, width), bf16)]
        + [jax.ShapeDtypeStruct((rows, 2 * width), bf16)] * 4,
        compiler_params=pltpu.CompilerParams(vmem_limit_bytes=40 * 2**20),
        name="attend_back",
    )(queries, *blocks, grad, log_total)


def fc_outer(normed, grad_before, activated, grad_branch, add=None):
    rows, width = normed.shape
    wide = grad_before.shape[1]
    step = min(512, width)
    first = wide // step
    per = width // step
    blocks = first + (wide // width) * per
    second = lambda i: jnp.maximum(i - first, 0)

    def kernel(n_ref, b_ref, a_ref, g_ref, *rest):
        out_ref = rest[-1]
        i = pl.program_id(0)
        more = rest[0][...].astype(f32) if add is not None else 0.0

        @pl.when(i < first)
        def _():
            out_ref[...] = (mm(n_ref[...], b_ref[...]) + more).astype(bf16)

        @pl.when(i >= first)
        def _():
            out_ref[...] = (mm(a_ref[...], g_ref[...]) + more).astype(bf16)

    out_spec = pl.BlockSpec((width, step), lambda i: (0, i))
    in_specs = [
        pl.BlockSpec((width, rows), lambda i: (0, 0)),
        pl.BlockSpec((rows, step), lambda i: (0, jnp.minimum(i, first - 1))),
        pl.BlockSpec((width, rows), lambda i: (second(i) // per, 0)),
        pl.BlockSpec((rows, step), lambda i: (0, second(i) % per)),
    ]
    operands = [normed.T, grad_before, activated.T, grad_branch]
    if add is not None:
        in_specs.append(out_spec)
        operands.append(add)
    return pl.pallas_call(
        kernel,
        grid=(blocks,),
        in_specs=in_specs,
        out_specs=out_spec,
        out_shape=jax.ShapeDtypeStruct((width, blocks * step), bf16),
        compiler_params=pltpu.CompilerParams(vmem_limit_bytes=40 * 2**20),
        cost_estimate=pl.CostEstimate(
            flops=2 * rows * width * blocks * step,
            bytes_accessed=2 * width * blocks * step * (1 if add is None else 2),
            transcendentals=0,
        ),
        name="fc_outer",
    )(*operands)


def fc_sum(normed, grad_before, activated, grad_branch):
    parts = list(zip(grad_before, activated))
    sent = swap(fc_outer(normed, *parts[1], grad_branch), "core")
    return fc_outer(normed, *parts[0], grad_branch, add=sent)


FLIP = [(0, 0), (1, 2), (2, 1), (3, 3)]


def to_images(arrays):
    count, rows, width = arrays[0].shape
    mixed = jnp.stack(arrays, axis=1)
    mixed = lax.all_to_all(mixed, "z", split_axis=0, concat_axis=0, tiled=True)
    mixed = [mixed[:, i].reshape(count * rows, width) for i in range(len(arrays))]
    return [lax.ppermute(m, ("yh", "core"), FLIP) for m in mixed]


def from_images(arrays, count):
    rows, width = arrays[0].shape
    mixed = [lax.ppermute(a, ("yh", "core"), FLIP) for a in arrays]
    mixed = jnp.stack([m.reshape(count, rows // count, width) for m in mixed], axis=1)
    mixed = lax.all_to_all(mixed, "z", split_axis=0, concat_axis=0, tiled=True)
    return [mixed[:, i] for i in range(len(arrays))]


RING_Z, RING_Y = "z", ("yh", "yl")
AHEAD = [(i, (i + 1) % 4) for i in range(4)]
BACK = [(i, (i - 1) % 4) for i in range(4)]


def ring_place(value, axis, out_shapes, views):
    half = value.shape[0] // 2
    ahead = lax.ppermute(value, axis, AHEAD)
    back = lax.ppermute(value, axis, BACK)
    far_a = lax.ppermute(ahead[:half], axis, AHEAD)
    far_b = lax.ppermute(back[half:], axis, BACK)
    pieces = [(value, 0, 0), (ahead, 3, 0), (back, 1, 0), (far_a, 2, 0), (far_b, 2, half)]
    n_outs = len(out_shapes)

    def kernel(index_ref, *refs):
        sources, outs = refs[:5], refs[5:]
        for source, (_, step, start) in zip(sources, pieces):
            place = lax.rem(index_ref[0] + step, 4)
            views(outs, source, place, start)

    vmem = pl.BlockSpec(memory_space=pltpu.VMEM)
    return pl.pallas_call(
        kernel,
        in_specs=[pl.BlockSpec(memory_space=pltpu.SMEM)] + [vmem] * 5,
        out_specs=[vmem] * n_outs,
        out_shape=[jax.ShapeDtypeStruct(shape, value.dtype) for shape in out_shapes],
        compiler_params=pltpu.CompilerParams(vmem_limit_bytes=24 * 2**20),
        cost_estimate=pl.CostEstimate(
            flops=0, bytes_accessed=16 * value.size, transcendentals=0
        ),
        name="ring_place",
    )(lax.axis_index(axis).reshape(1), *(p[0] for p in pieces))


def in_order(outs, piece, place, start):
    outs[0][place, pl.ds(start, piece.shape[0])] = piece[...]


def ring_sum(blocks, axis):
    index = lax.axis_index(axis)
    block = lambda k: lax.dynamic_index_in_dim(blocks, (index + k) % 4, 0, keepdims=False)
    add = lambda *parts: sum(p.astype(f32) for p in parts).astype(bf16)
    far, after, before = block(2), block(1), block(3)
    half = far.shape[0] // 2
    low = lax.ppermute(far[:half], axis, AHEAD)
    high = lax.ppermute(far[half:], axis, BACK)
    after = jnp.concatenate([add(after[:half], low), after[half:]])
    before = jnp.concatenate([before[:half], add(before[half:], high)])
    after = lax.ppermute(after, axis, AHEAD)
    before = lax.ppermute(before, axis, BACK)
    return add(block(0), after, before)


def group_blocks(key_value):
    mate = swap(key_value, "core")
    near = swap(key_value, "yl")
    far = swap(near, "core")
    return (key_value, mate, near, far)


def group_sum(own, mate, near, far):
    mate, far = swap(mate, "core"), swap(far, "core")
    sent = (near.astype(f32) + far.astype(f32)).astype(bf16)
    kept = own.astype(f32) + mate.astype(f32)
    return (kept + swap(sent, "yl").astype(f32)).astype(bf16)


def normal_part(values):
    mean = jnp.mean(values, axis=-1, keepdims=True)
    centred = values - mean
    factor = lax.rsqrt(jnp.mean(centred * centred, axis=-1, keepdims=True) + EPSILON)
    return centred * factor, factor


def norm_back(grad, normal, factor, gain):
    e = grad * gain
    inner = jnp.mean(e * normal, axis=-1, keepdims=True)
    return factor * (e - jnp.mean(e, axis=-1, keepdims=True) - normal * inner)


def flip_halves(core, value):
    half = value.shape[-1] // 2
    turned = jnp.concatenate([value[..., half:], value[..., :half]], axis=-1)
    return jnp.where(core == 0, value, turned)


CHUNKS = 2


def chunked(halves):
    size = halves[0].shape[1] // CHUNKS
    cut = lambda h, i: h[:, i * size : (i + 1) * size]
    return [jnp.concatenate([cut(h, i) for h in halves], axis=1) for i in range(CHUNKS)]


def unchunked(chunks):
    size = chunks[0].shape[1] // 2
    return [
        jnp.concatenate([c[:, i * size : (i + 1) * size] for c in chunks], axis=1)
        for i in range(2)
    ]


def forward(tokens, w, late=None):
    inputs = tokens.astype(f32)
    normed_one = (normal_part(inputs)[0] * w["gain"][0] + w["shift"][0]).astype(bf16)
    project = lambda name: [
        (mm(normed_one, part) + bias).astype(bf16) for part, bias in zip(w[name], w[name + "_bias"])
    ]
    blocks = [group_blocks(c) for c in chunked(project("kv"))]
    queries = chunked(project("q"))
    if late is not None:
        blocks[0], gathered = lax.optimization_barrier((blocks[0], late[0]))
        w.update(late[1](gathered))
    attended, log_total = zip(*(attend(q, b) for q, b in zip(queries, blocks)))
    attended = jnp.concatenate(unchunked(attended), axis=1)
    attended = flip_halves(w["core"], attended)
    branch = flip_halves(w["core"], jnp.concatenate([mm(attended, p) for p in w["proj"]], axis=1))
    branch = branch + w["out_bias"][0]
    middle = inputs + w["scale"][0] * branch
    normed_two = (normal_part(middle)[0] * w["gain"][1] + w["shift"][1]).astype(bf16)
    activated, slope, branch_two = [], [], w["out_bias"][1]
    for up, bias, down in zip(w["fc1"], w["fc1_bias"], w["fc2"]):
        before = mm(normed_two, up) + bias
        phi = 0.5 * (1.0 + lax.erf(before * (0.5**0.5)))
        density = jnp.exp(-0.5 * before * before) * 0.3989422804014327
        active = (before * phi).astype(bf16)
        activated.append(active)
        slope.append((phi + before * density).astype(bf16))
        for i, part in enumerate(down):
            rows = part.shape[0]
            branch_two = branch_two + mm(active[:, i * rows : (i + 1) * rows], part)
    result = (middle + w["scale"][1] * branch_two).astype(bf16)
    kept = dict(
        inputs=inputs,
        normed_one=normed_one,
        queries=queries,
        blocks=blocks,
        attended=attended,
        log_total=log_total,
        branch=branch,
        middle=middle,
        normed_two=normed_two,
        activated=activated,
        slope=slope,
        branch_two=branch_two,
    )
    return result, kept


def backward(grad_out, kept, w, fc_sum=None):
    grad_branch_two = (w["scale"][1] * grad_out).astype(bf16)
    grad_before = []
    grad_normed_two = 0.0
    for up, down, slope in zip(w["fc1"], w["fc2"], kept["slope"]):
        part = jnp.concatenate([mm_t(grad_branch_two, d) for d in down], axis=1)
        part = (part * slope.astype(f32)).astype(bf16)
        grad_before.append(part)
        grad_normed_two = grad_normed_two + mm_t(part, up)
    normal_two, factor_two = normal_part(kept["middle"])
    grad_middle = grad_out + norm_back(grad_normed_two, normal_two, factor_two, w["gain"][1])
    grad_branch = (w["scale"][0] * grad_middle).astype(bf16)
    width = grad_branch.shape[1]
    half = width // 2
    grad_halves = flip_halves(w["core"], grad_branch)
    grad_halves = [grad_halves[:, :half], grad_halves[:, half:]]
    grad_attended = sum(mm_t(g, p) for g, p in zip(grad_halves, w["proj"])).astype(bf16)
    grad_attended = flip_halves(w["core"], grad_attended)
    fc_grad = None
    if fc_sum is not None:
        fc_grad = fc_sum(
            kept["normed_two"], grad_before, kept["activated"], grad_branch_two
        )
        fc_grad, grad_attended = lax.optimization_barrier((fc_grad, grad_attended))
    grad_chunks = chunked([grad_attended[:, :half], grad_attended[:, half:]])
    q_chunks, kv_chunks = [], []
    for q, b, g, t in zip(kept["queries"], kept["blocks"], grad_chunks, kept["log_total"]):
        parts = attend_back(q, b, g, t)
        q_chunks.append(parts[0])
        kv_chunks.append(group_sum(*parts[1:]))
    grad_q, grad_kv = unchunked(q_chunks), unchunked(kv_chunks)
    grad_normed_one = sum(
        mm_t(g, part) for g, part in zip(grad_q + grad_kv, w["q"] + w["kv"])
    )
    normal_one, factor_one = normal_part(kept["inputs"])
    grad_inputs = grad_middle + norm_back(grad_normed_one, normal_one, factor_one, w["gain"][0])
    total = lambda a: jnp.sum(a.astype(f32), axis=0)
    vectors = dict(
        gain=(total(grad_normed_one * normal_one), total(grad_normed_two * normal_two)),
        shift=(total(grad_normed_one), total(grad_normed_two)),
        out_bias=(total(grad_branch), total(grad_branch_two)),
        scale=(total(grad_middle * kept["branch"]), total(grad_out * kept["branch_two"])),
        q=[total(g) for g in grad_q],
        kv=[total(g) for g in grad_kv],
        fc1_bias=[total(g) for g in grad_before],
    )
    outer = dict(
        q=(kept["normed_one"], grad_q),
        kv=(kept["normed_one"], grad_kv),
        proj=(kept["attended"], grad_halves),
        fc=fc_grad,
    )
    return grad_inputs.astype(bf16), vectors, outer


def ordered(core, mine, other):
    return jnp.where(core == 0, mine, other), jnp.where(core == 0, other, mine)


def per_device(
    patch_tokens,
    out_grad,
    batch_counts,
    norm_gain,
    norm_bias,
    qkv_weight,
    qv_bias,
    proj_weight,
    fc1_weight,
    fc1_bias,
    fc2_weight,
    out_bias,
    layer_scale,
):
    section = lax.axis_index("section")
    core = lax.axis_index("core")
    shards = lax.axis_size(FSDP)
    images, rows, width = patch_tokens.shape
    half = width // 2
    own = width // shards
    hidden = fc2_weight.shape[1]
    mid = hidden // 2
    groups = half // PAIR
    pick = lambda a, i, axis: lax.dynamic_index_in_dim(a, i, axis, keepdims=False)

    part = mid // 2
    q, k, v = (qkv_weight[0][:, i * width : (i + 1) * width] for i in range(3))
    q_mine = pick(q.reshape(own, 2, half), core, 1)
    kv = jnp.stack([k.reshape(own, 2, groups, PAIR), v.reshape(own, 2, groups, PAIR)], axis=3)
    kv_mine = pick(kv, core, 1).reshape(own, width)
    proj_mine = pick(proj_weight[0].reshape(own, 2, half), core, 1)
    vectors = jnp.concatenate(
        [a[0] for a in (norm_gain, norm_bias, qv_bias, out_bias, layer_scale)]
        + [fc1_bias[0].reshape(own, hidden // own).T],
        axis=0,
    ).T
    count = vectors.shape[1]
    vectors = jnp.pad(vectors, ((0, 0), (0, 128 - count)))
    fc1_mine = pick(fc1_weight[0].reshape(own, shards, 2, 2, part), core, 2)
    fc1_mine = jnp.swapaxes(fc1_mine, 1, 2).reshape(own, shards * mid)
    fc2_mine = pick(fc2_weight[0].reshape(2, 2, part, width), core, 0)
    fc_mine = jnp.concatenate([fc1_mine, fc2_mine[0], fc2_mine[1]], axis=1)
    fc_half = lax.all_gather(fc_mine, FSDP, axis=0, tiled=True)

    a_mine = jnp.concatenate([q_mine, proj_mine, vectors], axis=1)
    a_row = ring_place(a_mine, RING_Y, [(4, own, a_mine.shape[1])], in_order)[0]
    a_row = a_row.reshape(4 * own, a_mine.shape[1])
    b_row = ring_place(kv_mine, RING_Z, [(4, own, width)], in_order)[0]

    def a_views(outs, piece, place, start):
        at = 0
        for out in outs:
            size = out.shape[-1]
            out[place, pl.ds(start, piece.shape[0])] = piece[:, pl.ds(at, size)]
            at += size

    def b_views(outs, piece, place, start):
        for i in range(piece.shape[0]):
            outs[0][start + i, place] = piece[i]

    q_half, proj_half, vectors = (
        o.reshape(width, -1)
        for o in ring_place(
            a_row, RING_Z, [(4, 4 * own, half), (4, 4 * own, half), (4, 4 * own, 128)], a_views
        )
    )
    kv_half = ring_place(b_row, RING_Y, [(4, 4, own, width)], b_views)[0].reshape(width, width)
    vectors = vectors[:, :count].T.astype(f32)
    fc1_b = vectors[10:].T.reshape(shards, 2, 2, part)

    def halves(vector):
        pair = vector.reshape(2, half)
        return pick(pair, core, 0), pick(pair, 1 - core, 0)

    def kv_bias(v_half):
        v_part = v_half.reshape(groups, 1, PAIR)
        return jnp.concatenate([jnp.zeros_like(v_part), v_part], axis=1).reshape(width)

    wide = shards * mid
    w = dict(
        core=core,
        gain=vectors[0:2],
        shift=vectors[2:4],
        out_bias=vectors[6:8],
        scale=vectors[8:10],
        q=[q_half, swap(q_half, "core")],
        q_bias=halves(vectors[4]),
        kv=[kv_half, swap(kv_half, "core")],
        kv_bias=[kv_bias(b) for b in halves(vectors[5])],
        proj=(proj_half, swap(proj_half, "core")),
        fc1_bias=[
            jnp.swapaxes(pick(fc1_b, c, 1), 0, 1).reshape(-1) for c in (core, 1 - core)
        ],
    )

    def fc_weights(gathered):
        pair = (gathered, swap(gathered, "core"))
        return dict(
            fc1=[f[:, :wide] for f in pair],
            fc2=[(f[:, wide : wide + width], f[:, wide + width :]) for f in pair],
        )


    live = (
        jnp.arange(images) % IMG_MB < jnp.repeat(batch_counts[0], IMG_MB)
    ).astype(bf16)
    first_tokens, last_grad = to_images([patch_tokens, out_grad * live[:, None, None]])

    sent, _ = forward(first_tokens, w, late=(fc_half, fc_weights))
    passed = lax.ppermute(sent, "section", [(0, 1)])
    tokens = jnp.where(section == 0, first_tokens, passed)
    result, kept = forward(tokens, w)

    sent, _, _ = backward(last_grad.astype(f32), kept, w)
    passed = lax.ppermute(sent, "section", [(1, 0)])
    grad_out = jnp.where(section == 1, last_grad, passed).astype(f32)
    grad_inputs, sums, outer = backward(grad_out, kept, w, fc_sum)
    result, grad_inputs = lax.optimization_barrier((result, grad_inputs))
    block_out, in_grad = from_images([result, grad_inputs], images)

    def core_sum(mine, other):
        return (mine + swap(other.astype(bf16), "core").astype(f32)).astype(bf16)

    def natural(pair):
        return jnp.concatenate(ordered(core, *pair))

    v_sum = lambda a: a.reshape(groups, 2, PAIR)[:, 1].reshape(half)
    fc1_sum = jnp.stack(
        ordered(
            core, *(jnp.swapaxes(s.reshape(2, shards, part), 0, 1) for s in sums["fc1_bias"])
        ),
        axis=1,
    ).reshape(width, hidden // own)
    vector_grads = jnp.concatenate(
        [
            jnp.stack(
                [
                    *sums["gain"],
                    *sums["shift"],
                    natural(sums["q"]),
                    natural([v_sum(g) for g in sums["kv"]]),
                    *sums["out_bias"],
                    *sums["scale"],
                ],
                axis=1,
            ),
            fc1_sum,
        ],
        axis=1,
    )
    vector_grads = jnp.pad(vector_grads, ((0, 0), (0, 128 - count)))

    fc_grad = lax.psum_scatter(outer["fc"], FSDP, scatter_dimension=0, tiled=True)
    a1, dq = outer["q"]
    dkv = outer["kv"][1]
    o, e1 = outer["proj"]
    a_parts = [
        jnp.concatenate([t_mm(a1, dq[i]), t_mm(o, e1[i]), vector_grads], axis=1) for i in range(2)
    ]
    b_parts = [t_mm(a1, dkv[i]) for i in range(2)]
    b_sum = ring_sum(core_sum(*b_parts).reshape(4, 4, own, width), RING_Z)
    b_grad = ring_sum(b_sum, RING_Y)
    a_blocks = core_sum(*a_parts).reshape(4, 4, own, width + 128)
    a_sum = ring_sum(jnp.swapaxes(a_blocks, 0, 1), RING_Y)
    a_grad = ring_sum(a_sum, RING_Z)

    parts = [a_grad, b_grad, fc_grad]
    parts = [(a.astype(f32) + swap(a, "xhi").astype(f32)).astype(bf16) for a in parts]
    vec_grad = parts[0][:, width : width + count].T.astype(f32)
    others = [swap(a, "core") for a in parts]
    a_pair, b_pair, fc_pair = (
        ordered(core, a.astype(f32), b.astype(f32)) for a, b in zip(parts, others)
    )
    q_grad = jnp.concatenate([p[:, :half] for p in a_pair], axis=1)
    proj_out = jnp.concatenate([p[:, half:width] for p in a_pair], axis=1)
    kv_grads = [p.reshape(own, groups, 2, PAIR) for p in b_pair]
    k_grad, v_grad = (
        jnp.concatenate([p[:, :, i].reshape(own, half) for p in kv_grads], axis=1)
        for i in range(2)
    )
    qkv_out = jnp.concatenate([q_grad, k_grad, v_grad], axis=1)
    fc1_out = jnp.stack(
        [jnp.swapaxes(p[:, :wide].reshape(own, 2, shards, part), 1, 2) for p in fc_pair], axis=2
    ).reshape(own, 2 * wide)
    fc2_out = jnp.concatenate(
        [p[:, wide + i * width : wide + (i + 1) * width] for p in fc_pair for i in range(2)], axis=0
    )
    return (
        block_out[None],
        in_grad[None],
        vec_grad[0:2][None],
        vec_grad[2:4][None],
        qkv_out[None],
        vec_grad[4:6][None],
        proj_out[None],
        fc1_out[None],
        vec_grad[10:].T.reshape(1, hidden),
        fc2_out[None],
        vec_grad[6:8][None],
        vec_grad[8:10][None],
    )


def solution(mesh):
    sections, fsdp, rep = mesh.devices.shape
    inner = Mesh(
        mesh.devices.reshape(sections, fsdp // 4, 2, 2, rep // 2, 2),
        ("section",) + FSDP + REP,
    )
    weight = P("section", FSDP, None)
    vector = P("section", None, FSDP)
    tokens = P(REP, FSDP, None)
    both = P("section", REP, FSDP, None)
    return jax.shard_map(
        per_device,
        mesh=inner,
        in_specs=(
            tokens,
            tokens,
            P(REP, None),
            vector,
            vector,
            weight,
            vector,
            weight,
            weight,
            P("section", FSDP),
            weight,
            vector,
            vector,
        ),
        out_specs=(
            both,
            both,
            vector,
            vector,
            weight,
            vector,
            weight,
            weight,
            P("section", FSDP),
            weight,
            vector,
            vector,
        ),
        check_vma=False,
    )
```

```python
import jax
import jax.numpy as jnp
from jax import lax
from jax.experimental import pallas as pl
from jax.experimental.pallas import tpu as pltpu
from jax.sharding import Mesh, PartitionSpec as P

HEAD_DIM = 64
IMG_MB = 2
PAIR = 2 * HEAD_DIM
EPSILON = 1e-06

FSDP = ("z", "yh", "yl")
REP = ("xhi", "core")
bf16 = jnp.bfloat16
f32 = jnp.float32


def dot(a, b, dims):
    return lax.dot_general(a, b, (dims, ((), ())), preferred_element_type=f32)


def mm(a, b):
    return dot(a, b, ((1,), (0,)))


def mm_t(a, b):
    return dot(a, b, ((1,), (1,)))


def t_mm(a, b):
    return dot(a, b, ((0,), (0,)))


def swap(value, axis):
    return lax.ppermute(value, axis, [(0, 1), (1, 0)])


def attend_kernel(q_ref, own_ref, mate_ref, near_ref, far_ref, out_ref, log_ref):
    rows = q_ref.shape[0]
    both = [r[...] for r in (own_ref, mate_ref, near_ref, far_ref)]
    keys = jnp.concatenate([b[:, :PAIR] for b in both], axis=0)
    values = jnp.concatenate([b[:, PAIR:] for b in both], axis=0)
    queries = q_ref[...] * jnp.asarray(HEAD_DIM**-0.5, bf16)
    lane = lax.broadcasted_iota(jnp.int32, (rows, PAIR), 1)
    outs = []
    for head in range(2):
        mine = (lane >= head * HEAD_DIM) & (lane < (head + 1) * HEAD_DIM)
        picked = jnp.where(mine, queries, jnp.zeros_like(queries))
        scores = mm_t(keys, picked)
        top = jnp.max(scores, axis=0, keepdims=True)
        raised = jnp.exp(scores - top)
        total = jnp.sum(raised, axis=0, keepdims=True)
        out = t_mm(values, raised.astype(bf16))
        outs.append(out * (1.0 / total))
        log_ref[0, head : head + 1, :] = top + jnp.log(total)
    row = lax.broadcasted_iota(jnp.int32, (PAIR, rows), 0)
    joined = jnp.where(row < HEAD_DIM, outs[0], outs[1])
    out_ref[...] = joined.T.astype(bf16)


def attend_back_kernel(
    q_ref, own_ref, mate_ref, near_ref, far_ref, grad_ref, log_ref, dq_ref, *dkv_refs
):
    rows = q_ref.shape[0]
    both = [r[...] for r in (own_ref, mate_ref, near_ref, far_ref)]
    keys = jnp.concatenate([b[:, :PAIR] for b in both], axis=0)
    values = jnp.concatenate([b[:, PAIR:] for b in both], axis=0)
    queries = q_ref[...] * jnp.asarray(HEAD_DIM**-0.5, bf16)
    grads = grad_ref[...]
    lane = lax.broadcasted_iota(jnp.int32, (rows, PAIR), 1)
    dqs, dk, dv = [], None, None
    for head in range(2):
        mine = (lane >= head * HEAD_DIM) & (lane < (head + 1) * HEAD_DIM)
        picked = jnp.where(mine, queries, jnp.zeros_like(queries))
        grad = jnp.where(mine, grads, jnp.zeros_like(grads))
        scores = mm_t(keys, picked)
        weighting = jnp.exp(scores - log_ref[0, head : head + 1, :])
        grad_weighting = mm_t(values, grad)
        row_term = jnp.sum(grad_weighting * weighting, axis=0, keepdims=True)
        grad_scores = (weighting * (grad_weighting - row_term)).astype(bf16)
        dqs.append(t_mm(keys, grad_scores))
        k_part = mm(grad_scores, picked)
        v_part = mm(weighting.astype(bf16), grad)
        dk = k_part if dk is None else dk + k_part
        dv = v_part if dv is None else dv + v_part
    row = lax.broadcasted_iota(jnp.int32, (PAIR, rows), 0)
    joined = jnp.where(row < HEAD_DIM, dqs[0], dqs[1]) * (HEAD_DIM**-0.5)
    dq_ref[...] = joined.T.astype(bf16)
    for i, ref in enumerate(dkv_refs):
        ref[:, :PAIR] = dk[i * rows : (i + 1) * rows].astype(bf16)
        ref[:, PAIR:] = dv[i * rows : (i + 1) * rows].astype(bf16)


def pair_specs(rows, pairs):
    half = pairs // 2
    q_spec = pl.BlockSpec((rows, PAIR), lambda i: (0, i))
    kv_spec = pl.BlockSpec((rows, 2 * PAIR), lambda i: (0, i))
    kv_swapped = pl.BlockSpec((rows, 2 * PAIR), lambda i: (0, (i + half) % pairs))
    log_spec = pl.BlockSpec((1, 2, rows), lambda i: (i, 0, 0))
    return q_spec, [kv_spec, kv_swapped, kv_spec, kv_swapped], log_spec


def attend_cost(queries, blocks, products):
    rows, width = queries.shape
    scores = rows * rows * len(blocks) * width // HEAD_DIM
    return pl.CostEstimate(
        flops=products * scores * 2 * 256,
        bytes_accessed=2 * 2 * len(blocks) * rows * width * 2,
        transcendentals=scores,
    )


def attend(queries, blocks):
    rows, width = queries.shape
    pairs = width // PAIR
    q_spec, kv_specs, log_spec = pair_specs(rows, pairs)
    return pl.pallas_call(
        attend_kernel,
        grid=(pairs,),
        in_specs=[q_spec] + kv_specs,
        out_specs=[q_spec, log_spec],
        out_shape=[
            jax.ShapeDtypeStruct((rows, width), bf16),
            jax.ShapeDtypeStruct((pairs, 2, rows), f32),
        ],
        compiler_params=pltpu.CompilerParams(vmem_limit_bytes=40 * 2**20),
        cost_estimate=attend_cost(queries, blocks, 2),
        name="attend",
    )(queries, *blocks)


def attend_back(queries, blocks, grad, log_total):
    rows, width = queries.shape
    pairs = width // PAIR
    q_spec, kv_specs, log_spec = pair_specs(rows, pairs)
    return pl.pallas_call(
        attend_back_kernel,
        grid=(pairs,),
        in_specs=[q_spec] + kv_specs + [q_spec, log_spec],
        out_specs=[q_spec] + kv_specs,
        out_shape=[jax.ShapeDtypeStruct((rows, width), bf16)]
        + [jax.ShapeDtypeStruct((rows, 2 * width), bf16)] * 4,
        compiler_params=pltpu.CompilerParams(vmem_limit_bytes=40 * 2**20),
        cost_estimate=attend_cost(queries, blocks, 5),
        name="attend_back",
    )(queries, *blocks, grad, log_total)


def outer(segments, step, add=None, tail=None):
    rows = segments[0][1].shape[0]
    width = segments[0][2]
    counts = [right.shape[1] // step for _, right, _ in segments]
    starts = [sum(counts[:k]) for k in range(len(counts))]
    total = sum(counts)
    grid = total + (tail is not None)
    n = len(segments)

    def kernel(*refs):
        out_ref = refs[-1]
        i = pl.program_id(0)
        for k in range(n):

            @pl.when((i >= starts[k]) & (i < starts[k] + counts[k]))
            def _(k=k):
                value = t_mm(refs[2 * k][...], refs[2 * k + 1][...])
                if add is not None:
                    value = value + refs[2 * n][...].astype(f32)
                out_ref[...] = value.astype(bf16)

        if tail is not None:

            @pl.when(i == total)
            def _():
                out_ref[...] = refs[2 * n + (add is not None)][...]

    in_specs, operands = [], []
    for (left, right, _), start, count in zip(segments, starts, counts):
        array, which = left
        in_specs.append(pl.BlockSpec((rows, width), lambda i, w=which: (0, w)))
        in_specs.append(
            pl.BlockSpec((rows, step), lambda i, s=start, c=count: (0, jnp.clip(i - s, 0, c - 1)))
        )
        operands += [array, right]
    if add is not None:
        in_specs.append(pl.BlockSpec((width, step), lambda i: (0, jnp.minimum(i, total - 1))))
        operands.append(add)
    if tail is not None:
        in_specs.append(pl.BlockSpec((width, step), lambda i: (0, 0)))
        operands.append(tail)
    return pl.pallas_call(
        kernel,
        grid=(grid,),
        in_specs=in_specs,
        out_specs=pl.BlockSpec((width, step), lambda i: (0, i)),
        out_shape=jax.ShapeDtypeStruct((width, grid * step), bf16),
        compiler_params=pltpu.CompilerParams(vmem_limit_bytes=40 * 2**20),
        cost_estimate=pl.CostEstimate(
            flops=2 * rows * width * total * step,
            bytes_accessed=2 * width * grid * step * (1 if add is None else 2),
            transcendentals=0,
        ),
        name="outer",
    )(*operands)


def fc1_sum(normed, grad_before):
    width = normed.shape[1]
    make = lambda g, add=None: outer([((normed, 0), g, width)], 512, add=add)
    return make(grad_before[0], swap(make(grad_before[1]), "core"))


def fc2_sum(activated, grad_branch):
    width = grad_branch.shape[1]
    make = lambda z, add=None: outer(
        [((z, i), grad_branch, width) for i in range(z.shape[1] // width)], 512, add=add
    )
    return make(activated[0], swap(make(activated[1]), "core"))


FLIP = [(0, 0), (1, 2), (2, 1), (3, 3)]


def to_images(tokens):
    count, rows, width = tokens.shape
    mixed = lax.all_to_all(tokens, "z", split_axis=0, concat_axis=0, tiled=True)
    return lax.ppermute(mixed.reshape(count * rows, width), ("yh", "core"), FLIP)


def from_images(arrays, count):
    rows, width = arrays[0].shape
    mixed = [lax.ppermute(a, ("yh", "core"), FLIP) for a in arrays]
    mixed = jnp.stack([m.reshape(count, rows // count, width) for m in mixed], axis=1)
    mixed = lax.all_to_all(mixed, "z", split_axis=0, concat_axis=0, tiled=True)
    return [mixed[:, i] for i in range(len(arrays))]


RING_Z, RING_Y = "z", ("yh", "yl")
AHEAD = [(i, (i + 1) % 4) for i in range(4)]
BACK = [(i, (i - 1) % 4) for i in range(4)]


ACROSS = [(i, (i + 2) % 4) for i in range(4)]


def ring_place(value, axis, out_shapes, views, direct=False):
    half = value.shape[0] // 2
    ahead = lax.ppermute(value, axis, AHEAD)
    back = lax.ppermute(value, axis, BACK)
    pieces = [(value, 0, 0), (ahead, 3, 0), (back, 1, 0)]
    if direct:
        pieces.append((lax.ppermute(value, axis, ACROSS), 2, 0))
    else:
        pieces.append((lax.ppermute(ahead[:half], axis, AHEAD), 2, 0))
        pieces.append((lax.ppermute(back[half:], axis, BACK), 2, half))
    n_outs = len(out_shapes)

    def kernel(index_ref, *refs):
        sources, outs = refs[: len(pieces)], refs[len(pieces) :]
        for source, (_, step, start) in zip(sources, pieces):
            place = lax.rem(index_ref[0] + step, 4)
            views(outs, source, place, start)

    vmem = pl.BlockSpec(memory_space=pltpu.VMEM)
    return pl.pallas_call(
        kernel,
        in_specs=[pl.BlockSpec(memory_space=pltpu.SMEM)] + [vmem] * len(pieces),
        out_specs=[vmem] * n_outs,
        out_shape=[jax.ShapeDtypeStruct(shape, value.dtype) for shape in out_shapes],
        compiler_params=pltpu.CompilerParams(vmem_limit_bytes=24 * 2**20),
        cost_estimate=pl.CostEstimate(
            flops=0, bytes_accessed=16 * value.size, transcendentals=0
        ),
        name="ring_place",
    )(lax.axis_index(axis).reshape(1), *(p[0] for p in pieces))


def in_order(outs, piece, place, start):
    outs[0][place, pl.ds(start, piece.shape[0])] = piece[...]


def ring_sum(blocks, axis, dim, direct=False):
    index = lax.axis_index(axis)
    block = lambda k: lax.dynamic_index_in_dim(blocks, (index + k) % 4, dim, keepdims=False)
    add = lambda *parts: sum(p.astype(f32) for p in parts).astype(bf16)
    if direct:
        ways = [(1, AHEAD), (3, BACK), (2, ACROSS)]
        return add(block(0), *(lax.ppermute(block(k), axis, way) for k, way in ways))
    far, after, before = block(2), block(1), block(3)
    half = far.shape[0] // 2
    low = lax.ppermute(far[:half], axis, AHEAD)
    high = lax.ppermute(far[half:], axis, BACK)
    after = jnp.concatenate([add(after[:half], low), after[half:]])
    before = jnp.concatenate([before[:half], add(before[half:], high)])
    after = lax.ppermute(after, axis, AHEAD)
    before = lax.ppermute(before, axis, BACK)
    return add(block(0), after, before)


def group_blocks(key_value):
    mate = swap(key_value, "core")
    near = swap(key_value, "yl")
    far = swap(near, "core")
    return (key_value, mate, near, far)


def group_parts(own, mate, near, far):
    mate, far = swap(mate, "core"), swap(far, "core")
    sent = (near.astype(f32) + far.astype(f32)).astype(bf16)
    return own.astype(f32) + mate.astype(f32), sent


def group_add(kept, sent):
    return (kept + swap(sent, "yl").astype(f32)).astype(bf16)


def normal_part(values):
    mean = jnp.mean(values, axis=-1, keepdims=True)
    centred = values - mean
    factor = lax.rsqrt(jnp.mean(centred * centred, axis=-1, keepdims=True) + EPSILON)
    return centred * factor, factor


def norm_back(grad, normal, factor, gain):
    e = grad * gain
    inner = jnp.mean(e * normal, axis=-1, keepdims=True)
    return factor * (e - jnp.mean(e, axis=-1, keepdims=True) - normal * inner)


def flip_halves(core, value):
    half = value.shape[-1] // 2
    turned = jnp.concatenate([value[..., half:], value[..., :half]], axis=-1)
    return jnp.where(core == 0, value, turned)


CHUNKS = 2


def chunked(halves):
    size = halves[0].shape[1] // CHUNKS
    cut = lambda h, i: h[:, i * size : (i + 1) * size]
    return [jnp.concatenate([cut(h, i) for h in halves], axis=1) for i in range(CHUNKS)]


def unchunked(chunks):
    size = chunks[0].shape[1] // 2
    return [
        jnp.concatenate([c[:, i * size : (i + 1) * size] for c in chunks], axis=1)
        for i in range(2)
    ]


def forward(tokens, w, late=None):
    inputs = tokens.astype(f32)
    normed_one = (normal_part(inputs)[0] * w["gain"][0] + w["shift"][0]).astype(bf16)
    project = lambda name: [
        (mm(normed_one, part) + bias).astype(bf16) for part, bias in zip(w[name], w[name + "_bias"])
    ]
    key_value = chunked(project("kv"))
    if late is not None:
        key_value, gathered = lax.optimization_barrier((key_value, late[0]))
        w.update(late[1](gathered))
    blocks = [group_blocks(key_value[0])]
    for c in key_value[1:]:
        c, near = lax.optimization_barrier((c, blocks[-1][2]))
        blocks[-1] = (*blocks[-1][:2], near, blocks[-1][3])
        blocks.append(group_blocks(c))
    queries = chunked(project("q"))
    attended, log_total = zip(*(attend(q, b) for q, b in zip(queries, blocks)))
    attended = jnp.concatenate(unchunked(attended), axis=1)
    attended = flip_halves(w["core"], attended)
    branch = flip_halves(w["core"], jnp.concatenate([mm(attended, p) for p in w["proj"]], axis=1))
    branch = branch + w["out_bias"][0]
    middle = inputs + w["scale"][0] * branch
    normed_two = (normal_part(middle)[0] * w["gain"][1] + w["shift"][1]).astype(bf16)
    activated, slope, branch_two = [], [], w["out_bias"][1]
    for up, bias, down in zip(w["fc1"], w["fc1_bias"], w["fc2"]):
        before = mm(normed_two, up) + bias
        phi = 0.5 * (1.0 + lax.erf(before * (0.5**0.5)))
        density = jnp.exp(-0.5 * before * before) * 0.3989422804014327
        active = (before * phi).astype(bf16)
        activated.append(active)
        slope.append((phi + before * density).astype(bf16))
        for i, part in enumerate(down):
            rows = part.shape[0]
            branch_two = branch_two + mm(active[:, i * rows : (i + 1) * rows], part)
    result = (middle + w["scale"][1] * branch_two).astype(bf16)
    kept = dict(
        inputs=inputs,
        normed_one=normed_one,
        queries=queries,
        blocks=blocks,
        attended=attended,
        log_total=log_total,
        branch=branch,
        middle=middle,
        normed_two=normed_two,
        activated=activated,
        slope=slope,
        branch_two=branch_two,
    )
    return result, kept


def backward(grad_out, kept, w, last=False):
    grad_branch_two = (w["scale"][1] * grad_out).astype(bf16)
    grad_before = []
    grad_normed_two = 0.0
    if last:
        fc2 = fc2_sum(kept["activated"], grad_branch_two)
    for up, down, slope in zip(w["fc1"], w["fc2"], kept["slope"]):
        part = jnp.concatenate([mm_t(grad_branch_two, d) for d in down], axis=1)
        part = (part * slope.astype(f32)).astype(bf16)
        grad_before.append(part)
        grad_normed_two = grad_normed_two + mm_t(part, up)
    normal_two, factor_two = normal_part(kept["middle"])
    grad_middle = grad_out + norm_back(grad_normed_two, normal_two, factor_two, w["gain"][1])
    grad_branch = (w["scale"][0] * grad_middle).astype(bf16)
    width = grad_branch.shape[1]
    half = width // 2
    grad_halves = flip_halves(w["core"], grad_branch)
    grad_halves = [grad_halves[:, :half], grad_halves[:, half:]]
    grad_attended = sum(mm_t(g, p) for g, p in zip(grad_halves, w["proj"])).astype(bf16)
    grad_attended = flip_halves(w["core"], grad_attended)
    fc_grad = None
    if last:
        fc_grad = [fc1_sum(kept["normed_two"], grad_before), fc2]
        fc_grad, grad_attended = lax.optimization_barrier((fc_grad, grad_attended))
    grad_chunks = chunked([grad_attended[:, :half], grad_attended[:, half:]])
    q_chunks, kv_chunks = [], []
    ready = None
    for q, b, g, t in zip(kept["queries"], kept["blocks"], grad_chunks, kept["log_total"]):
        if ready is not None:
            sent, g = lax.optimization_barrier((ready[1], g))
            kv_chunks.append(group_add(ready[0], sent))
        parts = attend_back(q, b, g, t)
        q_chunks.append(parts[0])
        ready = group_parts(*parts[1:])
    kv_chunks.append(group_add(*ready))
    grad_q, grad_kv = unchunked(q_chunks), unchunked(kv_chunks)
    grad_normed_one = sum(
        mm_t(g, part) for g, part in zip(grad_q + grad_kv, w["q"] + w["kv"])
    )
    normal_one, factor_one = normal_part(kept["inputs"])
    grad_inputs = grad_middle + norm_back(grad_normed_one, normal_one, factor_one, w["gain"][0])
    total = lambda a: jnp.sum(a.astype(f32), axis=0)
    vectors = dict(
        gain=(total(grad_normed_one * normal_one), total(grad_normed_two * normal_two)),
        shift=(total(grad_normed_one), total(grad_normed_two)),
        out_bias=(total(grad_branch), total(grad_branch_two)),
        scale=(total(grad_middle * kept["branch"]), total(grad_out * kept["branch_two"])),
        q=[total(g) for g in grad_q],
        kv=[total(g) for g in grad_kv],
        fc1_bias=[total(g) for g in grad_before],
    )
    products = dict(
        q=(kept["normed_one"], grad_q),
        kv=(kept["normed_one"], grad_kv),
        proj=(kept["attended"], grad_halves),
        fc=fc_grad,
    )
    return grad_inputs.astype(bf16), vectors, products


def ordered(core, mine, other):
    return jnp.where(core == 0, mine, other), jnp.where(core == 0, other, mine)


def per_device(
    patch_tokens,
    out_grad,
    batch_counts,
    norm_gain,
    norm_bias,
    qkv_weight,
    qv_bias,
    proj_weight,
    fc1_weight,
    fc1_bias,
    fc2_weight,
    out_bias,
    layer_scale,
):
    section = lax.axis_index("section")
    core = lax.axis_index("core")
    shards = lax.axis_size(FSDP)
    images, rows, width = patch_tokens.shape
    half = width // 2
    own = width // shards
    hidden = fc2_weight.shape[1]
    mid = hidden // 2
    groups = half // PAIR
    pick = lambda a, i, axis: lax.dynamic_index_in_dim(a, i, axis, keepdims=False)

    part = mid // 2
    q, k, v = (qkv_weight[0][:, i * width : (i + 1) * width] for i in range(3))
    q_mine = pick(q.reshape(own, 2, half), core, 1)
    kv = jnp.stack([k.reshape(own, 2, groups, PAIR), v.reshape(own, 2, groups, PAIR)], axis=3)
    kv_mine = pick(kv, core, 1).reshape(own, width)
    proj_mine = pick(proj_weight[0].reshape(own, 2, half), core, 1)
    vectors = jnp.concatenate(
        [a[0] for a in (norm_gain, norm_bias, qv_bias, out_bias, layer_scale)]
        + [fc1_bias[0].reshape(own, hidden // own).T],
        axis=0,
    ).T
    count = vectors.shape[1]
    vectors = jnp.pad(vectors, ((0, 0), (0, 128 - count)))
    fc1_mine = pick(fc1_weight[0].reshape(own, shards, 2, 2, part), core, 2)
    fc1_mine = jnp.swapaxes(fc1_mine, 1, 2).reshape(own, shards * mid)
    fc2_mine = pick(fc2_weight[0].reshape(2, 2, part, width), core, 0)
    fc_mine = jnp.concatenate([fc1_mine, fc2_mine[0], fc2_mine[1]], axis=1)

    a_mine = jnp.concatenate([q_mine, proj_mine, vectors], axis=1)
    first_tokens = to_images(patch_tokens)
    a_row = ring_place(a_mine, RING_Y, [(4, own, a_mine.shape[1])], in_order, direct=True)[0]
    b_row = ring_place(kv_mine, RING_Z, [(4, own, width)], in_order, direct=True)[0]
    a_row, b_row, fc_mine = lax.optimization_barrier((a_row, b_row, fc_mine))
    fc_half = lax.all_gather(fc_mine, FSDP, axis=0, tiled=True)
    a_row = a_row.reshape(4 * own, a_mine.shape[1])

    def a_views(outs, piece, place, start):
        at = 0
        for out in outs:
            size = out.shape[-1]
            out[place, pl.ds(start, piece.shape[0])] = piece[:, pl.ds(at, size)]
            at += size

    def b_views(outs, piece, place, start):
        for i in range(piece.shape[0]):
            outs[0][start + i, place] = piece[i]

    q_half, proj_half, vectors = (
        o.reshape(width, -1)
        for o in ring_place(
            a_row, RING_Z, [(4, 4 * own, half), (4, 4 * own, half), (4, 4 * own, 128)], a_views
        )
    )
    kv_half = ring_place(b_row, RING_Y, [(4, 4, own, width)], b_views)[0].reshape(width, width)
    vectors = vectors[:, :count].T.astype(f32)
    fc1_b = vectors[10:].T.reshape(shards, 2, 2, part)

    def halves(vector):
        pair = vector.reshape(2, half)
        return pick(pair, core, 0), pick(pair, 1 - core, 0)

    def kv_bias(v_half):
        v_part = v_half.reshape(groups, 1, PAIR)
        return jnp.concatenate([jnp.zeros_like(v_part), v_part], axis=1).reshape(width)

    wide = shards * mid
    w = dict(
        core=core,
        gain=vectors[0:2],
        shift=vectors[2:4],
        out_bias=vectors[6:8],
        scale=vectors[8:10],
        q=[q_half, swap(q_half, "core")],
        q_bias=halves(vectors[4]),
        kv=[kv_half, swap(kv_half, "core")],
        kv_bias=[kv_bias(b) for b in halves(vectors[5])],
        proj=(proj_half, swap(proj_half, "core")),
        fc1_bias=[
            jnp.swapaxes(pick(fc1_b, c, 1), 0, 1).reshape(-1) for c in (core, 1 - core)
        ],
    )

    def fc_weights(gathered):
        pair = (gathered, swap(gathered, "core"))
        return dict(
            fc1=[f[:, :wide] for f in pair],
            fc2=[(f[:, wide : wide + width], f[:, wide + width :]) for f in pair],
        )


    live = (
        jnp.arange(images) % IMG_MB < jnp.repeat(batch_counts[0], IMG_MB)
    ).astype(bf16)

    sent, _ = forward(first_tokens, w, late=(fc_half, fc_weights))
    live_grad = out_grad * live[:, None, None]
    sent, live_grad = lax.optimization_barrier((sent, live_grad))
    passed = lax.ppermute(sent, "section", [(0, 1)])
    last_grad = to_images(live_grad)
    tokens = jnp.where(section == 0, first_tokens, passed)
    result, kept = forward(tokens, w)

    sent, _, _ = backward(last_grad.astype(f32), kept, w)
    passed = lax.ppermute(sent, "section", [(1, 0)])
    grad_out = jnp.where(section == 1, last_grad, passed).astype(f32)
    grad_inputs, sums, outer_parts = backward(grad_out, kept, w, last=True)
    result, grad_inputs = lax.optimization_barrier((result, grad_inputs))
    block_out, in_grad = from_images([result, grad_inputs], images)

    def natural(pair):
        return jnp.concatenate(ordered(core, *pair))

    v_sum = lambda a: a.reshape(groups, 2, PAIR)[:, 1].reshape(half)
    fc1_bias_sum = jnp.stack(
        ordered(
            core, *(jnp.swapaxes(s.reshape(2, shards, part), 0, 1) for s in sums["fc1_bias"])
        ),
        axis=1,
    ).reshape(width, hidden // own)
    vector_grads = jnp.concatenate(
        [
            jnp.stack(
                [
                    *sums["gain"],
                    *sums["shift"],
                    natural(sums["q"]),
                    natural([v_sum(g) for g in sums["kv"]]),
                    *sums["out_bias"],
                    *sums["scale"],
                ],
                axis=1,
            ),
            fc1_bias_sum,
        ],
        axis=1,
    )
    step = 256
    vector_grads = jnp.pad(vector_grads, ((0, 0), (0, step - count))).astype(bf16)

    rows = [
        lax.psum_scatter(g, RING_Z, scatter_dimension=0, tiled=True) for g in outer_parts["fc"]
    ]
    fc_grad = lax.psum_scatter(
        jnp.concatenate(rows, axis=1), RING_Y, scatter_dimension=0, tiled=True
    )
    a1, dq = outer_parts["q"]
    dkv = outer_parts["kv"][1]
    o, e1 = outer_parts["proj"]
    make = lambda i, **more: outer(
        [((a1, 0), dq[i], width), ((o, 0), e1[i], width), ((a1, 0), dkv[i], width)], step, **more
    )
    ab = make(0, add=swap(make(1), "core"), tail=vector_grads)
    ab = ring_sum(ab.reshape(4, 4, own, 2 * width + step), RING_Y, 1)
    ab_grad = ring_sum(ab, RING_Z, 0, direct=True)

    parts = [ab_grad, fc_grad]
    parts = [(a.astype(f32) + swap(a, "xhi").astype(f32)).astype(bf16) for a in parts]
    others = [swap(a, "core") for a in parts]
    vec_grad = sum(p[0][:, 2 * width : 2 * width + count].astype(f32) for p in (parts, others)).T
    ab_pair, fc_pair = (
        ordered(core, a.astype(f32), b.astype(f32)) for a, b in zip(parts, others)
    )
    q_grad = jnp.concatenate([p[:, :half] for p in ab_pair], axis=1)
    proj_out = jnp.concatenate([p[:, half:width] for p in ab_pair], axis=1)
    kv_grads = [p[:, width : 2 * width].reshape(own, groups, 2, PAIR) for p in ab_pair]
    k_grad, v_grad = (
        jnp.concatenate([p[:, :, i].reshape(own, half) for p in kv_grads], axis=1)
        for i in range(2)
    )
    qkv_out = jnp.concatenate([q_grad, k_grad, v_grad], axis=1)
    fc1_out = jnp.stack(
        [jnp.swapaxes(p[:, :wide].reshape(own, 2, shards, part), 1, 2) for p in fc_pair], axis=2
    ).reshape(own, 2 * wide)
    fc2_out = jnp.concatenate(
        [p[:, wide + i * width : wide + (i + 1) * width] for p in fc_pair for i in range(2)], axis=0
    )
    return (
        block_out[None],
        in_grad[None],
        vec_grad[0:2][None],
        vec_grad[2:4][None],
        qkv_out[None],
        vec_grad[4:6][None],
        proj_out[None],
        fc1_out[None],
        vec_grad[10:].T.reshape(1, hidden),
        fc2_out[None],
        vec_grad[6:8][None],
        vec_grad[8:10][None],
    )


def solution(mesh):
    sections, fsdp, rep = mesh.devices.shape
    inner = Mesh(
        mesh.devices.reshape(sections, fsdp // 4, 2, 2, rep // 2, 2),
        ("section",) + FSDP + REP,
    )
    weight = P("section", FSDP, None)
    vector = P("section", None, FSDP)
    tokens = P(REP, FSDP, None)
    both = P("section", REP, FSDP, None)
    return jax.shard_map(
        per_device,
        mesh=inner,
        in_specs=(
            tokens,
            tokens,
            P(REP, None),
            vector,
            vector,
            weight,
            vector,
            weight,
            weight,
            P("section", FSDP),
            weight,
            vector,
            vector,
        ),
        out_specs=(
            both,
            both,
            vector,
            vector,
            weight,
            vector,
            weight,
            weight,
            P("section", FSDP),
            weight,
            vector,
            vector,
        ),
        check_vma=False,
    )
```

```python
import jax
import jax.numpy as jnp
from jax import lax
from jax.experimental import pallas as pl
from jax.experimental.pallas import tpu as pltpu
from jax.sharding import Mesh, PartitionSpec as P

HEAD_DIM = 64
IMG_MB = 2
PAIR = 2 * HEAD_DIM
EPSILON = 1e-06

FSDP = ("z", "yh", "yl")
REP = ("xhi", "core")
bf16 = jnp.bfloat16
f32 = jnp.float32


def dot(a, b, dims):
    return lax.dot_general(a, b, (dims, ((), ())), preferred_element_type=f32)


def mm(a, b):
    return dot(a, b, ((1,), (0,)))


def mm_t(a, b):
    return dot(a, b, ((1,), (1,)))


def t_mm(a, b):
    return dot(a, b, ((0,), (0,)))


def swap(value, axis):
    return lax.ppermute(value, axis, [(0, 1), (1, 0)])


def attend_kernel(q_ref, own_ref, mate_ref, near_ref, far_ref, out_ref, log_ref):
    rows = q_ref.shape[0]
    both = [r[...] for r in (own_ref, mate_ref, near_ref, far_ref)]
    keys = jnp.concatenate([b[:, :PAIR] for b in both], axis=0)
    values = jnp.concatenate([b[:, PAIR:] for b in both], axis=0)
    queries = q_ref[...] * jnp.asarray(HEAD_DIM**-0.5, bf16)
    lane = lax.broadcasted_iota(jnp.int32, (rows, PAIR), 1)
    outs = []
    for head in range(2):
        mine = (lane >= head * HEAD_DIM) & (lane < (head + 1) * HEAD_DIM)
        picked = jnp.where(mine, queries, jnp.zeros_like(queries))
        scores = mm_t(keys, picked)
        top = jnp.max(scores, axis=0, keepdims=True)
        raised = jnp.exp(scores - top)
        total = jnp.sum(raised, axis=0, keepdims=True)
        out = t_mm(values, raised.astype(bf16))
        outs.append(out * (1.0 / total))
        log_ref[0, head : head + 1, :] = top + jnp.log(total)
    row = lax.broadcasted_iota(jnp.int32, (PAIR, rows), 0)
    joined = jnp.where(row < HEAD_DIM, outs[0], outs[1])
    out_ref[...] = joined.T.astype(bf16)


def attend_back_kernel(
    q_ref, own_ref, mate_ref, near_ref, far_ref, grad_ref, log_ref, dq_ref, *dkv_refs
):
    rows = q_ref.shape[0]
    both = [r[...] for r in (own_ref, mate_ref, near_ref, far_ref)]
    keys = jnp.concatenate([b[:, :PAIR] for b in both], axis=0)
    values = jnp.concatenate([b[:, PAIR:] for b in both], axis=0)
    queries = q_ref[...] * jnp.asarray(HEAD_DIM**-0.5, bf16)
    grads = grad_ref[...]
    lane = lax.broadcasted_iota(jnp.int32, (rows, PAIR), 1)
    dqs, dk, dv = [], None, None
    for head in range(2):
        mine = (lane >= head * HEAD_DIM) & (lane < (head + 1) * HEAD_DIM)
        picked = jnp.where(mine, queries, jnp.zeros_like(queries))
        grad = jnp.where(mine, grads, jnp.zeros_like(grads))
        scores = mm_t(keys, picked)
        weighting = jnp.exp(scores - log_ref[0, head : head + 1, :])
        grad_weighting = mm_t(values, grad)
        row_term = jnp.sum(grad_weighting * weighting, axis=0, keepdims=True)
        grad_scores = (weighting * (grad_weighting - row_term)).astype(bf16)
        dqs.append(t_mm(keys, grad_scores))
        k_part = mm(grad_scores, picked)
        v_part = mm(weighting.astype(bf16), grad)
        dk = k_part if dk is None else dk + k_part
        dv = v_part if dv is None else dv + v_part
    row = lax.broadcasted_iota(jnp.int32, (PAIR, rows), 0)
    joined = jnp.where(row < HEAD_DIM, dqs[0], dqs[1]) * (HEAD_DIM**-0.5)
    dq_ref[...] = joined.T.astype(bf16)
    for i, ref in enumerate(dkv_refs):
        ref[:, :PAIR] = dk[i * rows : (i + 1) * rows].astype(bf16)
        ref[:, PAIR:] = dv[i * rows : (i + 1) * rows].astype(bf16)


def pair_specs(rows, pairs):
    half = pairs // 2
    q_spec = pl.BlockSpec((rows, PAIR), lambda i: (0, i))
    kv_spec = pl.BlockSpec((rows, 2 * PAIR), lambda i: (0, i))
    kv_swapped = pl.BlockSpec((rows, 2 * PAIR), lambda i: (0, (i + half) % pairs))
    log_spec = pl.BlockSpec((1, 2, rows), lambda i: (i, 0, 0))
    return q_spec, [kv_spec, kv_swapped, kv_spec, kv_swapped], log_spec


def attend_cost(queries, blocks, products):
    rows, width = queries.shape
    scores = rows * rows * len(blocks) * width // HEAD_DIM
    return pl.CostEstimate(
        flops=products * scores * 2 * 256,
        bytes_accessed=2 * 2 * len(blocks) * rows * width * 2,
        transcendentals=scores,
    )


def attend(queries, blocks):
    rows, width = queries.shape
    pairs = width // PAIR
    q_spec, kv_specs, log_spec = pair_specs(rows, pairs)
    return pl.pallas_call(
        attend_kernel,
        grid=(pairs,),
        in_specs=[q_spec] + kv_specs,
        out_specs=[q_spec, log_spec],
        out_shape=[
            jax.ShapeDtypeStruct((rows, width), bf16),
            jax.ShapeDtypeStruct((pairs, 2, rows), f32),
        ],
        compiler_params=pltpu.CompilerParams(vmem_limit_bytes=40 * 2**20),
        cost_estimate=attend_cost(queries, blocks, 2),
        name="attend",
    )(queries, *blocks)


def attend_back(queries, blocks, grad, log_total):
    rows, width = queries.shape
    pairs = width // PAIR
    q_spec, kv_specs, log_spec = pair_specs(rows, pairs)
    return pl.pallas_call(
        attend_back_kernel,
        grid=(pairs,),
        in_specs=[q_spec] + kv_specs + [q_spec, log_spec],
        out_specs=[q_spec] + kv_specs,
        out_shape=[jax.ShapeDtypeStruct((rows, width), bf16)]
        + [jax.ShapeDtypeStruct((rows, 2 * width), bf16)] * 4,
        compiler_params=pltpu.CompilerParams(vmem_limit_bytes=40 * 2**20),
        cost_estimate=attend_cost(queries, blocks, 5),
        name="attend_back",
    )(queries, *blocks, grad, log_total)


def outer(segments, step, add=None, tail=None):
    rows = segments[0][1].shape[0]
    width = segments[0][2]
    counts = [right.shape[1] // step for _, right, _ in segments]
    starts = [sum(counts[:k]) for k in range(len(counts))]
    total = sum(counts)
    grid = total + (tail is not None)
    n = len(segments)

    def kernel(*refs):
        out_ref = refs[-1]
        i = pl.program_id(0)
        for k in range(n):

            @pl.when((i >= starts[k]) & (i < starts[k] + counts[k]))
            def _(k=k):
                value = t_mm(refs[2 * k][...], refs[2 * k + 1][...])
                if add is not None:
                    value = value + refs[2 * n][...].astype(f32)
                out_ref[...] = value.astype(bf16)

        if tail is not None:

            @pl.when(i == total)
            def _():
                out_ref[...] = refs[2 * n + (add is not None)][...]

    in_specs, operands = [], []
    for (left, right, _), start, count in zip(segments, starts, counts):
        array, which = left
        in_specs.append(pl.BlockSpec((rows, width), lambda i, w=which: (0, w)))
        in_specs.append(
            pl.BlockSpec((rows, step), lambda i, s=start, c=count: (0, jnp.clip(i - s, 0, c - 1)))
        )
        operands += [array, right]
    if add is not None:
        in_specs.append(pl.BlockSpec((width, step), lambda i: (0, jnp.minimum(i, total - 1))))
        operands.append(add)
    if tail is not None:
        in_specs.append(pl.BlockSpec((width, step), lambda i: (0, 0)))
        operands.append(tail)
    return pl.pallas_call(
        kernel,
        grid=(grid,),
        in_specs=in_specs,
        out_specs=pl.BlockSpec((width, step), lambda i: (0, i)),
        out_shape=jax.ShapeDtypeStruct((width, grid * step), bf16),
        compiler_params=pltpu.CompilerParams(vmem_limit_bytes=40 * 2**20),
        cost_estimate=pl.CostEstimate(
            flops=2 * rows * width * total * step,
            bytes_accessed=2 * width * grid * step * (1 if add is None else 2),
            transcendentals=0,
        ),
        name="outer",
    )(*operands)


def fc1_part(normed, grad_before, add=None):
    return outer([((normed, 0), grad_before, normed.shape[1])], 512, add=add)


def fc2_part(activated, grad_branch, add=None):
    width = grad_branch.shape[1]
    count = activated.shape[1] // width
    return outer([((activated, i), grad_branch, width) for i in range(count)], 512, add=add)


def join(kernel, core, inputs, shapes):
    vmem = pl.BlockSpec(memory_space=pltpu.VMEM)
    return pl.pallas_call(
        kernel,
        in_specs=[pl.BlockSpec(memory_space=pltpu.SMEM)] + [vmem] * len(inputs),
        out_specs=[vmem] * len(shapes),
        out_shape=[jax.ShapeDtypeStruct(shape, f32) for shape in shapes],
        compiler_params=pltpu.CompilerParams(vmem_limit_bytes=24 * 2**20),
        cost_estimate=pl.CostEstimate(
            flops=0, bytes_accessed=6 * sum(a.size for a in inputs), transcendentals=0
        ),
        name="join",
    )(core.reshape(1), *inputs)


def join_qkv(core, mine, other, width):
    rows, half = mine.shape[0], width // 2

    def kernel(core_ref, mine_ref, other_ref, qkv_ref, proj_ref):
        for ref, place in ((mine_ref, core_ref[0]), (other_ref, 1 - core_ref[0])):
            at = place * half
            columns = lambda start, size: pl.ds(pl.multiple_of(at + start, PAIR), size)
            qkv_ref[:, columns(0, half)] = ref[:, :half].astype(f32)
            proj_ref[:, columns(0, half)] = ref[:, half:width].astype(f32)
            for g in range(half // PAIR):
                k = width + 2 * g * PAIR
                for i in range(2):
                    qkv_ref[:, columns((i + 1) * width + g * PAIR, PAIR)] = ref[
                        :, k + i * PAIR : k + (i + 1) * PAIR
                    ].astype(f32)

    return join(kernel, core, [mine, other], [(rows, 3 * width), (rows, width)])


def join_fc(core, mine, other, width, shards):
    rows = mine.shape[0]
    wide = mine.shape[1] - 2 * width
    part = wide // (2 * shards)
    pair = 2 * part

    def kernel(core_ref, mine_ref, other_ref, fc1_ref, fc2_ref):
        for ref, place in ((mine_ref, core_ref[0]), (other_ref, 1 - core_ref[0])):
            for f in range(shards):
                at = pl.multiple_of(2 * pair * f + place * pair, pair)
                value = [
                    ref[:, i * shards * part + f * part : i * shards * part + (f + 1) * part]
                    for i in range(2)
                ]
                fc1_ref[:, pl.ds(at, pair)] = jnp.concatenate(value, axis=1).astype(f32)
            for i in range(2):
                at = pl.multiple_of(place * 2 * rows + i * rows, rows)
                fc2_ref[pl.ds(at, rows)] = ref[
                    :, wide + i * width : wide + (i + 1) * width
                ].astype(f32)

    return join(kernel, core, [mine, other], [(rows, 2 * wide), (4 * rows, width)])


FLIP = [(0, 0), (1, 2), (2, 1), (3, 3)]


def to_images(tokens):
    count, rows, width = tokens.shape
    mixed = lax.all_to_all(tokens, "z", split_axis=0, concat_axis=0, tiled=True)
    return mixed.reshape(count * rows, width)


def flip(tokens):
    return lax.ppermute(tokens, ("yh", "core"), FLIP)


def from_images(arrays, count):
    rows, width = arrays[0].shape
    mixed = [flip(a) for a in arrays]
    mixed = jnp.stack([m.reshape(count, rows // count, width) for m in mixed], axis=1)
    mixed = lax.all_to_all(mixed, "z", split_axis=0, concat_axis=0, tiled=True)
    return [mixed[:, i] for i in range(len(arrays))]


RING_Z, RING_Y = "z", ("yh", "yl")
AHEAD = [(i, (i + 1) % 4) for i in range(4)]
BACK = [(i, (i - 1) % 4) for i in range(4)]


ACROSS = [(i, (i + 2) % 4) for i in range(4)]


def ring_place(value, axis, out_shapes, views, direct=False):
    half = value.shape[0] // 2
    ahead = lax.ppermute(value, axis, AHEAD)
    back = lax.ppermute(value, axis, BACK)
    pieces = [(value, 0, 0), (ahead, 3, 0), (back, 1, 0)]
    if direct:
        pieces.append((lax.ppermute(value, axis, ACROSS), 2, 0))
    else:
        pieces.append((lax.ppermute(ahead[:half], axis, AHEAD), 2, 0))
        pieces.append((lax.ppermute(back[half:], axis, BACK), 2, half))
    n_outs = len(out_shapes)

    def kernel(index_ref, *refs):
        sources, outs = refs[: len(pieces)], refs[len(pieces) :]
        for source, (_, step, start) in zip(sources, pieces):
            place = lax.rem(index_ref[0] + step, 4)
            views(outs, source, place, start)

    vmem = pl.BlockSpec(memory_space=pltpu.VMEM)
    return pl.pallas_call(
        kernel,
        in_specs=[pl.BlockSpec(memory_space=pltpu.SMEM)] + [vmem] * len(pieces),
        out_specs=[vmem] * n_outs,
        out_shape=[jax.ShapeDtypeStruct(shape, value.dtype) for shape in out_shapes],
        compiler_params=pltpu.CompilerParams(vmem_limit_bytes=24 * 2**20),
        cost_estimate=pl.CostEstimate(
            flops=0, bytes_accessed=16 * value.size, transcendentals=0
        ),
        name="ring_place",
    )(lax.axis_index(axis).reshape(1), *(p[0] for p in pieces))


def in_order(outs, piece, place, start):
    outs[0][place, pl.ds(start, piece.shape[0])] = piece[...]


def ring_sum(blocks, axis, dim, direct=False):
    index = lax.axis_index(axis)
    block = lambda k: lax.dynamic_index_in_dim(blocks, (index + k) % 4, dim, keepdims=False)
    add = lambda *parts: sum(p.astype(f32) for p in parts).astype(bf16)
    if direct:
        ways = [(1, AHEAD), (3, BACK), (2, ACROSS)]
        return add(block(0), *(lax.ppermute(block(k), axis, way) for k, way in ways))
    far, after, before = block(2), block(1), block(3)
    half = far.shape[0] // 2
    low = lax.ppermute(far[:half], axis, AHEAD)
    high = lax.ppermute(far[half:], axis, BACK)
    after = jnp.concatenate([add(after[:half], low), after[half:]])
    before = jnp.concatenate([before[:half], add(before[half:], high)])
    after = lax.ppermute(after, axis, AHEAD)
    before = lax.ppermute(before, axis, BACK)
    return add(block(0), after, before)


def group_parts(own, mate, near, far):
    mate, far = swap(mate, "core"), swap(far, "core")
    sent = (near.astype(f32) + far.astype(f32)).astype(bf16)
    return own.astype(f32) + mate.astype(f32), sent


def normal_part(values):
    mean = jnp.mean(values, axis=-1, keepdims=True)
    centred = values - mean
    factor = lax.rsqrt(jnp.mean(centred * centred, axis=-1, keepdims=True) + EPSILON)
    return centred * factor, factor


def norm_back(grad, normal, factor, gain):
    e = grad * gain
    inner = jnp.mean(e * normal, axis=-1, keepdims=True)
    return factor * (e - jnp.mean(e, axis=-1, keepdims=True) - normal * inner)


def flip_halves(core, value):
    half = value.shape[-1] // 2
    turned = jnp.concatenate([value[..., half:], value[..., :half]], axis=-1)
    return jnp.where(core == 0, value, turned)


CHUNKS = 2


def chunked(halves):
    size = halves[0].shape[1] // CHUNKS
    cut = lambda h, i: h[:, i * size : (i + 1) * size]
    return [jnp.concatenate([cut(h, i) for h in halves], axis=1) for i in range(CHUNKS)]


def unchunked(chunks):
    size = chunks[0].shape[1] // 2
    return [
        jnp.concatenate([c[:, i * size : (i + 1) * size] for c in chunks], axis=1)
        for i in range(2)
    ]


def forward(tokens, w, late=None):
    inputs = tokens.astype(f32)
    normed_one = (normal_part(inputs)[0] * w["gain"][0] + w["shift"][0]).astype(bf16)
    project = lambda name: [
        (mm(normed_one, part) + bias).astype(bf16) for part, bias in zip(w[name], w[name + "_bias"])
    ]
    key_value = chunked(project("kv"))
    queries = chunked(project("q"))
    mate, near = swap(key_value[0], "core"), swap(key_value[0], "yl")
    blocks, results = [], []
    for i, own in enumerate(key_value):
        blocks.append((own, mate, near, swap(near, "core")))
        if i + 1 < CHUNKS:
            following, near = lax.optimization_barrier((key_value[i + 1], near))
            mate, near = swap(following, "core"), swap(following, "yl")
            result = attend(queries[i], blocks[i])
            result, near = lax.optimization_barrier((result, near))
        else:
            if late is not None:
                (own, near), gathered = lax.optimization_barrier(((own, near), late[0]))
                w.update(late[1](gathered))
                blocks[i] = (own, mate, near, blocks[i][3])
            result = attend(queries[i], blocks[i])
        results.append(result)
    attended, log_total = zip(*results)
    attended = jnp.concatenate(unchunked(attended), axis=1)
    attended = flip_halves(w["core"], attended)
    branch = flip_halves(w["core"], jnp.concatenate([mm(attended, p) for p in w["proj"]], axis=1))
    branch = branch + w["out_bias"][0]
    middle = inputs + w["scale"][0] * branch
    normed_two = (normal_part(middle)[0] * w["gain"][1] + w["shift"][1]).astype(bf16)
    activated, slope, branch_two = [], [], w["out_bias"][1]
    for up, bias, down in zip(w["fc1"], w["fc1_bias"], w["fc2"]):
        before = mm(normed_two, up) + bias
        phi = 0.5 * (1.0 + lax.erf(before * (0.5**0.5)))
        density = jnp.exp(-0.5 * before * before) * 0.3989422804014327
        active = (before * phi).astype(bf16)
        activated.append(active)
        slope.append((phi + before * density).astype(bf16))
        for i, part in enumerate(down):
            rows = part.shape[0]
            branch_two = branch_two + mm(active[:, i * rows : (i + 1) * rows], part)
    result = (middle + w["scale"][1] * branch_two).astype(bf16)
    kept = dict(
        inputs=inputs,
        normed_one=normed_one,
        queries=queries,
        blocks=blocks,
        attended=attended,
        log_total=log_total,
        branch=branch,
        middle=middle,
        normed_two=normed_two,
        activated=activated,
        slope=slope,
        branch_two=branch_two,
    )
    return result, kept


def backward(grad_out, kept, w, last=False):
    grad_branch_two = (w["scale"][1] * grad_out).astype(bf16)
    grad_before = []
    grad_normed_two = 0.0
    if last:
        fc2_sent = swap(fc2_part(kept["activated"][1], grad_branch_two), "core")
    for up, down, slope in zip(w["fc1"], w["fc2"], kept["slope"]):
        part = jnp.concatenate([mm_t(grad_branch_two, d) for d in down], axis=1)
        part = (part * slope.astype(f32)).astype(bf16)
        grad_before.append(part)
        grad_normed_two = grad_normed_two + mm_t(part, up)
    if last:
        fc2 = fc2_part(kept["activated"][0], grad_branch_two, fc2_sent)
        fc2, grad_normed_two = lax.optimization_barrier((fc2, grad_normed_two))
        fc2 = lax.psum_scatter(fc2, RING_Z, scatter_dimension=0, tiled=True)
    normal_two, factor_two = normal_part(kept["middle"])
    grad_middle = grad_out + norm_back(grad_normed_two, normal_two, factor_two, w["gain"][1])
    grad_branch = (w["scale"][0] * grad_middle).astype(bf16)
    width = grad_branch.shape[1]
    half = width // 2
    grad_halves = flip_halves(w["core"], grad_branch)
    grad_halves = [grad_halves[:, :half], grad_halves[:, half:]]
    grad_attended = sum(mm_t(g, p) for g, p in zip(grad_halves, w["proj"])).astype(bf16)
    grad_attended = flip_halves(w["core"], grad_attended)
    fc_grad = None
    if last:
        fc1_sent = fc1_part(kept["normed_two"], grad_before[1])
        fc1_sent, grad_attended = lax.optimization_barrier((fc1_sent, grad_attended))
        fc1_sent = swap(fc1_sent, "core")
    grad_chunks = chunked([grad_attended[:, :half], grad_attended[:, half:]])
    q_chunks, kv_chunks = [], []
    ready = None
    for i in range(CHUNKS):
        g = grad_chunks[i]
        if ready is not None:
            own, sent = ready
            if last and fc_grad is None:
                fc1 = fc1_part(kept["normed_two"], grad_before[0], fc1_sent)
                sent, g, fc1 = lax.optimization_barrier((sent, g, fc1))
                fc1 = lax.psum_scatter(fc1, RING_Z, scatter_dimension=0, tiled=True)
                fc_grad = [fc1, fc2]
            else:
                sent, g = lax.optimization_barrier((sent, g))
            came = swap(sent, "yl")
        parts = attend_back(kept["queries"][i], kept["blocks"][i], g, kept["log_total"][i])
        if ready is not None:
            parts, came = lax.optimization_barrier((parts, came))
            kv_chunks.append((own + came.astype(f32)).astype(bf16))
        q_chunks.append(parts[0])
        ready = group_parts(*parts[1:])
    kv_chunks.append((ready[0] + swap(ready[1], "yl").astype(f32)).astype(bf16))
    grad_q, grad_kv = unchunked(q_chunks), unchunked(kv_chunks)
    grad_normed_one = sum(
        mm_t(g, part) for g, part in zip(grad_q + grad_kv, w["q"] + w["kv"])
    )
    normal_one, factor_one = normal_part(kept["inputs"])
    grad_inputs = grad_middle + norm_back(grad_normed_one, normal_one, factor_one, w["gain"][0])
    total = lambda a: jnp.sum(a.astype(f32), axis=0)
    vectors = dict(
        gain=(total(grad_normed_one * normal_one), total(grad_normed_two * normal_two)),
        shift=(total(grad_normed_one), total(grad_normed_two)),
        out_bias=(total(grad_branch), total(grad_branch_two)),
        scale=(total(grad_middle * kept["branch"]), total(grad_out * kept["branch_two"])),
        q=[total(g) for g in grad_q],
        kv=[total(g) for g in grad_kv],
        fc1_bias=[total(g) for g in grad_before],
    )
    products = dict(
        q=(kept["normed_one"], grad_q),
        kv=(kept["normed_one"], grad_kv),
        proj=(kept["attended"], grad_halves),
        fc=fc_grad,
    )
    return grad_inputs.astype(bf16), vectors, products


def ordered(core, mine, other):
    return jnp.where(core == 0, mine, other), jnp.where(core == 0, other, mine)


def per_device(
    patch_tokens,
    out_grad,
    batch_counts,
    norm_gain,
    norm_bias,
    qkv_weight,
    qv_bias,
    proj_weight,
    fc1_weight,
    fc1_bias,
    fc2_weight,
    out_bias,
    layer_scale,
):
    section = lax.axis_index("section")
    core = lax.axis_index("core")
    shards = lax.axis_size(FSDP)
    images, rows, width = patch_tokens.shape
    half = width // 2
    own = width // shards
    hidden = fc2_weight.shape[1]
    mid = hidden // 2
    groups = half // PAIR
    pick = lambda a, i, axis: lax.dynamic_index_in_dim(a, i, axis, keepdims=False)

    part = mid // 2
    q, k, v = (qkv_weight[0][:, i * width : (i + 1) * width] for i in range(3))
    q_mine = pick(q.reshape(own, 2, half), core, 1)
    kv = jnp.stack([k.reshape(own, 2, groups, PAIR), v.reshape(own, 2, groups, PAIR)], axis=3)
    kv_mine = pick(kv, core, 1).reshape(own, width)
    proj_mine = pick(proj_weight[0].reshape(own, 2, half), core, 1)
    vectors = jnp.concatenate(
        [a[0] for a in (norm_gain, norm_bias, qv_bias, out_bias, layer_scale)]
        + [fc1_bias[0].reshape(own, hidden // own).T],
        axis=0,
    ).T
    count = vectors.shape[1]
    vectors = jnp.pad(vectors, ((0, 0), (0, 128 - count)))
    fc1_mine = pick(fc1_weight[0].reshape(own, shards, 2, 2, part), core, 2)
    fc1_mine = jnp.swapaxes(fc1_mine, 1, 2).reshape(own, shards * mid)
    fc2_mine = pick(fc2_weight[0].reshape(2, 2, part, width), core, 0)
    fc_mine = jnp.concatenate([fc1_mine, fc2_mine[0], fc2_mine[1]], axis=1)

    a_mine = jnp.concatenate([q_mine, proj_mine, vectors], axis=1)
    first_tokens = to_images(patch_tokens)
    a_row = ring_place(a_mine, RING_Y, [(4, own, a_mine.shape[1])], in_order, direct=True)[0]
    b_row = ring_place(kv_mine, RING_Z, [(4, own, width)], in_order, direct=True)[0]
    a_row, b_row, fc_mine, first_tokens = lax.optimization_barrier(
        (a_row, b_row, fc_mine, first_tokens)
    )
    first_tokens = flip(first_tokens)
    fc_half = lax.all_gather(fc_mine, FSDP, axis=0, tiled=True)
    a_row = a_row.reshape(4 * own, a_mine.shape[1])

    def a_views(outs, piece, place, start):
        at = 0
        for out in outs:
            size = out.shape[-1]
            out[place, pl.ds(start, piece.shape[0])] = piece[:, pl.ds(at, size)]
            at += size

    def b_views(outs, piece, place, start):
        for i in range(piece.shape[0]):
            outs[0][start + i, place] = piece[i]

    q_half, proj_half, vectors = (
        o.reshape(width, -1)
        for o in ring_place(
            a_row, RING_Z, [(4, 4 * own, half), (4, 4 * own, half), (4, 4 * own, 128)], a_views
        )
    )
    kv_half = ring_place(b_row, RING_Y, [(4, 4, own, width)], b_views)[0].reshape(width, width)
    vectors = vectors[:, :count].T.astype(f32)
    fc1_b = vectors[10:].T.reshape(shards, 2, 2, part)

    def halves(vector):
        pair = vector.reshape(2, half)
        return pick(pair, core, 0), pick(pair, 1 - core, 0)

    def kv_bias(v_half):
        v_part = v_half.reshape(groups, 1, PAIR)
        return jnp.concatenate([jnp.zeros_like(v_part), v_part], axis=1).reshape(width)

    wide = shards * mid
    w = dict(
        core=core,
        gain=vectors[0:2],
        shift=vectors[2:4],
        out_bias=vectors[6:8],
        scale=vectors[8:10],
        q=[q_half, swap(q_half, "core")],
        q_bias=halves(vectors[4]),
        kv=[kv_half, swap(kv_half, "core")],
        kv_bias=[kv_bias(b) for b in halves(vectors[5])],
        proj=(proj_half, swap(proj_half, "core")),
        fc1_bias=[
            jnp.swapaxes(pick(fc1_b, c, 1), 0, 1).reshape(-1) for c in (core, 1 - core)
        ],
    )

    def fc_weights(gathered):
        pair = (gathered, swap(gathered, "core"))
        return dict(
            fc1=[f[:, :wide] for f in pair],
            fc2=[(f[:, wide : wide + width], f[:, wide + width :]) for f in pair],
        )


    live = (
        jnp.arange(images) % IMG_MB < jnp.repeat(batch_counts[0], IMG_MB)
    ).astype(bf16)

    sent, _ = forward(first_tokens, w, late=(fc_half, fc_weights))
    live_grad = out_grad * live[:, None, None]
    sent, live_grad = lax.optimization_barrier((sent, live_grad))
    passed = lax.ppermute(sent, "section", [(0, 1)])
    last_grad = flip(to_images(live_grad))
    tokens = jnp.where(section == 0, first_tokens, passed)
    result, kept = forward(tokens, w)

    sent, _, _ = backward(last_grad.astype(f32), kept, w)
    passed = lax.ppermute(sent, "section", [(1, 0)])
    grad_out = jnp.where(section == 1, last_grad, passed).astype(f32)
    grad_inputs, sums, products = backward(grad_out, kept, w, last=True)
    result, grad_inputs = lax.optimization_barrier((result, grad_inputs))
    block_out, in_grad = from_images([result, grad_inputs], images)

    def natural(pair):
        return jnp.concatenate(ordered(core, *pair))

    v_sum = lambda a: a.reshape(groups, 2, PAIR)[:, 1].reshape(half)
    fc1_bias_sum = jnp.stack(
        ordered(
            core, *(jnp.swapaxes(s.reshape(2, shards, part), 0, 1) for s in sums["fc1_bias"])
        ),
        axis=1,
    ).reshape(width, hidden // own)
    vector_grads = jnp.stack(
        [
            *sums["gain"],
            *sums["shift"],
            natural(sums["q"]),
            natural([v_sum(g) for g in sums["kv"]]),
            *sums["out_bias"],
            *sums["scale"],
            *fc1_bias_sum.T,
        ]
    )
    vector_grads = jnp.pad(vector_grads, ((0, PAIR - count), (0, 0))).astype(bf16).T

    a1, dq = products["q"]
    dkv = products["kv"][1]
    o, e1 = products["proj"]
    make = lambda i, add=None: outer(
        [((a1, 0), dq[i], width), ((o, 0), e1[i], width), ((a1, 0), dkv[i], width)], 256, add=add
    )
    ab = make(0, swap(make(1), "core")).reshape(4, 4, own, 2 * width)
    ab = ring_sum(ab, RING_Y, 1)
    vector_grads = ring_sum(vector_grads.reshape(4, 4, own, PAIR), RING_Y, 1, direct=True)
    ab, vector_grads, rows = lax.optimization_barrier((ab, vector_grads, products["fc"]))
    fc_grad = lax.psum_scatter(
        jnp.concatenate(rows, axis=1), RING_Y, scatter_dimension=0, tiled=True
    )
    ab = ring_sum(jnp.concatenate([ab, vector_grads], axis=2), RING_Z, 0, direct=True)

    def chips_sum(a):
        return (a.astype(f32) + swap(a, "xhi").astype(f32)).astype(bf16)

    ab = chips_sum(ab)
    ab_other = swap(ab, "core")
    qkv_out, proj_out = join_qkv(core, ab, ab_other, width)
    vec_grad = sum(p[:, 2 * width : 2 * width + count].astype(f32) for p in (ab, ab_other)).T
    fc_grad = chips_sum(fc_grad)
    fc1_out, fc2_out = join_fc(core, fc_grad, swap(fc_grad, "core"), width, shards)
    return (
        block_out[None],
        in_grad[None],
        vec_grad[0:2][None],
        vec_grad[2:4][None],
        qkv_out[None],
        vec_grad[4:6][None],
        proj_out[None],
        fc1_out[None],
        vec_grad[10:].T.reshape(1, hidden),
        fc2_out[None],
        vec_grad[6:8][None],
        vec_grad[8:10][None],
    )


def solution(mesh):
    sections, fsdp, rep = mesh.devices.shape
    inner = Mesh(
        mesh.devices.reshape(sections, fsdp // 4, 2, 2, rep // 2, 2),
        ("section",) + FSDP + REP,
    )
    weight = P("section", FSDP, None)
    vector = P("section", None, FSDP)
    tokens = P(REP, FSDP, None)
    both = P("section", REP, FSDP, None)
    return jax.shard_map(
        per_device,
        mesh=inner,
        in_specs=(
            tokens,
            tokens,
            P(REP, None),
            vector,
            vector,
            weight,
            vector,
            weight,
            weight,
            P("section", FSDP),
            weight,
            vector,
            vector,
        ),
        out_specs=(
            both,
            both,
            vector,
            vector,
            weight,
            vector,
            weight,
            weight,
            P("section", FSDP),
            weight,
            vector,
            vector,
        ),
        check_vma=False,
    )
```

```python
import jax
import jax.numpy as jnp
from jax import lax
from jax.experimental import pallas as pl
from jax.experimental.pallas import tpu as pltpu
from jax.sharding import Mesh, PartitionSpec as P

HEAD_DIM = 64
IMG_MB = 2
PAIR = 2 * HEAD_DIM
EPSILON = 1e-06

FSDP = ("z", "yh", "yl")
REP = ("xhi", "core")
bf16 = jnp.bfloat16
f32 = jnp.float32


def dot(a, b, dims):
    return lax.dot_general(a, b, (dims, ((), ())), preferred_element_type=f32)


def mm(a, b):
    return dot(a, b, ((1,), (0,)))


def mm_t(a, b):
    return dot(a, b, ((1,), (1,)))


def t_mm(a, b):
    return dot(a, b, ((0,), (0,)))


def swap(value, axis):
    return lax.ppermute(value, axis, [(0, 1), (1, 0)])


def attend_kernel(q_ref, own_ref, mate_ref, near_ref, far_ref, out_ref, log_ref):
    rows = q_ref.shape[0]
    both = [r[...] for r in (own_ref, mate_ref, near_ref, far_ref)]
    keys = jnp.concatenate([b[:, :PAIR] for b in both], axis=0)
    values = jnp.concatenate([b[:, PAIR:] for b in both], axis=0)
    queries = q_ref[...] * jnp.asarray(HEAD_DIM**-0.5, bf16)
    lane = lax.broadcasted_iota(jnp.int32, (rows, PAIR), 1)
    outs = []
    for head in range(2):
        mine = (lane >= head * HEAD_DIM) & (lane < (head + 1) * HEAD_DIM)
        picked = jnp.where(mine, queries, jnp.zeros_like(queries))
        scores = mm_t(keys, picked)
        top = jnp.max(scores, axis=0, keepdims=True)
        raised = jnp.exp(scores - top)
        total = jnp.sum(raised, axis=0, keepdims=True)
        out = t_mm(values, raised.astype(bf16))
        outs.append(out * (1.0 / total))
        log_ref[0, head : head + 1, :] = top + jnp.log(total)
    row = lax.broadcasted_iota(jnp.int32, (PAIR, rows), 0)
    joined = jnp.where(row < HEAD_DIM, outs[0], outs[1])
    out_ref[...] = joined.T.astype(bf16)


def attend_back_kernel(
    q_ref, own_ref, mate_ref, near_ref, far_ref, grad_ref, log_ref, dq_ref, *dkv_refs
):
    rows = q_ref.shape[0]
    both = [r[...] for r in (own_ref, mate_ref, near_ref, far_ref)]
    keys = jnp.concatenate([b[:, :PAIR] for b in both], axis=0)
    values = jnp.concatenate([b[:, PAIR:] for b in both], axis=0)
    queries = q_ref[...] * jnp.asarray(HEAD_DIM**-0.5, bf16)
    grads = grad_ref[...]
    lane = lax.broadcasted_iota(jnp.int32, (rows, PAIR), 1)
    dqs, dk, dv = [], None, None
    for head in range(2):
        mine = (lane >= head * HEAD_DIM) & (lane < (head + 1) * HEAD_DIM)
        picked = jnp.where(mine, queries, jnp.zeros_like(queries))
        grad = jnp.where(mine, grads, jnp.zeros_like(grads))
        scores = mm_t(keys, picked)
        weighting = jnp.exp(scores - log_ref[0, head : head + 1, :])
        grad_weighting = mm_t(values, grad)
        row_term = jnp.sum(grad_weighting * weighting, axis=0, keepdims=True)
        grad_scores = (weighting * (grad_weighting - row_term)).astype(bf16)
        dqs.append(t_mm(keys, grad_scores))
        k_part = mm(grad_scores, picked)
        v_part = mm(weighting.astype(bf16), grad)
        dk = k_part if dk is None else dk + k_part
        dv = v_part if dv is None else dv + v_part
    row = lax.broadcasted_iota(jnp.int32, (PAIR, rows), 0)
    joined = jnp.where(row < HEAD_DIM, dqs[0], dqs[1]) * (HEAD_DIM**-0.5)
    dq_ref[...] = joined.T.astype(bf16)
    for i, ref in enumerate(dkv_refs):
        ref[:, :PAIR] = dk[i * rows : (i + 1) * rows].astype(bf16)
        ref[:, PAIR:] = dv[i * rows : (i + 1) * rows].astype(bf16)


def pair_specs(rows, pairs):
    half = pairs // 2
    q_spec = pl.BlockSpec((rows, PAIR), lambda i: (0, i))
    kv_spec = pl.BlockSpec((rows, 2 * PAIR), lambda i: (0, i))
    kv_swapped = pl.BlockSpec((rows, 2 * PAIR), lambda i: (0, (i + half) % pairs))
    log_spec = pl.BlockSpec((1, 2, rows), lambda i: (i, 0, 0))
    return q_spec, [kv_spec, kv_swapped, kv_spec, kv_swapped], log_spec


def attend_cost(queries, blocks, products):
    rows, width = queries.shape
    scores = rows * rows * len(blocks) * width // HEAD_DIM
    return pl.CostEstimate(
        flops=products * scores * 2 * 256,
        bytes_accessed=2 * 2 * len(blocks) * rows * width * 2,
        transcendentals=scores,
    )


def attend(queries, blocks):
    rows, width = queries.shape
    pairs = width // PAIR
    q_spec, kv_specs, log_spec = pair_specs(rows, pairs)
    return pl.pallas_call(
        attend_kernel,
        grid=(pairs,),
        in_specs=[q_spec] + kv_specs,
        out_specs=[q_spec, log_spec],
        out_shape=[
            jax.ShapeDtypeStruct((rows, width), bf16),
            jax.ShapeDtypeStruct((pairs, 2, rows), f32),
        ],
        compiler_params=pltpu.CompilerParams(vmem_limit_bytes=40 * 2**20),
        cost_estimate=attend_cost(queries, blocks, 2),
        name="attend",
    )(queries, *blocks)


def attend_back(queries, blocks, grad, log_total):
    rows, width = queries.shape
    pairs = width // PAIR
    q_spec, kv_specs, log_spec = pair_specs(rows, pairs)
    return pl.pallas_call(
        attend_back_kernel,
        grid=(pairs,),
        in_specs=[q_spec] + kv_specs + [q_spec, log_spec],
        out_specs=[q_spec] + kv_specs,
        out_shape=[jax.ShapeDtypeStruct((rows, width), bf16)]
        + [jax.ShapeDtypeStruct((rows, 2 * width), bf16)] * 4,
        compiler_params=pltpu.CompilerParams(vmem_limit_bytes=40 * 2**20),
        cost_estimate=attend_cost(queries, blocks, 5),
        name="attend_back",
    )(queries, *blocks, grad, log_total)


def outer(segments, step, add=None, tail=None):
    rows = segments[0][1].shape[0]
    width = segments[0][2]
    counts = [right.shape[1] // step for _, right, _ in segments]
    starts = [sum(counts[:k]) for k in range(len(counts))]
    total = sum(counts)
    grid = total + (tail is not None)
    n = len(segments)

    def kernel(*refs):
        out_ref = refs[-1]
        i = pl.program_id(0)
        for k in range(n):

            @pl.when((i >= starts[k]) & (i < starts[k] + counts[k]))
            def _(k=k):
                value = t_mm(refs[2 * k][...], refs[2 * k + 1][...])
                if add is not None:
                    value = value + refs[2 * n][...].astype(f32)
                out_ref[...] = value.astype(bf16)

        if tail is not None:

            @pl.when(i == total)
            def _():
                out_ref[...] = refs[2 * n + (add is not None)][...]

    in_specs, operands = [], []
    for (left, right, _), start, count in zip(segments, starts, counts):
        array, which = left
        in_specs.append(pl.BlockSpec((rows, width), lambda i, w=which: (0, w)))
        in_specs.append(
            pl.BlockSpec((rows, step), lambda i, s=start, c=count: (0, jnp.clip(i - s, 0, c - 1)))
        )
        operands += [array, right]
    if add is not None:
        in_specs.append(pl.BlockSpec((width, step), lambda i: (0, jnp.minimum(i, total - 1))))
        operands.append(add)
    if tail is not None:
        in_specs.append(pl.BlockSpec((width, step), lambda i: (0, 0)))
        operands.append(tail)
    return pl.pallas_call(
        kernel,
        grid=(grid,),
        in_specs=in_specs,
        out_specs=pl.BlockSpec((width, step), lambda i: (0, i)),
        out_shape=jax.ShapeDtypeStruct((width, grid * step), bf16),
        compiler_params=pltpu.CompilerParams(vmem_limit_bytes=40 * 2**20),
        cost_estimate=pl.CostEstimate(
            flops=2 * rows * width * total * step,
            bytes_accessed=2 * width * grid * step * (1 if add is None else 2),
            transcendentals=0,
        ),
        name="outer",
    )(*operands)


def fc1_part(normed, grad_before, add=None):
    return outer([((normed, 0), grad_before, normed.shape[1])], 512, add=add)


def fc2_part(activated, grad_branch, add=None):
    width = grad_branch.shape[1]
    count = activated.shape[1] // width
    return outer([((activated, i), grad_branch, width) for i in range(count)], 512, add=add)


def join(kernel, core, inputs, shapes):
    vmem = pl.BlockSpec(memory_space=pltpu.VMEM)
    return pl.pallas_call(
        kernel,
        in_specs=[pl.BlockSpec(memory_space=pltpu.SMEM)] + [vmem] * len(inputs),
        out_specs=[vmem] * len(shapes),
        out_shape=[jax.ShapeDtypeStruct(shape, f32) for shape in shapes],
        compiler_params=pltpu.CompilerParams(vmem_limit_bytes=24 * 2**20),
        cost_estimate=pl.CostEstimate(
            flops=0, bytes_accessed=6 * sum(a.size for a in inputs), transcendentals=0
        ),
        name="join",
    )(core.reshape(1), *inputs)


def join_qkv(core, mine, other, width):
    rows, half = mine.shape[0], width // 2

    def kernel(core_ref, mine_ref, other_ref, qkv_ref, proj_ref):
        for ref, place in ((mine_ref, core_ref[0]), (other_ref, 1 - core_ref[0])):
            at = place * half
            columns = lambda start, size: pl.ds(pl.multiple_of(at + start, PAIR), size)
            qkv_ref[:, columns(0, half)] = ref[:, :half].astype(f32)
            proj_ref[:, columns(0, half)] = ref[:, half:width].astype(f32)
            for g in range(half // PAIR):
                k = width + 2 * g * PAIR
                for i in range(2):
                    qkv_ref[:, columns((i + 1) * width + g * PAIR, PAIR)] = ref[
                        :, k + i * PAIR : k + (i + 1) * PAIR
                    ].astype(f32)

    return join(kernel, core, [mine, other], [(rows, 3 * width), (rows, width)])


def join_fc(core, mine, other, width, shards):
    rows = mine.shape[0]
    wide = mine.shape[1] - 2 * width
    part = wide // (2 * shards)
    pair = 2 * part

    def kernel(core_ref, mine_ref, other_ref, fc1_ref, fc2_ref):
        for ref, place in ((mine_ref, core_ref[0]), (other_ref, 1 - core_ref[0])):
            for f in range(shards):
                at = pl.multiple_of(2 * pair * f + place * pair, pair)
                value = [
                    ref[:, i * shards * part + f * part : i * shards * part + (f + 1) * part]
                    for i in range(2)
                ]
                fc1_ref[:, pl.ds(at, pair)] = jnp.concatenate(value, axis=1).astype(f32)
            for i in range(2):
                at = pl.multiple_of(place * 2 * rows + i * rows, rows)
                fc2_ref[pl.ds(at, rows)] = ref[
                    :, wide + i * width : wide + (i + 1) * width
                ].astype(f32)

    return join(kernel, core, [mine, other], [(rows, 2 * wide), (4 * rows, width)])


FLIP = [(0, 0), (1, 2), (2, 1), (3, 3)]


def to_images(tokens):
    count, rows, width = tokens.shape
    mixed = lax.all_to_all(tokens, "z", split_axis=0, concat_axis=0, tiled=True)
    return mixed.reshape(count * rows, width)


def flip(tokens):
    return lax.ppermute(tokens, ("yh", "core"), FLIP)


def from_images(arrays, count):
    rows, width = arrays[0].shape
    mixed = [flip(a) for a in arrays]
    mixed = jnp.stack([m.reshape(count, rows // count, width) for m in mixed], axis=1)
    mixed = lax.all_to_all(mixed, "z", split_axis=0, concat_axis=0, tiled=True)
    return [mixed[:, i] for i in range(len(arrays))]


RING_Z, RING_Y = "z", ("yh", "yl")
AHEAD = [(i, (i + 1) % 4) for i in range(4)]
BACK = [(i, (i - 1) % 4) for i in range(4)]


ACROSS = [(i, (i + 2) % 4) for i in range(4)]


def first_hop(value, axis):
    return lax.ppermute(value, axis, AHEAD), lax.ppermute(value, axis, BACK)


def second_hop(ahead, back, axis):
    half = ahead.shape[0] // 2
    return (
        lax.ppermute(ahead[:half], axis, AHEAD),
        lax.ppermute(back[half:], axis, BACK),
    )


def ring_place(value, axis, hops, out_shapes, views):
    pieces = [(value, 0, 0), (hops[0], 3, 0), (hops[1], 1, 0), (hops[2], 2, 0)]
    if len(hops) > 3:
        pieces.append((hops[3], 2, hops[2].shape[0]))
    n_outs = len(out_shapes)

    def kernel(index_ref, *refs):
        sources, outs = refs[: len(pieces)], refs[len(pieces) :]
        for source, (_, step, start) in zip(sources, pieces):
            place = lax.rem(index_ref[0] + step, 4)
            views(outs, source, place, start)

    vmem = pl.BlockSpec(memory_space=pltpu.VMEM)
    return pl.pallas_call(
        kernel,
        in_specs=[pl.BlockSpec(memory_space=pltpu.SMEM)] + [vmem] * len(pieces),
        out_specs=[vmem] * n_outs,
        out_shape=[jax.ShapeDtypeStruct(shape, value.dtype) for shape in out_shapes],
        compiler_params=pltpu.CompilerParams(vmem_limit_bytes=24 * 2**20),
        cost_estimate=pl.CostEstimate(
            flops=0, bytes_accessed=16 * value.size, transcendentals=0
        ),
        name="ring_place",
    )(lax.axis_index(axis).reshape(1), *(p[0] for p in pieces))


def in_order(outs, piece, place, start):
    outs[0][place, pl.ds(start, piece.shape[0])] = piece[...]


def add(*parts):
    return sum(p.astype(f32) for p in parts).astype(bf16)


def ring_blocks(blocks, axis, dim):
    index = lax.axis_index(axis)
    return [
        lax.dynamic_index_in_dim(blocks, (index + k) % 4, dim, keepdims=False) for k in range(4)
    ]


def ring_sums(items, beside):
    blocks = [ring_blocks(*item) for item in items]
    hops = []
    for (_, axis, _), (_, _, far, _) in zip(items, blocks):
        half = far.shape[0] // 2
        hops.append(
            (lax.ppermute(far[:half], axis, AHEAD), lax.ppermute(far[half:], axis, BACK))
        )
    hops, beside = lax.optimization_barrier((hops, beside))
    ends = []
    for (_, axis, _), (own, after, _, before), (low, high) in zip(items, blocks, hops):
        half = low.shape[0]
        after = jnp.concatenate([add(after[:half], low), after[half:]])
        before = jnp.concatenate([before[:half], add(before[half:], high)])
        ends.append((own, lax.ppermute(after, axis, AHEAD), lax.ppermute(before, axis, BACK)))
    ends = lax.optimization_barrier(ends)
    return [add(*e) for e in ends], beside


def direct_sums(items):
    ways = [(1, AHEAD), (3, BACK), (2, ACROSS)]
    parts = []
    for blocks, axis, dim in items:
        block = ring_blocks(blocks, axis, dim)
        parts.append([block[0]] + [lax.ppermute(block[k], axis, way) for k, way in ways])
    return [add(*p) for p in lax.optimization_barrier(parts)]


def group_parts(own, mate, near, far):
    mate, far = swap(mate, "core"), swap(far, "core")
    sent = (near.astype(f32) + far.astype(f32)).astype(bf16)
    return own.astype(f32) + mate.astype(f32), sent


def normal_part(values):
    mean = jnp.mean(values, axis=-1, keepdims=True)
    centred = values - mean
    factor = lax.rsqrt(jnp.mean(centred * centred, axis=-1, keepdims=True) + EPSILON)
    return centred * factor, factor


def norm_back(grad, normal, factor, gain):
    e = grad * gain
    inner = jnp.mean(e * normal, axis=-1, keepdims=True)
    return factor * (e - jnp.mean(e, axis=-1, keepdims=True) - normal * inner)


def flip_halves(core, value):
    half = value.shape[-1] // 2
    turned = jnp.concatenate([value[..., half:], value[..., :half]], axis=-1)
    return jnp.where(core == 0, value, turned)


CHUNKS = 2


def chunked(halves):
    size = halves[0].shape[1] // CHUNKS
    cut = lambda h, i: h[:, i * size : (i + 1) * size]
    return [jnp.concatenate([cut(h, i) for h in halves], axis=1) for i in range(CHUNKS)]


def unchunked(chunks):
    size = chunks[0].shape[1] // 2
    return [
        jnp.concatenate([c[:, i * size : (i + 1) * size] for c in chunks], axis=1)
        for i in range(2)
    ]


def forward(tokens, w, late=None):
    inputs = tokens.astype(f32)
    normed_one = (normal_part(inputs)[0] * w["gain"][0] + w["shift"][0]).astype(bf16)
    project = lambda name: [
        (mm(normed_one, part) + bias).astype(bf16) for part, bias in zip(w[name], w[name + "_bias"])
    ]
    key_value = chunked(project("kv"))
    queries = chunked(project("q"))
    mate, near = swap(key_value[0], "core"), swap(key_value[0], "yl")
    blocks, results = [], []
    for i, own in enumerate(key_value):
        blocks.append((own, mate, near, swap(near, "core")))
        if i + 1 < CHUNKS:
            following, near = lax.optimization_barrier((key_value[i + 1], near))
            mate, near = swap(following, "core"), swap(following, "yl")
            result = attend(queries[i], blocks[i])
            result, near = lax.optimization_barrier((result, near))
        else:
            if late is not None:
                (own, near), gathered = lax.optimization_barrier(((own, near), late[0]))
                w.update(late[1](gathered))
                blocks[i] = (own, mate, near, blocks[i][3])
            result = attend(queries[i], blocks[i])
        results.append(result)
    attended, log_total = zip(*results)
    attended = jnp.concatenate(unchunked(attended), axis=1)
    attended = flip_halves(w["core"], attended)
    branch = flip_halves(w["core"], jnp.concatenate([mm(attended, p) for p in w["proj"]], axis=1))
    branch = branch + w["out_bias"][0]
    middle = inputs + w["scale"][0] * branch
    normed_two = (normal_part(middle)[0] * w["gain"][1] + w["shift"][1]).astype(bf16)
    activated, slope, branch_two = [], [], w["out_bias"][1]
    for up, bias, down in zip(w["fc1"], w["fc1_bias"], w["fc2"]):
        before = mm(normed_two, up) + bias
        phi = 0.5 * (1.0 + lax.erf(before * (0.5**0.5)))
        density = jnp.exp(-0.5 * before * before) * 0.3989422804014327
        active = (before * phi).astype(bf16)
        activated.append(active)
        slope.append((phi + before * density).astype(bf16))
        for i, part in enumerate(down):
            rows = part.shape[0]
            branch_two = branch_two + mm(active[:, i * rows : (i + 1) * rows], part)
    result = (middle + w["scale"][1] * branch_two).astype(bf16)
    kept = dict(
        inputs=inputs,
        normed_one=normed_one,
        queries=queries,
        blocks=blocks,
        attended=attended,
        log_total=log_total,
        branch=branch,
        middle=middle,
        normed_two=normed_two,
        activated=activated,
        slope=slope,
        branch_two=branch_two,
    )
    return result, kept


def backward(grad_out, kept, w, last=False):
    grad_branch_two = (w["scale"][1] * grad_out).astype(bf16)
    grad_before = []
    grad_normed_two = 0.0
    if last:
        fc2_sent = swap(fc2_part(kept["activated"][1], grad_branch_two), "core")
    for up, down, slope in zip(w["fc1"], w["fc2"], kept["slope"]):
        part = jnp.concatenate([mm_t(grad_branch_two, d) for d in down], axis=1)
        part = (part * slope.astype(f32)).astype(bf16)
        grad_before.append(part)
        grad_normed_two = grad_normed_two + mm_t(part, up)
    if last:
        fc2 = fc2_part(kept["activated"][0], grad_branch_two, fc2_sent)
        fc2, grad_normed_two = lax.optimization_barrier((fc2, grad_normed_two))
        fc2 = lax.psum_scatter(fc2, RING_Z, scatter_dimension=0, tiled=True)
    normal_two, factor_two = normal_part(kept["middle"])
    grad_middle = grad_out + norm_back(grad_normed_two, normal_two, factor_two, w["gain"][1])
    grad_branch = (w["scale"][0] * grad_middle).astype(bf16)
    width = grad_branch.shape[1]
    half = width // 2
    grad_halves = flip_halves(w["core"], grad_branch)
    grad_halves = [grad_halves[:, :half], grad_halves[:, half:]]
    grad_attended = sum(mm_t(g, p) for g, p in zip(grad_halves, w["proj"])).astype(bf16)
    grad_attended = flip_halves(w["core"], grad_attended)
    fc_grad = None
    if last:
        fc1_sent = fc1_part(kept["normed_two"], grad_before[1])
        fc1_sent, grad_attended = lax.optimization_barrier((fc1_sent, grad_attended))
        fc1_sent = swap(fc1_sent, "core")
    grad_chunks = chunked([grad_attended[:, :half], grad_attended[:, half:]])
    q_chunks, kv_chunks = [], []
    ready = None
    for i in range(CHUNKS):
        g = grad_chunks[i]
        if ready is not None:
            own, sent = ready
            if last and fc_grad is None:
                fc1 = fc1_part(kept["normed_two"], grad_before[0], fc1_sent)
                sent, g, fc1 = lax.optimization_barrier((sent, g, fc1))
                fc1 = lax.psum_scatter(fc1, RING_Z, scatter_dimension=0, tiled=True)
                fc_grad = [fc1, fc2]
            else:
                sent, g = lax.optimization_barrier((sent, g))
            came = swap(sent, "yl")
        parts = attend_back(kept["queries"][i], kept["blocks"][i], g, kept["log_total"][i])
        if ready is not None:
            parts, came = lax.optimization_barrier((parts, came))
            kv_chunks.append((own + came.astype(f32)).astype(bf16))
        q_chunks.append(parts[0])
        ready = group_parts(*parts[1:])
    kv_chunks.append((ready[0] + swap(ready[1], "yl").astype(f32)).astype(bf16))
    grad_q, grad_kv = unchunked(q_chunks), unchunked(kv_chunks)
    grad_normed_one = sum(
        mm_t(g, part) for g, part in zip(grad_q + grad_kv, w["q"] + w["kv"])
    )
    normal_one, factor_one = normal_part(kept["inputs"])
    grad_inputs = grad_middle + norm_back(grad_normed_one, normal_one, factor_one, w["gain"][0])
    total = lambda a: jnp.sum(a.astype(f32), axis=0, keepdims=True)
    vectors = dict(
        gain=(total(grad_normed_one * normal_one), total(grad_normed_two * normal_two)),
        shift=(total(grad_normed_one), total(grad_normed_two)),
        out_bias=(total(grad_branch), total(grad_branch_two)),
        scale=(total(grad_middle * kept["branch"]), total(grad_out * kept["branch_two"])),
        q=[total(g) for g in grad_q],
        kv=[total(g) for g in grad_kv],
        fc1_bias=[total(g) for g in grad_before],
    )
    products = dict(
        q=(kept["normed_one"], grad_q),
        kv=(kept["normed_one"], grad_kv),
        proj=(kept["attended"], grad_halves),
        fc=fc_grad,
    )
    return grad_inputs.astype(bf16), vectors, products


def ordered(core, mine, other):
    return jnp.where(core == 0, mine, other), jnp.where(core == 0, other, mine)


def per_device(
    patch_tokens,
    out_grad,
    batch_counts,
    norm_gain,
    norm_bias,
    qkv_weight,
    qv_bias,
    proj_weight,
    fc1_weight,
    fc1_bias,
    fc2_weight,
    out_bias,
    layer_scale,
):
    section = lax.axis_index("section")
    core = lax.axis_index("core")
    shards = lax.axis_size(FSDP)
    images, rows, width = patch_tokens.shape
    half = width // 2
    own = width // shards
    hidden = fc2_weight.shape[1]
    mid = hidden // 2
    groups = half // PAIR
    pick = lambda a, i, axis: lax.dynamic_index_in_dim(a, i, axis, keepdims=False)

    part = mid // 2
    q, k, v = (qkv_weight[0][:, i * width : (i + 1) * width] for i in range(3))
    q_mine = pick(q.reshape(own, 2, half), core, 1)
    kv = jnp.stack([k.reshape(own, 2, groups, PAIR), v.reshape(own, 2, groups, PAIR)], axis=3)
    kv_mine = pick(kv, core, 1).reshape(own, width)
    proj_mine = pick(proj_weight[0].reshape(own, 2, half), core, 1)
    vectors = jnp.concatenate(
        [a[0] for a in (norm_gain, norm_bias, qv_bias, out_bias, layer_scale)]
        + [fc1_bias[0].reshape(hidden // own, own)],
        axis=0,
    ).T
    count = vectors.shape[1]
    vectors = jnp.pad(vectors, ((0, 0), (0, 128 - count)))
    fc1_mine = pick(fc1_weight[0].reshape(own, shards, 2, 2, part), core, 2)
    fc1_mine = jnp.swapaxes(fc1_mine, 1, 2).reshape(own, shards * mid)
    fc2_mine = pick(fc2_weight[0].reshape(2, 2, part, width), core, 0)
    fc_mine = jnp.concatenate([fc1_mine, fc2_mine[0], fc2_mine[1]], axis=1)

    a_mine = jnp.concatenate([q_mine, proj_mine, vectors], axis=1)
    live = (
        jnp.arange(images) % IMG_MB < jnp.repeat(batch_counts[0], IMG_MB)
    ).astype(bf16)
    live_grad = out_grad * live[:, None, None]
    direct = lambda value, axis: (*first_hop(value, axis), lax.ppermute(value, axis, ACROSS))
    first = (direct(a_mine, RING_Y), direct(kv_mine, RING_Z))
    first, fc_mine, live_grad, first_tokens = lax.optimization_barrier(
        (first, fc_mine, live_grad, to_images(patch_tokens))
    )
    fc_half = lax.all_gather(fc_mine, FSDP, axis=0, tiled=True)
    a_wide = a_mine.shape[1]
    a_row = ring_place(a_mine, RING_Y, first[0], [(4, own, a_wide)], in_order)[0]
    a_row = a_row.reshape(4 * own, a_wide)
    b_row = ring_place(kv_mine, RING_Z, first[1], [(4, own, width)], in_order)[0]
    hops = lax.optimization_barrier((first_hop(a_row, RING_Z), first_hop(b_row, RING_Y)))
    more = (second_hop(*hops[0], RING_Z), second_hop(*hops[1], RING_Y))
    more, first_tokens = lax.optimization_barrier((more, flip(first_tokens)))

    def a_views(outs, piece, place, start):
        at = 0
        for out in outs:
            size = out.shape[-1]
            out[place, pl.ds(start, piece.shape[0])] = piece[:, pl.ds(at, size)]
            at += size

    def b_views(outs, piece, place, start):
        for i in range(piece.shape[0]):
            outs[0][start + i, place] = piece[i]

    q_half, proj_half, vectors = (
        o.reshape(width, -1)
        for o in ring_place(
            a_row, RING_Z, hops[0] + more[0], [(4, 4 * own, half), (4, 4 * own, half), (4, 4 * own, 128)], a_views
        )
    )
    kv_half = ring_place(b_row, RING_Y, hops[1] + more[1], [(4, 4, own, width)], b_views)[0]
    kv_half = kv_half.reshape(width, width)
    vectors = vectors[:, :16].T.astype(f32)

    def halves(row):
        return ordered(core, row[:, :half], row[:, half:])

    def fc1_bias_of(which):
        rows = jnp.where(which == 0, vectors[10:12], vectors[12:14])
        return jnp.concatenate([rows[0:1], rows[1:2]], axis=1)

    def kv_bias(v_half):
        zeros = jnp.zeros((1, PAIR), f32)
        cuts = [v_half[:, i * PAIR : (i + 1) * PAIR] for i in range(groups)]
        return jnp.concatenate([x for c in cuts for x in (zeros, c)], axis=1)

    wide = shards * mid
    w = dict(
        core=core,
        gain=(vectors[0:1], vectors[1:2]),
        shift=(vectors[2:3], vectors[3:4]),
        out_bias=(vectors[6:7], vectors[7:8]),
        scale=(vectors[8:9], vectors[9:10]),
        q=[q_half, swap(q_half, "core")],
        q_bias=halves(vectors[4:5]),
        kv=[kv_half, swap(kv_half, "core")],
        kv_bias=[kv_bias(b) for b in halves(vectors[5:6])],
        proj=(proj_half, swap(proj_half, "core")),
        fc1_bias=[fc1_bias_of(c) for c in (core, 1 - core)],
    )

    def fc_weights(gathered):
        pair = (gathered, swap(gathered, "core"))
        return dict(
            fc1=[f[:, :wide] for f in pair],
            fc2=[(f[:, wide : wide + width], f[:, wide + width :]) for f in pair],
        )


    sent, _ = forward(first_tokens, w, late=(fc_half, fc_weights))
    sent, live_grad = lax.optimization_barrier((sent, live_grad))
    passed = lax.ppermute(sent, "section", [(0, 1)])
    last_grad = flip(to_images(live_grad))
    tokens = jnp.where(section == 0, first_tokens, passed)
    result, kept = forward(tokens, w)

    sent, _, _ = backward(last_grad.astype(f32), kept, w)
    passed = lax.ppermute(sent, "section", [(1, 0)])
    grad_out = jnp.where(section == 1, last_grad, passed).astype(f32)
    grad_inputs, sums, products = backward(grad_out, kept, w, last=True)
    result, grad_inputs = lax.optimization_barrier((result, grad_inputs))
    block_out, in_grad = from_images([result, grad_inputs], images)

    def natural(pair):
        return jnp.concatenate(ordered(core, *pair), axis=1)

    def v_sum(a):
        cuts = [a[:, (2 * i + 1) * PAIR : (2 * i + 2) * PAIR] for i in range(groups)]
        return jnp.concatenate(cuts, axis=1)

    fc1_rows = [
        jnp.concatenate([b[:, :width], b[:, width:]], axis=0)
        for b in ordered(core, *sums["fc1_bias"])
    ]
    vector_grads = jnp.concatenate(
        [
            *sums["gain"],
            *sums["shift"],
            natural(sums["q"]),
            natural([v_sum(g) for g in sums["kv"]]),
            *sums["out_bias"],
            *sums["scale"],
            *fc1_rows,
            jnp.zeros((PAIR - count, width), f32),
        ],
        axis=0,
    )
    vector_grads = vector_grads.astype(bf16).T

    a1, dq = products["q"]
    dkv = products["kv"][1]
    o, e1 = products["proj"]
    make = lambda i, add=None: outer(
        [((a1, 0), dq[i], width), ((o, 0), e1[i], width), ((a1, 0), dkv[i], width)], 256, add=add
    )
    ab = make(0, swap(make(1), "core")).reshape(4, 4, own, 2 * width)
    (a_sum, b_sum), (rows, vector_grads) = ring_sums(
        [(ab[..., :width], RING_Y, 1), (ab[..., width:], RING_Z, 0)],
        (products["fc"], vector_grads),
    )
    fc_grad = lax.psum_scatter(
        jnp.concatenate(rows, axis=1), RING_Y, scatter_dimension=0, tiled=True
    )
    vector_grads = vector_grads.reshape(4, 4, own, PAIR)
    (vector_sum,) = direct_sums([(vector_grads, RING_Y, 1)])
    ab = direct_sums(
        [(jnp.concatenate([a_sum, vector_sum], axis=2), RING_Z, 0), (b_sum, RING_Y, 0)]
    )
    ab = jnp.concatenate([ab[0][:, :width], ab[1], ab[0][:, width:]], axis=1)

    def chips_sum(a):
        return (a.astype(f32) + swap(a, "xhi").astype(f32)).astype(bf16)

    ab = chips_sum(ab)
    ab_other = swap(ab, "core")
    qkv_out, proj_out = join_qkv(core, ab, ab_other, width)
    vec_grad = sum(p[:, 2 * width : 2 * width + count].astype(f32) for p in (ab, ab_other)).T
    fc_grad = chips_sum(fc_grad)
    fc1_out, fc2_out = join_fc(core, fc_grad, swap(fc_grad, "core"), width, shards)
    return (
        block_out[None],
        in_grad[None],
        vec_grad[0:2][None],
        vec_grad[2:4][None],
        qkv_out[None],
        vec_grad[4:6][None],
        proj_out[None],
        fc1_out[None],
        vec_grad[10:].reshape(1, hidden),
        fc2_out[None],
        vec_grad[6:8][None],
        vec_grad[8:10][None],
    )


def solution(mesh):
    sections, fsdp, rep = mesh.devices.shape
    inner = Mesh(
        mesh.devices.reshape(sections, fsdp // 4, 2, 2, rep // 2, 2),
        ("section",) + FSDP + REP,
    )
    weight = P("section", FSDP, None)
    vector = P("section", None, FSDP)
    tokens = P(REP, FSDP, None)
    both = P("section", REP, FSDP, None)
    return jax.shard_map(
        per_device,
        mesh=inner,
        in_specs=(
            tokens,
            tokens,
            P(REP, None),
            vector,
            vector,
            weight,
            vector,
            weight,
            weight,
            P("section", FSDP),
            weight,
            vector,
            vector,
        ),
        out_specs=(
            both,
            both,
            vector,
            vector,
            weight,
            vector,
            weight,
            weight,
            P("section", FSDP),
            weight,
            vector,
            vector,
        ),
        check_vma=False,
    )
```

```python
import jax
import jax.numpy as jnp
from jax import lax
from jax.experimental import pallas as pl
from jax.experimental.pallas import tpu as pltpu
from jax.sharding import Mesh, PartitionSpec as P

HEAD_DIM = 64
IMG_MB = 2
PAIR = 2 * HEAD_DIM
EPSILON = 1e-06

FSDP = ("z", "yh", "yl")
REP = ("xhi", "core")
bf16 = jnp.bfloat16
f32 = jnp.float32


def dot(a, b, dims):
    return lax.dot_general(a, b, (dims, ((), ())), preferred_element_type=f32)


def mm(a, b):
    return dot(a, b, ((1,), (0,)))


def mm_t(a, b):
    return dot(a, b, ((1,), (1,)))


def t_mm(a, b):
    return dot(a, b, ((0,), (0,)))


def swap(value, axis):
    return lax.ppermute(value, axis, [(0, 1), (1, 0)])


def attend_kernel(q_ref, own_ref, mate_ref, near_ref, far_ref, out_ref, log_ref):
    rows = q_ref.shape[0]
    both = [r[...] for r in (own_ref, mate_ref, near_ref, far_ref)]
    keys = jnp.concatenate([b[:, :PAIR] for b in both], axis=0)
    values = jnp.concatenate([b[:, PAIR:] for b in both], axis=0)
    queries = q_ref[...] * jnp.asarray(HEAD_DIM**-0.5, bf16)
    lane = lax.broadcasted_iota(jnp.int32, (rows, PAIR), 1)
    outs = []
    for head in range(2):
        mine = (lane >= head * HEAD_DIM) & (lane < (head + 1) * HEAD_DIM)
        picked = jnp.where(mine, queries, jnp.zeros_like(queries))
        scores = mm_t(keys, picked)
        top = jnp.max(scores, axis=0, keepdims=True)
        raised = jnp.exp(scores - top)
        total = jnp.sum(raised, axis=0, keepdims=True)
        out = t_mm(values, raised.astype(bf16))
        outs.append(out * (1.0 / total))
        log_ref[0, head : head + 1, :] = top + jnp.log(total)
    row = lax.broadcasted_iota(jnp.int32, (PAIR, rows), 0)
    joined = jnp.where(row < HEAD_DIM, outs[0], outs[1])
    out_ref[...] = joined.T.astype(bf16)


def attend_back_kernel(
    q_ref, own_ref, mate_ref, near_ref, far_ref, grad_ref, log_ref, dq_ref, *dkv_refs
):
    rows = q_ref.shape[0]
    both = [r[...] for r in (own_ref, mate_ref, near_ref, far_ref)]
    keys = jnp.concatenate([b[:, :PAIR] for b in both], axis=0)
    values = jnp.concatenate([b[:, PAIR:] for b in both], axis=0)
    queries = q_ref[...] * jnp.asarray(HEAD_DIM**-0.5, bf16)
    grads = grad_ref[...]
    lane = lax.broadcasted_iota(jnp.int32, (rows, PAIR), 1)
    dqs, dk, dv = [], None, None
    for head in range(2):
        mine = (lane >= head * HEAD_DIM) & (lane < (head + 1) * HEAD_DIM)
        picked = jnp.where(mine, queries, jnp.zeros_like(queries))
        grad = jnp.where(mine, grads, jnp.zeros_like(grads))
        scores = mm_t(keys, picked)
        weighting = jnp.exp(scores - log_ref[0, head : head + 1, :])
        grad_weighting = mm_t(values, grad)
        row_term = jnp.sum(grad_weighting * weighting, axis=0, keepdims=True)
        grad_scores = (weighting * (grad_weighting - row_term)).astype(bf16)
        dqs.append(t_mm(keys, grad_scores))
        k_part = mm(grad_scores, picked)
        v_part = mm(weighting.astype(bf16), grad)
        dk = k_part if dk is None else dk + k_part
        dv = v_part if dv is None else dv + v_part
    row = lax.broadcasted_iota(jnp.int32, (PAIR, rows), 0)
    joined = jnp.where(row < HEAD_DIM, dqs[0], dqs[1]) * (HEAD_DIM**-0.5)
    dq_ref[...] = joined.T.astype(bf16)
    for i, ref in enumerate(dkv_refs):
        ref[:, :PAIR] = dk[i * rows : (i + 1) * rows].astype(bf16)
        ref[:, PAIR:] = dv[i * rows : (i + 1) * rows].astype(bf16)


def pair_specs(rows, pairs):
    half = pairs // 2
    q_spec = pl.BlockSpec((rows, PAIR), lambda i: (0, i))
    kv_spec = pl.BlockSpec((rows, 2 * PAIR), lambda i: (0, i))
    kv_swapped = pl.BlockSpec((rows, 2 * PAIR), lambda i: (0, (i + half) % pairs))
    log_spec = pl.BlockSpec((1, 2, rows), lambda i: (i, 0, 0))
    return q_spec, [kv_spec, kv_swapped, kv_spec, kv_swapped], log_spec


def attend_cost(queries, blocks, products):
    rows, width = queries.shape
    scores = rows * rows * len(blocks) * width // HEAD_DIM
    return pl.CostEstimate(
        flops=products * scores * 2 * 256,
        bytes_accessed=2 * 2 * len(blocks) * rows * width * 2,
        transcendentals=scores,
    )


def attend(queries, blocks):
    rows, width = queries.shape
    pairs = width // PAIR
    q_spec, kv_specs, log_spec = pair_specs(rows, pairs)
    return pl.pallas_call(
        attend_kernel,
        grid=(pairs,),
        in_specs=[q_spec] + kv_specs,
        out_specs=[q_spec, log_spec],
        out_shape=[
            jax.ShapeDtypeStruct((rows, width), bf16),
            jax.ShapeDtypeStruct((pairs, 2, rows), f32),
        ],
        compiler_params=pltpu.CompilerParams(vmem_limit_bytes=40 * 2**20),
        cost_estimate=attend_cost(queries, blocks, 2),
        name="attend",
    )(queries, *blocks)


def attend_back(queries, blocks, grad, log_total):
    rows, width = queries.shape
    pairs = width // PAIR
    q_spec, kv_specs, log_spec = pair_specs(rows, pairs)
    return pl.pallas_call(
        attend_back_kernel,
        grid=(pairs,),
        in_specs=[q_spec] + kv_specs + [q_spec, log_spec],
        out_specs=[q_spec] + kv_specs,
        out_shape=[jax.ShapeDtypeStruct((rows, width), bf16)]
        + [jax.ShapeDtypeStruct((rows, 2 * width), bf16)] * 4,
        compiler_params=pltpu.CompilerParams(vmem_limit_bytes=40 * 2**20),
        cost_estimate=attend_cost(queries, blocks, 5),
        name="attend_back",
    )(queries, *blocks, grad, log_total)


def outer(segments, step, add=None, tail=None):
    rows = segments[0][1].shape[0]
    width = segments[0][2]
    counts = [right.shape[1] // step for _, right, _ in segments]
    starts = [sum(counts[:k]) for k in range(len(counts))]
    total = sum(counts)
    grid = total + (tail is not None)
    n = len(segments)

    def kernel(*refs):
        out_ref = refs[-1]
        i = pl.program_id(0)
        for k in range(n):

            @pl.when((i >= starts[k]) & (i < starts[k] + counts[k]))
            def _(k=k):
                value = t_mm(refs[2 * k][...], refs[2 * k + 1][...])
                if add is not None:
                    value = value + refs[2 * n][...].astype(f32)
                out_ref[...] = value.astype(bf16)

        if tail is not None:

            @pl.when(i == total)
            def _():
                out_ref[...] = refs[2 * n + (add is not None)][...]

    in_specs, operands = [], []
    for (left, right, _), start, count in zip(segments, starts, counts):
        array, which = left
        in_specs.append(pl.BlockSpec((rows, width), lambda i, w=which: (0, w)))
        in_specs.append(
            pl.BlockSpec((rows, step), lambda i, s=start, c=count: (0, jnp.clip(i - s, 0, c - 1)))
        )
        operands += [array, right]
    if add is not None:
        in_specs.append(pl.BlockSpec((width, step), lambda i: (0, jnp.minimum(i, total - 1))))
        operands.append(add)
    if tail is not None:
        in_specs.append(pl.BlockSpec((width, step), lambda i: (0, 0)))
        operands.append(tail)
    return pl.pallas_call(
        kernel,
        grid=(grid,),
        in_specs=in_specs,
        out_specs=pl.BlockSpec((width, step), lambda i: (0, i)),
        out_shape=jax.ShapeDtypeStruct((width, grid * step), bf16),
        compiler_params=pltpu.CompilerParams(vmem_limit_bytes=40 * 2**20),
        cost_estimate=pl.CostEstimate(
            flops=2 * rows * width * total * step,
            bytes_accessed=2 * width * grid * step * (1 if add is None else 2),
            transcendentals=0,
        ),
        name="outer",
    )(*operands)


def fc1_part(normed, grad_before, add=None):
    return outer([((normed, 0), grad_before, normed.shape[1])], 512, add=add)


def fc2_part(activated, grad_branch, add=None):
    width = grad_branch.shape[1]
    count = activated.shape[1] // width
    return outer([((activated, i), grad_branch, width) for i in range(count)], 512, add=add)


def join(kernel, core, inputs, shapes):
    vmem = pl.BlockSpec(memory_space=pltpu.VMEM)
    return pl.pallas_call(
        kernel,
        in_specs=[pl.BlockSpec(memory_space=pltpu.SMEM)] + [vmem] * len(inputs),
        out_specs=[vmem] * len(shapes),
        out_shape=[jax.ShapeDtypeStruct(shape, f32) for shape in shapes],
        compiler_params=pltpu.CompilerParams(vmem_limit_bytes=24 * 2**20),
        cost_estimate=pl.CostEstimate(
            flops=0, bytes_accessed=6 * sum(a.size for a in inputs), transcendentals=0
        ),
        name="join",
    )(core.reshape(1), *inputs)


def vector_block(core, sums, width, columns):
    half = width // 2
    whole = [*sums["gain"], *sums["shift"], *sums["out_bias"], *sums["scale"]]
    halves = [*sums["q"], *sums["kv"], *sums["fc1_bias"]]

    def kernel(core_ref, *refs):
        out_ref, rows_ref = refs[-2:]
        flag = core_ref[0]
        order = lambda a, b: (jnp.where(flag == 0, a, b), jnp.where(flag == 0, b, a))
        rows_ref[...] = jnp.zeros(rows_ref.shape, f32)
        for ref, row in zip(refs, (0, 1, 2, 3, 6, 7, 8, 9)):
            rows_ref[row : row + 1, :] = ref[...]
        q_mine, q_other, kv_mine, kv_other, fc_mine, fc_other = (
            r[...] for r in refs[len(whole) : len(whole) + len(halves)]
        )
        for i, value in enumerate(order(q_mine, q_other)):
            rows_ref[4:5, i * half : (i + 1) * half] = value
        for i, value in enumerate(order(kv_mine, kv_other)):
            for g in range(half // PAIR):
                at = i * half + g * PAIR
                rows_ref[5:6, at : at + PAIR] = value[:, (2 * g + 1) * PAIR : (2 * g + 2) * PAIR]
        for i, value in enumerate(order(fc_mine, fc_other)):
            for k in range(2):
                row = 10 + 2 * i + k
                rows_ref[row : row + 1, :] = value[:, k * width : (k + 1) * width]
        out_ref[...] = rows_ref[...].T.astype(bf16)

    vmem = pl.BlockSpec(memory_space=pltpu.VMEM)
    return pl.pallas_call(
        kernel,
        in_specs=[pl.BlockSpec(memory_space=pltpu.SMEM)] + [vmem] * len(whole + halves),
        out_specs=vmem,
        out_shape=jax.ShapeDtypeStruct((width, columns), bf16),
        scratch_shapes=[pltpu.VMEM((columns, width), f32)],
        name="vector_block",
    )(core.reshape(1), *whole, *halves)


def join_qkv(core, mine, other, width):
    rows, half = mine.shape[0], width // 2

    def kernel(core_ref, mine_ref, other_ref, qkv_ref, proj_ref):
        for ref, place in ((mine_ref, core_ref[0]), (other_ref, 1 - core_ref[0])):
            at = place * half
            columns = lambda start, size: pl.ds(pl.multiple_of(at + start, PAIR), size)
            qkv_ref[:, columns(0, half)] = ref[:, :half].astype(f32)
            proj_ref[:, columns(0, half)] = ref[:, half:width].astype(f32)
            for g in range(half // PAIR):
                k = width + 2 * g * PAIR
                for i in range(2):
                    qkv_ref[:, columns((i + 1) * width + g * PAIR, PAIR)] = ref[
                        :, k + i * PAIR : k + (i + 1) * PAIR
                    ].astype(f32)

    return join(kernel, core, [mine, other], [(rows, 3 * width), (rows, width)])


def join_fc(core, mine, other, width, shards):
    rows = mine.shape[0]
    wide = mine.shape[1] - 2 * width
    part = wide // (2 * shards)
    pair = 2 * part

    def kernel(core_ref, mine_ref, other_ref, fc1_ref, fc2_ref):
        for ref, place in ((mine_ref, core_ref[0]), (other_ref, 1 - core_ref[0])):
            for f in range(shards):
                at = pl.multiple_of(2 * pair * f + place * pair, pair)
                value = [
                    ref[:, i * shards * part + f * part : i * shards * part + (f + 1) * part]
                    for i in range(2)
                ]
                fc1_ref[:, pl.ds(at, pair)] = jnp.concatenate(value, axis=1).astype(f32)
            for i in range(2):
                at = pl.multiple_of(place * 2 * rows + i * rows, rows)
                fc2_ref[pl.ds(at, rows)] = ref[
                    :, wide + i * width : wide + (i + 1) * width
                ].astype(f32)

    return join(kernel, core, [mine, other], [(rows, 2 * wide), (4 * rows, width)])


FLIP = [(0, 0), (1, 2), (2, 1), (3, 3)]


def to_images(tokens):
    count, rows, width = tokens.shape
    mixed = lax.all_to_all(tokens, "z", split_axis=0, concat_axis=0, tiled=True)
    return mixed.reshape(count * rows, width)


def flip(tokens):
    return lax.ppermute(tokens, ("yh", "core"), FLIP)


def from_images(tokens, count):
    rows, width = tokens.shape
    mixed = flip(tokens).reshape(count, rows // count, width)
    return lax.all_to_all(mixed, "z", split_axis=0, concat_axis=0, tiled=True)


RING_Z, RING_Y = "z", ("yh", "yl")
AHEAD = [(i, (i + 1) % 4) for i in range(4)]
BACK = [(i, (i - 1) % 4) for i in range(4)]


ACROSS = [(i, (i + 2) % 4) for i in range(4)]


def first_hop(value, axis):
    return lax.ppermute(value, axis, AHEAD), lax.ppermute(value, axis, BACK)


def second_hop(ahead, back, axis):
    half = ahead.shape[0] // 2
    return (
        lax.ppermute(ahead[:half], axis, AHEAD),
        lax.ppermute(back[half:], axis, BACK),
    )


def ring_place(value, axis, hops, out_shapes, views):
    pieces = [(value, 0, 0), (hops[0], 3, 0), (hops[1], 1, 0), (hops[2], 2, 0)]
    if len(hops) > 3:
        pieces.append((hops[3], 2, hops[2].shape[0]))
    n_outs = len(out_shapes)

    def kernel(index_ref, *refs):
        sources, outs = refs[: len(pieces)], refs[len(pieces) :]
        for source, (_, step, start) in zip(sources, pieces):
            place = lax.rem(index_ref[0] + step, 4)
            views(outs, source, place, start)

    vmem = pl.BlockSpec(memory_space=pltpu.VMEM)
    return pl.pallas_call(
        kernel,
        in_specs=[pl.BlockSpec(memory_space=pltpu.SMEM)] + [vmem] * len(pieces),
        out_specs=[vmem] * n_outs,
        out_shape=[jax.ShapeDtypeStruct(shape, value.dtype) for shape in out_shapes],
        compiler_params=pltpu.CompilerParams(vmem_limit_bytes=24 * 2**20),
        cost_estimate=pl.CostEstimate(
            flops=0, bytes_accessed=16 * value.size, transcendentals=0
        ),
        name="ring_place",
    )(lax.axis_index(axis).reshape(1), *(p[0] for p in pieces))


def in_order(outs, piece, place, start):
    outs[0][place, pl.ds(start, piece.shape[0])] = piece[...]


def add(*parts):
    return sum(p.astype(f32) for p in parts).astype(bf16)


def ring_blocks(blocks, axis, dim):
    index = lax.axis_index(axis)
    return [
        lax.dynamic_index_in_dim(blocks, (index + k) % 4, dim, keepdims=False) for k in range(4)
    ]


def ring_sums(items, beside):
    blocks = [ring_blocks(*item) for item in items]
    hops = []
    for (_, axis, _), (_, _, far, _) in zip(items, blocks):
        half = far.shape[0] // 2
        hops.append(
            (lax.ppermute(far[:half], axis, AHEAD), lax.ppermute(far[half:], axis, BACK))
        )
    hops, beside = lax.optimization_barrier((hops, beside))
    ends = []
    for (_, axis, _), (own, after, _, before), (low, high) in zip(items, blocks, hops):
        half = low.shape[0]
        after = jnp.concatenate([add(after[:half], low), after[half:]])
        before = jnp.concatenate([before[:half], add(before[half:], high)])
        ends.append((own, lax.ppermute(after, axis, AHEAD), lax.ppermute(before, axis, BACK)))
    ends = lax.optimization_barrier(ends)
    return [add(*e) for e in ends], beside


def direct_sums(items, beside=None):
    ways = [(1, AHEAD), (3, BACK), (2, ACROSS)]
    parts = []
    for blocks, axis, dim in items:
        block = ring_blocks(blocks, axis, dim)
        parts.append([block[0]] + [lax.ppermute(block[k], axis, way) for k, way in ways])
    parts, beside = lax.optimization_barrier((parts, beside))
    return [add(*p) for p in parts], beside


def group_parts(own, mate, near, far):
    mate, far = swap(mate, "core"), swap(far, "core")
    sent = (near.astype(f32) + far.astype(f32)).astype(bf16)
    return own.astype(f32) + mate.astype(f32), sent


def normal_part(values):
    mean = jnp.mean(values, axis=-1, keepdims=True)
    centred = values - mean
    factor = lax.rsqrt(jnp.mean(centred * centred, axis=-1, keepdims=True) + EPSILON)
    return centred * factor, factor


def norm_back(grad, normal, factor, gain):
    e = grad * gain
    inner = jnp.mean(e * normal, axis=-1, keepdims=True)
    return factor * (e - jnp.mean(e, axis=-1, keepdims=True) - normal * inner)


def flip_halves(core, value):
    half = value.shape[-1] // 2
    turned = jnp.concatenate([value[..., half:], value[..., :half]], axis=-1)
    return jnp.where(core == 0, value, turned)


CHUNKS = 2


def chunked(halves):
    size = halves[0].shape[1] // CHUNKS
    cut = lambda h, i: h[:, i * size : (i + 1) * size]
    return [jnp.concatenate([cut(h, i) for h in halves], axis=1) for i in range(CHUNKS)]


def unchunked(chunks):
    size = chunks[0].shape[1] // 2
    return [
        jnp.concatenate([c[:, i * size : (i + 1) * size] for c in chunks], axis=1)
        for i in range(2)
    ]


def forward(tokens, w, late=None):
    inputs = tokens.astype(f32)
    normed_one = (normal_part(inputs)[0] * w["gain"][0] + w["shift"][0]).astype(bf16)
    project = lambda name: [
        (mm(normed_one, part) + bias).astype(bf16) for part, bias in zip(w[name], w[name + "_bias"])
    ]
    key_value = chunked(project("kv"))
    queries = chunked(project("q"))
    mate, near = swap(key_value[0], "core"), swap(key_value[0], "yl")
    blocks, results = [], []
    for i, own in enumerate(key_value):
        blocks.append((own, mate, near, swap(near, "core")))
        if i + 1 < CHUNKS:
            following, near = lax.optimization_barrier((key_value[i + 1], near))
            mate, near = swap(following, "core"), swap(following, "yl")
            result = attend(queries[i], blocks[i])
            result, near, mate = lax.optimization_barrier((result, near, mate))
        else:
            if late is not None:
                blocks[i], gathered = lax.optimization_barrier((blocks[i], late[0]))
                w.update(late[1](gathered))
            result = attend(queries[i], blocks[i])
        results.append(result)
    attended, log_total = zip(*results)
    attended = jnp.concatenate(unchunked(attended), axis=1)
    attended = flip_halves(w["core"], attended)
    branch = flip_halves(w["core"], jnp.concatenate([mm(attended, p) for p in w["proj"]], axis=1))
    branch = branch + w["out_bias"][0]
    middle = inputs + w["scale"][0] * branch
    normed_two = (normal_part(middle)[0] * w["gain"][1] + w["shift"][1]).astype(bf16)
    activated, slope, branch_two = [], [], w["out_bias"][1]
    for up, bias, down in zip(w["fc1"], w["fc1_bias"], w["fc2"]):
        before = mm(normed_two, up) + bias
        phi = 0.5 * (1.0 + lax.erf(before * (0.5**0.5)))
        density = jnp.exp(-0.5 * before * before) * 0.3989422804014327
        active = (before * phi).astype(bf16)
        activated.append(active)
        slope.append((phi + before * density).astype(bf16))
        for i, part in enumerate(down):
            rows = part.shape[0]
            branch_two = branch_two + mm(active[:, i * rows : (i + 1) * rows], part)
    result = (middle + w["scale"][1] * branch_two).astype(bf16)
    kept = dict(
        inputs=inputs,
        normed_one=normed_one,
        queries=queries,
        blocks=blocks,
        attended=attended,
        log_total=log_total,
        branch=branch,
        middle=middle,
        normed_two=normed_two,
        activated=activated,
        slope=slope,
        branch_two=branch_two,
    )
    return result, kept


def backward(grad_out, kept, w, last=False, beside=None):
    grad_branch_two = (w["scale"][1] * grad_out).astype(bf16)
    grad_before = []
    grad_normed_two = 0.0
    if last:
        fc2_sent = swap(fc2_part(kept["activated"][1], grad_branch_two), "core")
    for up, down, slope in zip(w["fc1"], w["fc2"], kept["slope"]):
        part = jnp.concatenate([mm_t(grad_branch_two, d) for d in down], axis=1)
        part = (part * slope.astype(f32)).astype(bf16)
        grad_before.append(part)
        grad_normed_two = grad_normed_two + mm_t(part, up)
    if last:
        fc2 = fc2_part(kept["activated"][0], grad_branch_two, fc2_sent)
        fc2, grad_normed_two = lax.optimization_barrier((fc2, grad_normed_two))
        fc2 = lax.psum_scatter(fc2, RING_Z, scatter_dimension=0, tiled=True)
    normal_two, factor_two = normal_part(kept["middle"])
    grad_middle = grad_out + norm_back(grad_normed_two, normal_two, factor_two, w["gain"][1])
    grad_branch = (w["scale"][0] * grad_middle).astype(bf16)
    width = grad_branch.shape[1]
    half = width // 2
    grad_halves = flip_halves(w["core"], grad_branch)
    grad_halves = [grad_halves[:, :half], grad_halves[:, half:]]
    grad_attended = sum(mm_t(g, p) for g, p in zip(grad_halves, w["proj"])).astype(bf16)
    grad_attended = flip_halves(w["core"], grad_attended)
    fc_grad = None
    if last:
        fc1_sent = fc1_part(kept["normed_two"], grad_before[1])
        fc1_sent, grad_attended = lax.optimization_barrier((fc1_sent, grad_attended))
        fc1_sent = swap(fc1_sent, "core")
    grad_chunks = chunked([grad_attended[:, :half], grad_attended[:, half:]])
    q_chunks, kv_chunks = [], []
    ready = None
    for i in range(CHUNKS):
        g = grad_chunks[i]
        if ready is not None:
            own, sent = ready
            if last and fc_grad is None:
                fc1 = fc1_part(kept["normed_two"], grad_before[0], fc1_sent)
                sent, g, fc1 = lax.optimization_barrier((sent, g, fc1))
                fc1 = lax.psum_scatter(fc1, RING_Z, scatter_dimension=0, tiled=True)
                fc_grad = [fc1, fc2]
            else:
                sent, g = lax.optimization_barrier((sent, g))
            came = swap(sent, "yl")
        parts = attend_back(kept["queries"][i], kept["blocks"][i], g, kept["log_total"][i])
        if ready is not None:
            parts, came, beside = lax.optimization_barrier((parts, came, beside))
            kv_chunks.append((own + came.astype(f32)).astype(bf16))
        q_chunks.append(parts[0])
        ready = group_parts(*parts[1:])
    kv_chunks.append((ready[0] + swap(ready[1], "yl").astype(f32)).astype(bf16))
    grad_q, grad_kv = unchunked(q_chunks), unchunked(kv_chunks)
    grad_normed_one = sum(
        mm_t(g, part) for g, part in zip(grad_q + grad_kv, w["q"] + w["kv"])
    )
    normal_one, factor_one = normal_part(kept["inputs"])
    grad_inputs = grad_middle + norm_back(grad_normed_one, normal_one, factor_one, w["gain"][0])
    total = lambda a: jnp.sum(a.astype(f32), axis=0, keepdims=True)
    vectors = dict(
        gain=(total(grad_normed_one * normal_one), total(grad_normed_two * normal_two)),
        shift=(total(grad_normed_one), total(grad_normed_two)),
        out_bias=(total(grad_branch), total(grad_branch_two)),
        scale=(total(grad_middle * kept["branch"]), total(grad_out * kept["branch_two"])),
        q=[total(g) for g in grad_q],
        kv=[total(g) for g in grad_kv],
        fc1_bias=[total(g) for g in grad_before],
    )
    products = dict(
        q=(kept["normed_one"], grad_q),
        kv=(kept["normed_one"], grad_kv),
        proj=(kept["attended"], grad_halves),
        fc=fc_grad,
        beside=beside,
    )
    return grad_inputs.astype(bf16), vectors, products


def ordered(core, mine, other):
    return jnp.where(core == 0, mine, other), jnp.where(core == 0, other, mine)


def per_device(
    patch_tokens,
    out_grad,
    batch_counts,
    norm_gain,
    norm_bias,
    qkv_weight,
    qv_bias,
    proj_weight,
    fc1_weight,
    fc1_bias,
    fc2_weight,
    out_bias,
    layer_scale,
):
    section = lax.axis_index("section")
    core = lax.axis_index("core")
    shards = lax.axis_size(FSDP)
    images, rows, width = patch_tokens.shape
    half = width // 2
    own = width // shards
    hidden = fc2_weight.shape[1]
    mid = hidden // 2
    groups = half // PAIR
    pick = lambda a, i, axis: lax.dynamic_index_in_dim(a, i, axis, keepdims=False)

    part = mid // 2
    q, k, v = (qkv_weight[0][:, i * width : (i + 1) * width] for i in range(3))
    q_mine = pick(q.reshape(own, 2, half), core, 1)
    kv = jnp.stack([k.reshape(own, 2, groups, PAIR), v.reshape(own, 2, groups, PAIR)], axis=3)
    kv_mine = pick(kv, core, 1).reshape(own, width)
    proj_mine = pick(proj_weight[0].reshape(own, 2, half), core, 1)
    vectors = jnp.concatenate(
        [a[0] for a in (norm_gain, norm_bias, qv_bias, out_bias, layer_scale)]
        + [fc1_bias[0].reshape(hidden // own, own)],
        axis=0,
    ).T
    count = vectors.shape[1]
    vectors = jnp.pad(vectors, ((0, 0), (0, 128 - count)))
    fc1_mine = pick(fc1_weight[0].reshape(own, shards, 2, 2, part), core, 2)
    fc1_mine = jnp.swapaxes(fc1_mine, 1, 2).reshape(own, shards * mid)
    fc2_mine = pick(fc2_weight[0].reshape(2, 2, part, width), core, 0)
    fc_mine = jnp.concatenate([fc1_mine, fc2_mine[0], fc2_mine[1]], axis=1)
    fc_row = lax.all_gather(fc_mine, RING_Y, axis=0, tiled=True)

    mine = jnp.concatenate([kv_mine, q_mine, proj_mine, vectors], axis=1)
    live = (
        jnp.arange(images) % IMG_MB < jnp.repeat(batch_counts[0], IMG_MB)
    ).astype(bf16)
    live_grad = out_grad * live[:, None, None]
    hops = (*first_hop(mine, RING_Z), lax.ppermute(mine, RING_Z, ACROSS))
    hops, fc_row, live_grad, first_tokens = lax.optimization_barrier(
        (hops, fc_row, live_grad, to_images(patch_tokens))
    )
    fc_half = lax.all_gather(fc_row, RING_Z, axis=0, tiled=True)
    row = ring_place(mine, RING_Z, hops, [(4, *mine.shape)], in_order)[0]
    hops = lax.optimization_barrier(first_hop(row, RING_Y))
    more, first_tokens = lax.optimization_barrier(
        (second_hop(*hops, RING_Y), flip(first_tokens))
    )

    def views(outs, piece, place, start):
        for i in range(piece.shape[0]):
            at = 0
            for out in outs:
                size = out.shape[-1]
                out[start + i, place] = piece[i, :, at : at + size]
                at += size

    sizes = (width, half, half, 128)
    kv_half, q_half, proj_half, vectors = (
        o.reshape(width, -1)
        for o in ring_place(
            row, RING_Y, hops + more, [(4, 4, own, size) for size in sizes], views
        )
    )
    vectors = vectors[:, :16].T.astype(f32)

    def halves(row):
        return ordered(core, row[:, :half], row[:, half:])

    def fc1_bias_of(which):
        rows = jnp.where(which == 0, vectors[10:12], vectors[12:14])
        return jnp.concatenate([rows[0:1], rows[1:2]], axis=1)

    def kv_bias(v_half):
        zeros = jnp.zeros((1, PAIR), f32)
        cuts = [v_half[:, i * PAIR : (i + 1) * PAIR] for i in range(groups)]
        return jnp.concatenate([x for c in cuts for x in (zeros, c)], axis=1)

    wide = shards * mid
    w = dict(
        core=core,
        gain=(vectors[0:1], vectors[1:2]),
        shift=(vectors[2:3], vectors[3:4]),
        out_bias=(vectors[6:7], vectors[7:8]),
        scale=(vectors[8:9], vectors[9:10]),
        q=[q_half, swap(q_half, "core")],
        q_bias=halves(vectors[4:5]),
        kv=[kv_half, swap(kv_half, "core")],
        kv_bias=[kv_bias(b) for b in halves(vectors[5:6])],
        proj=(proj_half, swap(proj_half, "core")),
        fc1_bias=[fc1_bias_of(c) for c in (core, 1 - core)],
    )

    def fc_weights(gathered):
        pair = (gathered, swap(gathered, "core"))
        return dict(
            fc1=[f[:, :wide] for f in pair],
            fc2=[(f[:, wide : wide + width], f[:, wide + width :]) for f in pair],
        )


    sent, _ = forward(first_tokens, w, late=(fc_half, fc_weights))
    sent, live_grad = lax.optimization_barrier((sent, live_grad))
    passed = lax.ppermute(sent, "section", [(0, 1)])
    last_grad = flip(to_images(live_grad))
    tokens = jnp.where(section == 0, first_tokens, passed)
    result, kept = forward(tokens, w)

    sent, _, _ = backward(last_grad.astype(f32), kept, w)
    sent, result = lax.optimization_barrier((sent, result))
    passed = lax.ppermute(sent, "section", [(1, 0)])
    block_out = from_images(result, images)
    grad_out = jnp.where(section == 1, last_grad, passed).astype(f32)
    grad_inputs, sums, products = backward(grad_out, kept, w, True, block_out)

    vector_grads = vector_block(core, sums, width, PAIR)

    a1, dq = products["q"]
    dkv = products["kv"][1]
    o, e1 = products["proj"]
    make_a = lambda i, add=None: outer(
        [((a1, 0), dq[i], width), ((o, 0), e1[i], width)], half // 2, add=add
    )
    make_b = lambda i, add=None: outer([((a1, 0), dkv[i], width)], half // 2, add=add)
    a_full, b_full = (
        make(0, swap(make(1), "core")).reshape(4, 4, own, width) for make in (make_a, make_b)
    )
    (a_sum, b_sum), (rows, vector_grads, grad_inputs) = ring_sums(
        [(a_full, RING_Y, 1), (b_full, RING_Z, 0)],
        (products["fc"], vector_grads, grad_inputs),
    )
    in_grad = from_images(grad_inputs, images)
    block_out = products["beside"]
    fc_grad = lax.psum_scatter(
        jnp.concatenate(rows, axis=1), RING_Y, scatter_dimension=0, tiled=True
    )
    vector_grads = vector_grads.reshape(4, 4, own, PAIR)
    (vector_sum,), _ = direct_sums([(vector_grads, RING_Y, 1)])
    ab, in_grad = direct_sums(
        [(jnp.concatenate([a_sum, vector_sum], axis=2), RING_Z, 0), (b_sum, RING_Y, 0)],
        in_grad,
    )
    ab = jnp.concatenate([ab[0][:, :width], ab[1], ab[0][:, width:]], axis=1)

    def chips_sum(a):
        return (a.astype(f32) + swap(a, "xhi").astype(f32)).astype(bf16)

    ab = chips_sum(ab)
    ab_other = swap(ab, "core")
    qkv_out, proj_out = join_qkv(core, ab, ab_other, width)
    vec_grad = sum(p[:, 2 * width : 2 * width + count].astype(f32) for p in (ab, ab_other)).T
    fc_grad = chips_sum(fc_grad)
    fc1_out, fc2_out = join_fc(core, fc_grad, swap(fc_grad, "core"), width, shards)
    return (
        block_out[None],
        in_grad[None],
        vec_grad[0:2][None],
        vec_grad[2:4][None],
        qkv_out[None],
        vec_grad[4:6][None],
        proj_out[None],
        fc1_out[None],
        vec_grad[10:].reshape(1, hidden),
        fc2_out[None],
        vec_grad[6:8][None],
        vec_grad[8:10][None],
    )


def solution(mesh):
    sections, fsdp, rep = mesh.devices.shape
    inner = Mesh(
        mesh.devices.reshape(sections, fsdp // 4, 2, 2, rep // 2, 2),
        ("section",) + FSDP + REP,
    )
    weight = P("section", FSDP, None)
    vector = P("section", None, FSDP)
    tokens = P(REP, FSDP, None)
    both = P("section", REP, FSDP, None)
    return jax.shard_map(
        per_device,
        mesh=inner,
        in_specs=(
            tokens,
            tokens,
            P(REP, None),
            vector,
            vector,
            weight,
            vector,
            weight,
            weight,
            P("section", FSDP),
            weight,
            vector,
            vector,
        ),
        out_specs=(
            both,
            both,
            vector,
            vector,
            weight,
            vector,
            weight,
            weight,
            P("section", FSDP),
            weight,
            vector,
            vector,
        ),
        check_vma=False,
    )
```

```python
import jax
import jax.numpy as jnp
from jax import lax
from jax.experimental import pallas as pl
from jax.experimental.pallas import tpu as pltpu
from jax.sharding import Mesh, PartitionSpec as P

HEAD_DIM = 64
IMG_MB = 2
PAIR = 2 * HEAD_DIM
EPSILON = 1e-06

FSDP = ("z", "yh", "yl")
REP = ("xhi", "core")
bf16 = jnp.bfloat16
f32 = jnp.float32


def dot(a, b, dims):
    return lax.dot_general(a, b, (dims, ((), ())), preferred_element_type=f32)


def mm(a, b):
    return dot(a, b, ((1,), (0,)))


def mm_t(a, b):
    return dot(a, b, ((1,), (1,)))


def t_mm(a, b):
    return dot(a, b, ((0,), (0,)))


def swap(value, axis):
    return lax.ppermute(value, axis, [(0, 1), (1, 0)])


def attend_kernel(q_ref, own_ref, mate_ref, near_ref, far_ref, out_ref, log_ref):
    rows = q_ref.shape[0]
    both = [r[...] for r in (own_ref, mate_ref, near_ref, far_ref)]
    keys = jnp.concatenate([b[:, :PAIR] for b in both], axis=0)
    values = jnp.concatenate([b[:, PAIR:] for b in both], axis=0)
    queries = q_ref[...] * jnp.asarray(HEAD_DIM**-0.5, bf16)
    lane = lax.broadcasted_iota(jnp.int32, (rows, PAIR), 1)
    outs = []
    for head in range(2):
        mine = (lane >= head * HEAD_DIM) & (lane < (head + 1) * HEAD_DIM)
        picked = jnp.where(mine, queries, jnp.zeros_like(queries))
        scores = mm_t(keys, picked)
        top = jnp.max(scores, axis=0, keepdims=True)
        raised = jnp.exp(scores - top)
        total = jnp.sum(raised, axis=0, keepdims=True)
        out = t_mm(values, raised.astype(bf16))
        outs.append(out * (1.0 / total))
        log_ref[0, head : head + 1, :] = top + jnp.log(total)
    row = lax.broadcasted_iota(jnp.int32, (PAIR, rows), 0)
    joined = jnp.where(row < HEAD_DIM, outs[0], outs[1])
    out_ref[...] = joined.T.astype(bf16)


def attend_back_kernel(
    q_ref, own_ref, mate_ref, near_ref, far_ref, grad_ref, log_ref, dq_ref, *dkv_refs
):
    rows = q_ref.shape[0]
    both = [r[...] for r in (own_ref, mate_ref, near_ref, far_ref)]
    keys = jnp.concatenate([b[:, :PAIR] for b in both], axis=0)
    values = jnp.concatenate([b[:, PAIR:] for b in both], axis=0)
    queries = q_ref[...] * jnp.asarray(HEAD_DIM**-0.5, bf16)
    grads = grad_ref[...]
    lane = lax.broadcasted_iota(jnp.int32, (rows, PAIR), 1)
    dqs, dk, dv = [], None, None
    for head in range(2):
        mine = (lane >= head * HEAD_DIM) & (lane < (head + 1) * HEAD_DIM)
        picked = jnp.where(mine, queries, jnp.zeros_like(queries))
        grad = jnp.where(mine, grads, jnp.zeros_like(grads))
        scores = mm_t(keys, picked)
        weighting = jnp.exp(scores - log_ref[0, head : head + 1, :])
        grad_weighting = mm_t(values, grad)
        row_term = jnp.sum(grad_weighting * weighting, axis=0, keepdims=True)
        grad_scores = (weighting * (grad_weighting - row_term)).astype(bf16)
        dqs.append(t_mm(keys, grad_scores))
        k_part = mm(grad_scores, picked)
        v_part = mm(weighting.astype(bf16), grad)
        dk = k_part if dk is None else dk + k_part
        dv = v_part if dv is None else dv + v_part
    row = lax.broadcasted_iota(jnp.int32, (PAIR, rows), 0)
    joined = jnp.where(row < HEAD_DIM, dqs[0], dqs[1]) * (HEAD_DIM**-0.5)
    dq_ref[...] = joined.T.astype(bf16)
    for i, ref in enumerate(dkv_refs):
        ref[:, :PAIR] = dk[i * rows : (i + 1) * rows].astype(bf16)
        ref[:, PAIR:] = dv[i * rows : (i + 1) * rows].astype(bf16)


def pair_specs(rows, pairs):
    half = pairs // 2
    q_spec = pl.BlockSpec((rows, PAIR), lambda i: (0, i))
    kv_spec = pl.BlockSpec((rows, 2 * PAIR), lambda i: (0, i))
    kv_swapped = pl.BlockSpec((rows, 2 * PAIR), lambda i: (0, (i + half) % pairs))
    log_spec = pl.BlockSpec((1, 2, rows), lambda i: (i, 0, 0))
    return q_spec, [kv_spec, kv_swapped, kv_spec, kv_swapped], log_spec


def attend_cost(queries, blocks, products):
    rows, width = queries.shape
    scores = rows * rows * len(blocks) * width // HEAD_DIM
    return pl.CostEstimate(
        flops=products * scores * 2 * 256,
        bytes_accessed=2 * 2 * len(blocks) * rows * width * 2,
        transcendentals=scores,
    )


def attend(queries, blocks):
    rows, width = queries.shape
    pairs = width // PAIR
    q_spec, kv_specs, log_spec = pair_specs(rows, pairs)
    return pl.pallas_call(
        attend_kernel,
        grid=(pairs,),
        in_specs=[q_spec] + kv_specs,
        out_specs=[q_spec, log_spec],
        out_shape=[
            jax.ShapeDtypeStruct((rows, width), bf16),
            jax.ShapeDtypeStruct((pairs, 2, rows), f32),
        ],
        compiler_params=pltpu.CompilerParams(vmem_limit_bytes=40 * 2**20),
        cost_estimate=attend_cost(queries, blocks, 2),
        name="attend",
    )(queries, *blocks)


def attend_back(queries, blocks, grad, log_total):
    rows, width = queries.shape
    pairs = width // PAIR
    q_spec, kv_specs, log_spec = pair_specs(rows, pairs)
    return pl.pallas_call(
        attend_back_kernel,
        grid=(pairs,),
        in_specs=[q_spec] + kv_specs + [q_spec, log_spec],
        out_specs=[q_spec] + kv_specs,
        out_shape=[jax.ShapeDtypeStruct((rows, width), bf16)]
        + [jax.ShapeDtypeStruct((rows, 2 * width), bf16)] * 4,
        compiler_params=pltpu.CompilerParams(vmem_limit_bytes=40 * 2**20),
        cost_estimate=attend_cost(queries, blocks, 5),
        name="attend_back",
    )(queries, *blocks, grad, log_total)


def outer(segments, step, add=None, tail=None):
    rows = segments[0][1].shape[0]
    width = segments[0][2]
    counts = [right.shape[1] // step for _, right, _ in segments]
    starts = [sum(counts[:k]) for k in range(len(counts))]
    total = sum(counts)
    grid = total + (tail is not None)
    n = len(segments)

    def kernel(*refs):
        out_ref = refs[-1]
        i = pl.program_id(0)
        for k in range(n):

            @pl.when((i >= starts[k]) & (i < starts[k] + counts[k]))
            def _(k=k):
                value = t_mm(refs[2 * k][...], refs[2 * k + 1][...])
                if add is not None:
                    value = value + refs[2 * n][...].astype(f32)
                out_ref[...] = value.astype(bf16)

        if tail is not None:

            @pl.when(i == total)
            def _():
                out_ref[...] = refs[2 * n + (add is not None)][...]

    in_specs, operands = [], []
    for (left, right, _), start, count in zip(segments, starts, counts):
        array, which = left
        in_specs.append(pl.BlockSpec((rows, width), lambda i, w=which: (0, w)))
        in_specs.append(
            pl.BlockSpec((rows, step), lambda i, s=start, c=count: (0, jnp.clip(i - s, 0, c - 1)))
        )
        operands += [array, right]
    if add is not None:
        in_specs.append(pl.BlockSpec((width, step), lambda i: (0, jnp.minimum(i, total - 1))))
        operands.append(add)
    if tail is not None:
        in_specs.append(pl.BlockSpec((width, step), lambda i: (0, 0)))
        operands.append(tail)
    return pl.pallas_call(
        kernel,
        grid=(grid,),
        in_specs=in_specs,
        out_specs=pl.BlockSpec((width, step), lambda i: (0, i)),
        out_shape=jax.ShapeDtypeStruct((width, grid * step), bf16),
        compiler_params=pltpu.CompilerParams(vmem_limit_bytes=40 * 2**20),
        cost_estimate=pl.CostEstimate(
            flops=2 * rows * width * total * step,
            bytes_accessed=2 * width * grid * step * (1 if add is None else 2),
            transcendentals=0,
        ),
        name="outer",
    )(*operands)


def fc1_part(normed, grad_before, add=None):
    return outer([((normed, 0), grad_before, normed.shape[1])], 512, add=add)


def fc2_part(activated, grad_branch, add=None):
    width = grad_branch.shape[1]
    count = activated.shape[1] // width
    return outer([((activated, i), grad_branch, width) for i in range(count)], 512, add=add)


def join(kernel, core, inputs, shapes):
    vmem = pl.BlockSpec(memory_space=pltpu.VMEM)
    return pl.pallas_call(
        kernel,
        in_specs=[pl.BlockSpec(memory_space=pltpu.SMEM)] + [vmem] * len(inputs),
        out_specs=[vmem] * len(shapes),
        out_shape=[jax.ShapeDtypeStruct(shape, f32) for shape in shapes],
        compiler_params=pltpu.CompilerParams(vmem_limit_bytes=24 * 2**20),
        cost_estimate=pl.CostEstimate(
            flops=0, bytes_accessed=6 * sum(a.size for a in inputs), transcendentals=0
        ),
        name="join",
    )(core.reshape(1), *inputs)


def vector_block(core, sums, width, columns):
    half = width // 2
    whole = [*sums["gain"], *sums["shift"], *sums["out_bias"], *sums["scale"]]
    halves = [*sums["q"], *sums["kv"], *sums["fc1_bias"]]

    def kernel(core_ref, *refs):
        out_ref, rows_ref = refs[-2:]
        flag = core_ref[0]
        order = lambda a, b: (jnp.where(flag == 0, a, b), jnp.where(flag == 0, b, a))
        rows_ref[...] = jnp.zeros(rows_ref.shape, f32)
        for ref, row in zip(refs, (0, 1, 2, 3, 6, 7, 8, 9)):
            rows_ref[row : row + 1, :] = ref[...]
        q_mine, q_other, kv_mine, kv_other, fc_mine, fc_other = (
            r[...] for r in refs[len(whole) : len(whole) + len(halves)]
        )
        for i, value in enumerate(order(q_mine, q_other)):
            rows_ref[4:5, i * half : (i + 1) * half] = value
        for i, value in enumerate(order(kv_mine, kv_other)):
            for g in range(half // PAIR):
                at = i * half + g * PAIR
                rows_ref[5:6, at : at + PAIR] = value[:, (2 * g + 1) * PAIR : (2 * g + 2) * PAIR]
        for i, value in enumerate(order(fc_mine, fc_other)):
            for k in range(2):
                row = 10 + 2 * i + k
                rows_ref[row : row + 1, :] = value[:, k * width : (k + 1) * width]
        out_ref[...] = rows_ref[...].T.astype(bf16)

    vmem = pl.BlockSpec(memory_space=pltpu.VMEM)
    return pl.pallas_call(
        kernel,
        in_specs=[pl.BlockSpec(memory_space=pltpu.SMEM)] + [vmem] * len(whole + halves),
        out_specs=vmem,
        out_shape=jax.ShapeDtypeStruct((width, columns), bf16),
        scratch_shapes=[pltpu.VMEM((columns, width), f32)],
        name="vector_block",
    )(core.reshape(1), *whole, *halves)


def join_qkv(core, mine, other, width):
    rows, half = mine.shape[0], width // 2

    def kernel(core_ref, mine_ref, other_ref, qkv_ref, proj_ref):
        for ref, place in ((mine_ref, core_ref[0]), (other_ref, 1 - core_ref[0])):
            at = place * half
            columns = lambda start, size: pl.ds(pl.multiple_of(at + start, PAIR), size)
            qkv_ref[:, columns(0, half)] = ref[:, :half].astype(f32)
            proj_ref[:, columns(0, half)] = ref[:, half:width].astype(f32)
            for g in range(half // PAIR):
                k = width + 2 * g * PAIR
                for i in range(2):
                    qkv_ref[:, columns((i + 1) * width + g * PAIR, PAIR)] = ref[
                        :, k + i * PAIR : k + (i + 1) * PAIR
                    ].astype(f32)

    return join(kernel, core, [mine, other], [(rows, 3 * width), (rows, width)])


def join_fc(core, mine, other, width, shards):
    rows = mine.shape[0]
    wide = mine.shape[1] - 2 * width
    part = wide // (2 * shards)
    pair = 2 * part

    def kernel(core_ref, mine_ref, other_ref, fc1_ref, fc2_ref):
        for ref, place in ((mine_ref, core_ref[0]), (other_ref, 1 - core_ref[0])):
            for f in range(shards):
                at = pl.multiple_of(2 * pair * f + place * pair, pair)
                value = [
                    ref[:, i * shards * part + f * part : i * shards * part + (f + 1) * part]
                    for i in range(2)
                ]
                fc1_ref[:, pl.ds(at, pair)] = jnp.concatenate(value, axis=1).astype(f32)
            for i in range(2):
                at = pl.multiple_of(place * 2 * rows + i * rows, rows)
                fc2_ref[pl.ds(at, rows)] = ref[
                    :, wide + i * width : wide + (i + 1) * width
                ].astype(f32)

    return join(kernel, core, [mine, other], [(rows, 2 * wide), (4 * rows, width)])


FLIP = [(0, 0), (1, 2), (2, 1), (3, 3)]


def flip(tokens):
    return lax.ppermute(tokens, ("yh", "core"), FLIP)


def trade(tokens):
    return lax.all_to_all(tokens, "z", split_axis=0, concat_axis=0, tiled=True)


def as_image(tokens):
    return tokens.reshape(-1, tokens.shape[-1])


RING_Z, RING_Y = "z", ("yh", "yl")
AHEAD = [(i, (i + 1) % 4) for i in range(4)]
BACK = [(i, (i - 1) % 4) for i in range(4)]


ACROSS = [(i, (i + 2) % 4) for i in range(4)]


def first_hop(value, axis):
    return lax.ppermute(value, axis, AHEAD), lax.ppermute(value, axis, BACK)


def second_hop(ahead, back, axis):
    half = ahead.shape[0] // 2
    return (
        lax.ppermute(ahead[:half], axis, AHEAD),
        lax.ppermute(back[half:], axis, BACK),
    )


def ring_place(value, axis, hops, out_shapes, views):
    pieces = [(value, 0, 0), (hops[0], 3, 0), (hops[1], 1, 0), (hops[2], 2, 0)]
    if len(hops) > 3:
        pieces.append((hops[3], 2, hops[2].shape[0]))
    n_outs = len(out_shapes)

    def kernel(index_ref, *refs):
        sources, outs = refs[: len(pieces)], refs[len(pieces) :]
        for source, (_, step, start) in zip(sources, pieces):
            place = lax.rem(index_ref[0] + step, 4)
            views(outs, source, place, start)

    vmem = pl.BlockSpec(memory_space=pltpu.VMEM)
    return pl.pallas_call(
        kernel,
        in_specs=[pl.BlockSpec(memory_space=pltpu.SMEM)] + [vmem] * len(pieces),
        out_specs=[vmem] * n_outs,
        out_shape=[jax.ShapeDtypeStruct(shape, value.dtype) for shape in out_shapes],
        compiler_params=pltpu.CompilerParams(vmem_limit_bytes=24 * 2**20),
        cost_estimate=pl.CostEstimate(
            flops=0, bytes_accessed=16 * value.size, transcendentals=0
        ),
        name="ring_place",
    )(lax.axis_index(axis).reshape(1), *(p[0] for p in pieces))


def in_order(outs, piece, place, start):
    outs[0][place, pl.ds(start, piece.shape[0])] = piece[...]


def add(*parts):
    return sum(p.astype(f32) for p in parts).astype(bf16)


def ring_blocks(blocks, axis, dim):
    index = lax.axis_index(axis)
    return [
        lax.dynamic_index_in_dim(blocks, (index + k) % 4, dim, keepdims=False) for k in range(4)
    ]


def ring_sums(items, beside, tokens):
    blocks = [ring_blocks(*item) for item in items]
    hops = []
    for (_, axis, _), (_, _, far, _) in zip(items, blocks):
        half = far.shape[0] // 2
        hops.append(
            (lax.ppermute(far[:half], axis, AHEAD), lax.ppermute(far[half:], axis, BACK))
        )
    hops, beside, tokens = lax.optimization_barrier((hops, beside, tokens))
    ends = []
    for (_, axis, _), (own, after, _, before), (low, high) in zip(items, blocks, hops):
        half = low.shape[0]
        after = jnp.concatenate([add(after[:half], low), after[half:]])
        before = jnp.concatenate([before[:half], add(before[half:], high)])
        ends.append((own, lax.ppermute(after, axis, AHEAD), lax.ppermute(before, axis, BACK)))
    ends, traded = lax.optimization_barrier((ends, trade(tokens)))
    return [add(*e) for e in ends], beside, traded


def direct_sums(items, beside=None):
    ways = [(1, AHEAD), (3, BACK), (2, ACROSS)]
    parts = []
    for blocks, axis, dim in items:
        block = ring_blocks(blocks, axis, dim)
        parts.append([block[0]] + [lax.ppermute(block[k], axis, way) for k, way in ways])
    parts, beside = lax.optimization_barrier((parts, beside))
    return [add(*p) for p in parts], beside


def group_parts(own, mate, near, far):
    mate, far = swap(mate, "core"), swap(far, "core")
    sent = (near.astype(f32) + far.astype(f32)).astype(bf16)
    return own.astype(f32) + mate.astype(f32), sent


def normal_part(values):
    mean = jnp.mean(values, axis=-1, keepdims=True)
    centred = values - mean
    factor = lax.rsqrt(jnp.mean(centred * centred, axis=-1, keepdims=True) + EPSILON)
    return centred * factor, factor


def norm_back(grad, normal, factor, gain):
    e = grad * gain
    inner = jnp.mean(e * normal, axis=-1, keepdims=True)
    return factor * (e - jnp.mean(e, axis=-1, keepdims=True) - normal * inner)


def flip_halves(core, value):
    half = value.shape[-1] // 2
    turned = jnp.concatenate([value[..., half:], value[..., :half]], axis=-1)
    return jnp.where(core == 0, value, turned)


CHUNKS = 2


def chunked(halves):
    size = halves[0].shape[1] // CHUNKS
    cut = lambda h, i: h[:, i * size : (i + 1) * size]
    return [jnp.concatenate([cut(h, i) for h in halves], axis=1) for i in range(CHUNKS)]


def unchunked(chunks):
    size = chunks[0].shape[1] // 2
    return [
        jnp.concatenate([c[:, i * size : (i + 1) * size] for c in chunks], axis=1)
        for i in range(2)
    ]


def forward(tokens, w, late=None):
    inputs = tokens.astype(f32)
    normed_one = (normal_part(inputs)[0] * w["gain"][0] + w["shift"][0]).astype(bf16)
    project = lambda name: [
        (mm(normed_one, part) + bias).astype(bf16) for part, bias in zip(w[name], w[name + "_bias"])
    ]
    key_value = chunked(project("kv"))
    queries = chunked(project("q"))
    mate, near = swap(key_value[0], "core"), swap(key_value[0], "yl")
    blocks, results = [], []
    for i, own in enumerate(key_value):
        blocks.append((own, mate, near, swap(near, "core")))
        if i + 1 < CHUNKS:
            following, near = lax.optimization_barrier((key_value[i + 1], near))
            mate, near = swap(following, "core"), swap(following, "yl")
            result = attend(queries[i], blocks[i])
            result, near, mate = lax.optimization_barrier((result, near, mate))
        else:
            if late is not None:
                blocks[i], gathered = lax.optimization_barrier((blocks[i], late[0]))
                w.update(late[1](gathered))
            result = attend(queries[i], blocks[i])
        results.append(result)
    attended, log_total = zip(*results)
    attended = jnp.concatenate(unchunked(attended), axis=1)
    attended = flip_halves(w["core"], attended)
    branch = flip_halves(w["core"], jnp.concatenate([mm(attended, p) for p in w["proj"]], axis=1))
    branch = branch + w["out_bias"][0]
    middle = inputs + w["scale"][0] * branch
    normed_two = (normal_part(middle)[0] * w["gain"][1] + w["shift"][1]).astype(bf16)
    activated, slope, branch_two = [], [], w["out_bias"][1]
    for up, bias, down in zip(w["fc1"], w["fc1_bias"], w["fc2"]):
        before = mm(normed_two, up) + bias
        phi = 0.5 * (1.0 + lax.erf(before * (0.5**0.5)))
        density = jnp.exp(-0.5 * before * before) * 0.3989422804014327
        active = (before * phi).astype(bf16)
        activated.append(active)
        slope.append((phi + before * density).astype(bf16))
        for i, part in enumerate(down):
            rows = part.shape[0]
            branch_two = branch_two + mm(active[:, i * rows : (i + 1) * rows], part)
    result = (middle + w["scale"][1] * branch_two).astype(bf16)
    kept = dict(
        inputs=inputs,
        normed_one=normed_one,
        queries=queries,
        blocks=blocks,
        attended=attended,
        log_total=log_total,
        branch=branch,
        middle=middle,
        normed_two=normed_two,
        activated=activated,
        slope=slope,
        branch_two=branch_two,
    )
    return result, kept


def backward(grad_out, kept, w, last=False, result=None):
    grad_branch_two = (w["scale"][1] * grad_out).astype(bf16)
    grad_before = []
    grad_normed_two = 0.0
    if last:
        fc2_sent = swap(fc2_part(kept["activated"][1], grad_branch_two), "core")
    for up, down, slope in zip(w["fc1"], w["fc2"], kept["slope"]):
        part = jnp.concatenate([mm_t(grad_branch_two, d) for d in down], axis=1)
        part = (part * slope.astype(f32)).astype(bf16)
        grad_before.append(part)
        grad_normed_two = grad_normed_two + mm_t(part, up)
    if last:
        fc2 = fc2_part(kept["activated"][0], grad_branch_two, fc2_sent)
        fc2, grad_normed_two = lax.optimization_barrier((fc2, grad_normed_two))
        fc2 = lax.psum_scatter(fc2, RING_Z, scatter_dimension=0, tiled=True)
    normal_two, factor_two = normal_part(kept["middle"])
    grad_middle = grad_out + norm_back(grad_normed_two, normal_two, factor_two, w["gain"][1])
    grad_branch = (w["scale"][0] * grad_middle).astype(bf16)
    width = grad_branch.shape[1]
    half = width // 2
    grad_halves = flip_halves(w["core"], grad_branch)
    grad_halves = [grad_halves[:, :half], grad_halves[:, half:]]
    grad_attended = sum(mm_t(g, p) for g, p in zip(grad_halves, w["proj"])).astype(bf16)
    grad_attended = flip_halves(w["core"], grad_attended)
    fc_grad = None
    if last:
        fc1_sent = fc1_part(kept["normed_two"], grad_before[1])
        fc1_sent, grad_attended = lax.optimization_barrier((fc1_sent, grad_attended))
        fc1_sent = swap(fc1_sent, "core")
    grad_chunks = chunked([grad_attended[:, :half], grad_attended[:, half:]])
    q_chunks, kv_chunks = [], []
    ready = None
    for i in range(CHUNKS):
        g = grad_chunks[i]
        if ready is not None:
            own, sent = ready
            if last and fc_grad is None:
                fc1 = fc1_part(kept["normed_two"], grad_before[0], fc1_sent)
                sent, g, fc1 = lax.optimization_barrier((sent, g, fc1))
                fc1 = lax.psum_scatter(fc1, RING_Z, scatter_dimension=0, tiled=True)
                fc_grad = [fc1, fc2]
            else:
                sent, g = lax.optimization_barrier((sent, g))
            came = swap(sent, "yl")
        parts = attend_back(kept["queries"][i], kept["blocks"][i], g, kept["log_total"][i])
        if ready is not None:
            parts, came = lax.optimization_barrier((parts, came))
            kv_chunks.append((own + came.astype(f32)).astype(bf16))
        q_chunks.append(parts[0])
        ready = group_parts(*parts[1:])
    own, sent = ready
    traded = None
    if result is not None:
        sent, result = lax.optimization_barrier((sent, result))
        traded = trade(result)
    came, traded = lax.optimization_barrier((swap(sent, "yl"), traded))
    kv_chunks.append((own + came.astype(f32)).astype(bf16))
    grad_q, grad_kv = unchunked(q_chunks), unchunked(kv_chunks)
    grad_normed_one = sum(
        mm_t(g, part) for g, part in zip(grad_q + grad_kv, w["q"] + w["kv"])
    )
    normal_one, factor_one = normal_part(kept["inputs"])
    grad_inputs = grad_middle + norm_back(grad_normed_one, normal_one, factor_one, w["gain"][0])
    total = lambda a: jnp.sum(a.astype(f32), axis=0, keepdims=True)
    vectors = dict(
        gain=(total(grad_normed_one * normal_one), total(grad_normed_two * normal_two)),
        shift=(total(grad_normed_one), total(grad_normed_two)),
        out_bias=(total(grad_branch), total(grad_branch_two)),
        scale=(total(grad_middle * kept["branch"]), total(grad_out * kept["branch_two"])),
        q=[total(g) for g in grad_q],
        kv=[total(g) for g in grad_kv],
        fc1_bias=[total(g) for g in grad_before],
    )
    products = dict(
        q=(kept["normed_one"], grad_q),
        kv=(kept["normed_one"], grad_kv),
        proj=(kept["attended"], grad_halves),
        fc=fc_grad,
        traded=traded,
    )
    return grad_inputs.astype(bf16), vectors, products


def ordered(core, mine, other):
    return jnp.where(core == 0, mine, other), jnp.where(core == 0, other, mine)


def per_device(
    patch_tokens,
    out_grad,
    batch_counts,
    norm_gain,
    norm_bias,
    qkv_weight,
    qv_bias,
    proj_weight,
    fc1_weight,
    fc1_bias,
    fc2_weight,
    out_bias,
    layer_scale,
):
    section = lax.axis_index("section")
    core = lax.axis_index("core")
    shards = lax.axis_size(FSDP)
    images, rows, width = patch_tokens.shape
    half = width // 2
    own = width // shards
    hidden = fc2_weight.shape[1]
    mid = hidden // 2
    groups = half // PAIR
    pick = lambda a, i, axis: lax.dynamic_index_in_dim(a, i, axis, keepdims=False)

    part = mid // 2
    q, k, v = (qkv_weight[0][:, i * width : (i + 1) * width] for i in range(3))
    q_mine = pick(q.reshape(own, 2, half), core, 1)
    kv = jnp.stack([k.reshape(own, 2, groups, PAIR), v.reshape(own, 2, groups, PAIR)], axis=3)
    kv_mine = pick(kv, core, 1).reshape(own, width)
    proj_mine = pick(proj_weight[0].reshape(own, 2, half), core, 1)
    vectors = jnp.concatenate(
        [a[0] for a in (norm_gain, norm_bias, qv_bias, out_bias, layer_scale)]
        + [fc1_bias[0].reshape(hidden // own, own)],
        axis=0,
    ).T
    count = vectors.shape[1]
    vectors = jnp.pad(vectors, ((0, 0), (0, 128 - count)))
    fc1_mine = pick(fc1_weight[0].reshape(own, shards, 2, 2, part), core, 2)
    fc1_mine = jnp.swapaxes(fc1_mine, 1, 2).reshape(own, shards * mid)
    fc2_mine = pick(fc2_weight[0].reshape(2, 2, part, width), core, 0)
    fc_mine = jnp.concatenate([fc1_mine, fc2_mine[0], fc2_mine[1]], axis=1)
    fc_row = lax.all_gather(fc_mine, RING_Y, axis=0, tiled=True)

    mine = jnp.concatenate([kv_mine, q_mine, proj_mine, vectors], axis=1)
    live = (
        jnp.arange(images) % IMG_MB < jnp.repeat(batch_counts[0], IMG_MB)
    ).astype(bf16)
    live_grad = out_grad * live[:, None, None]
    hops = (*first_hop(mine, RING_Z), lax.ppermute(mine, RING_Z, ACROSS))
    hops, fc_row, live_grad, first_tokens = lax.optimization_barrier(
        (hops, fc_row, live_grad, as_image(trade(flip(patch_tokens))))
    )
    fc_half = lax.all_gather(fc_row, RING_Z, axis=0, tiled=True)
    row = ring_place(mine, RING_Z, hops, [(4, *mine.shape)], in_order)[0]
    hops = lax.optimization_barrier(first_hop(row, RING_Y))
    more = lax.optimization_barrier(second_hop(*hops, RING_Y))

    def views(outs, piece, place, start):
        for i in range(piece.shape[0]):
            at = 0
            for out in outs:
                size = out.shape[-1]
                out[start + i, place] = piece[i, :, at : at + size]
                at += size

    sizes = (width, half, half, 128)
    kv_half, q_half, proj_half, vectors = (
        o.reshape(width, -1)
        for o in ring_place(
            row, RING_Y, hops + more, [(4, 4, own, size) for size in sizes], views
        )
    )
    vectors = vectors[:, :16].T.astype(f32)

    def halves(row):
        return ordered(core, row[:, :half], row[:, half:])

    def fc1_bias_of(which):
        rows = jnp.where(which == 0, vectors[10:12], vectors[12:14])
        return jnp.concatenate([rows[0:1], rows[1:2]], axis=1)

    def kv_bias(v_half):
        zeros = jnp.zeros((1, PAIR), f32)
        cuts = [v_half[:, i * PAIR : (i + 1) * PAIR] for i in range(groups)]
        return jnp.concatenate([x for c in cuts for x in (zeros, c)], axis=1)

    wide = shards * mid
    w = dict(
        core=core,
        gain=(vectors[0:1], vectors[1:2]),
        shift=(vectors[2:3], vectors[3:4]),
        out_bias=(vectors[6:7], vectors[7:8]),
        scale=(vectors[8:9], vectors[9:10]),
        q=[q_half, swap(q_half, "core")],
        q_bias=halves(vectors[4:5]),
        kv=[kv_half, swap(kv_half, "core")],
        kv_bias=[kv_bias(b) for b in halves(vectors[5:6])],
        proj=(proj_half, swap(proj_half, "core")),
        fc1_bias=[fc1_bias_of(c) for c in (core, 1 - core)],
    )

    def fc_weights(gathered):
        pair = (gathered, swap(gathered, "core"))
        return dict(
            fc1=[f[:, :wide] for f in pair],
            fc2=[(f[:, wide : wide + width], f[:, wide + width :]) for f in pair],
        )


    sent, _ = forward(first_tokens, w, late=(fc_half, fc_weights))
    sent, live_grad = lax.optimization_barrier((sent, live_grad))
    passed = lax.ppermute(sent, "section", [(0, 1)])
    last_grad = as_image(flip(trade(live_grad)))
    tokens = jnp.where(section == 0, first_tokens, passed)
    result, kept = forward(tokens, w)

    slots = (images, result.shape[0] // images, width)
    sent, _, early = backward(last_grad.astype(f32), kept, w, result=result.reshape(slots))
    sent, traded = lax.optimization_barrier((sent, early["traded"]))
    passed, block_out = lax.optimization_barrier(
        (lax.ppermute(sent, "section", [(1, 0)]), flip(traded))
    )
    grad_out = jnp.where(section == 1, last_grad, passed).astype(f32)
    grad_inputs, sums, products = backward(grad_out, kept, w, last=True)

    vector_grads = vector_block(core, sums, width, PAIR)

    a1, dq = products["q"]
    dkv = products["kv"][1]
    o, e1 = products["proj"]
    make_a = lambda i, add=None: outer(
        [((a1, 0), dq[i], width), ((o, 0), e1[i], width)], half // 2, add=add
    )
    make_b = lambda i, add=None: outer([((a1, 0), dkv[i], width)], half // 2, add=add)
    a_full, b_full = (make(0, swap(make(1), "core")) for make in (make_a, make_b))
    a_full = jnp.concatenate([a_full, vector_grads], axis=1).reshape(4, 4, own, width + PAIR)
    (a_sum, b_sum), rows, traded = ring_sums(
        [(a_full, RING_Y, 1), (b_full.reshape(4, 4, own, width), RING_Z, 0)],
        products["fc"],
        grad_inputs.reshape(slots),
    )
    fc_grad = lax.psum_scatter(
        jnp.concatenate(rows, axis=1), RING_Y, scatter_dimension=0, tiled=True
    )
    ab, in_grad = direct_sums([(a_sum, RING_Z, 0), (b_sum, RING_Y, 0)], flip(traded))
    ab = jnp.concatenate([ab[0][:, :width], ab[1], ab[0][:, width:]], axis=1)

    def chips_sum(a):
        return (a.astype(f32) + swap(a, "xhi").astype(f32)).astype(bf16)

    ab = chips_sum(ab)
    ab_other = swap(ab, "core")
    qkv_out, proj_out = join_qkv(core, ab, ab_other, width)
    vec_grad = sum(p[:, 2 * width : 2 * width + count].astype(f32) for p in (ab, ab_other)).T
    fc_grad = chips_sum(fc_grad)
    fc1_out, fc2_out = join_fc(core, fc_grad, swap(fc_grad, "core"), width, shards)
    return (
        block_out[None],
        in_grad[None],
        vec_grad[0:2][None],
        vec_grad[2:4][None],
        qkv_out[None],
        vec_grad[4:6][None],
        proj_out[None],
        fc1_out[None],
        vec_grad[10:].reshape(1, hidden),
        fc2_out[None],
        vec_grad[6:8][None],
        vec_grad[8:10][None],
    )


def solution(mesh):
    sections, fsdp, rep = mesh.devices.shape
    inner = Mesh(
        mesh.devices.reshape(sections, fsdp // 4, 2, 2, rep // 2, 2),
        ("section",) + FSDP + REP,
    )
    weight = P("section", FSDP, None)
    vector = P("section", None, FSDP)
    tokens = P(REP, FSDP, None)
    both = P("section", REP, FSDP, None)
    return jax.shard_map(
        per_device,
        mesh=inner,
        in_specs=(
            tokens,
            tokens,
            P(REP, None),
            vector,
            vector,
            weight,
            vector,
            weight,
            weight,
            P("section", FSDP),
            weight,
            vector,
            vector,
        ),
        out_specs=(
            both,
            both,
            vector,
            vector,
            weight,
            vector,
            weight,
            weight,
            P("section", FSDP),
            weight,
            vector,
            vector,
        ),
        check_vma=False,
    )
```

```python
import jax
import jax.numpy as jnp
from jax import lax
from jax.experimental import pallas as pl
from jax.experimental.pallas import tpu as pltpu
from jax.sharding import Mesh, PartitionSpec as P

HEAD_DIM = 64
IMG_MB = 2
PAIR = 2 * HEAD_DIM
EPSILON = 1e-06

FSDP = ("z", "yh", "yl")
REP = ("xhi", "core")
bf16 = jnp.bfloat16
f32 = jnp.float32


def dot(a, b, dims):
    return lax.dot_general(a, b, (dims, ((), ())), preferred_element_type=f32)


def mm(a, b):
    return dot(a, b, ((1,), (0,)))


def mm_t(a, b):
    return dot(a, b, ((1,), (1,)))


def t_mm(a, b):
    return dot(a, b, ((0,), (0,)))


def swap(value, axis):
    return lax.ppermute(value, axis, [(0, 1), (1, 0)])


def attend_kernel(q_ref, own_ref, mate_ref, near_ref, far_ref, out_ref, log_ref):
    rows = q_ref.shape[0]
    both = [r[...] for r in (own_ref, mate_ref, near_ref, far_ref)]
    keys = jnp.concatenate([b[:, :PAIR] for b in both], axis=0)
    values = jnp.concatenate([b[:, PAIR:] for b in both], axis=0)
    queries = q_ref[...] * jnp.asarray(HEAD_DIM**-0.5, bf16)
    lane = lax.broadcasted_iota(jnp.int32, (rows, PAIR), 1)
    outs = []
    for head in range(2):
        mine = (lane >= head * HEAD_DIM) & (lane < (head + 1) * HEAD_DIM)
        picked = jnp.where(mine, queries, jnp.zeros_like(queries))
        scores = mm_t(keys, picked)
        top = jnp.max(scores, axis=0, keepdims=True)
        raised = jnp.exp(scores - top)
        total = jnp.sum(raised, axis=0, keepdims=True)
        out = t_mm(values, raised.astype(bf16))
        outs.append(out * (1.0 / total))
        log_ref[0, head : head + 1, :] = top + jnp.log(total)
    row = lax.broadcasted_iota(jnp.int32, (PAIR, rows), 0)
    joined = jnp.where(row < HEAD_DIM, outs[0], outs[1])
    out_ref[...] = joined.T.astype(bf16)


def attend_back_kernel(
    q_ref, own_ref, mate_ref, near_ref, far_ref, grad_ref, log_ref, dq_ref, *dkv_refs
):
    rows = q_ref.shape[0]
    both = [r[...] for r in (own_ref, mate_ref, near_ref, far_ref)]
    keys = jnp.concatenate([b[:, :PAIR] for b in both], axis=0)
    values = jnp.concatenate([b[:, PAIR:] for b in both], axis=0)
    queries = q_ref[...] * jnp.asarray(HEAD_DIM**-0.5, bf16)
    grads = grad_ref[...]
    lane = lax.broadcasted_iota(jnp.int32, (rows, PAIR), 1)
    dqs, dk, dv = [], None, None
    for head in range(2):
        mine = (lane >= head * HEAD_DIM) & (lane < (head + 1) * HEAD_DIM)
        picked = jnp.where(mine, queries, jnp.zeros_like(queries))
        grad = jnp.where(mine, grads, jnp.zeros_like(grads))
        scores = mm_t(keys, picked)
        weighting = jnp.exp(scores - log_ref[0, head : head + 1, :])
        grad_weighting = mm_t(values, grad)
        row_term = jnp.sum(grad_weighting * weighting, axis=0, keepdims=True)
        grad_scores = (weighting * (grad_weighting - row_term)).astype(bf16)
        dqs.append(t_mm(keys, grad_scores))
        k_part = mm(grad_scores, picked)
        v_part = mm(weighting.astype(bf16), grad)
        dk = k_part if dk is None else dk + k_part
        dv = v_part if dv is None else dv + v_part
    row = lax.broadcasted_iota(jnp.int32, (PAIR, rows), 0)
    joined = jnp.where(row < HEAD_DIM, dqs[0], dqs[1]) * (HEAD_DIM**-0.5)
    dq_ref[...] = joined.T.astype(bf16)
    for i, ref in enumerate(dkv_refs):
        ref[:, :PAIR] = dk[i * rows : (i + 1) * rows].astype(bf16)
        ref[:, PAIR:] = dv[i * rows : (i + 1) * rows].astype(bf16)


def pair_specs(rows, pairs):
    half = pairs // 2
    q_spec = pl.BlockSpec((rows, PAIR), lambda i: (0, i))
    kv_spec = pl.BlockSpec((rows, 2 * PAIR), lambda i: (0, i))
    kv_swapped = pl.BlockSpec((rows, 2 * PAIR), lambda i: (0, (i + half) % pairs))
    log_spec = pl.BlockSpec((1, 2, rows), lambda i: (i, 0, 0))
    return q_spec, [kv_spec, kv_swapped, kv_spec, kv_swapped], log_spec


def attend_cost(queries, blocks, products):
    rows, width = queries.shape
    scores = rows * rows * len(blocks) * width // HEAD_DIM
    return pl.CostEstimate(
        flops=products * scores * 2 * 256,
        bytes_accessed=2 * 2 * len(blocks) * rows * width * 2,
        transcendentals=scores,
    )


def attend(queries, blocks):
    rows, width = queries.shape
    pairs = width // PAIR
    q_spec, kv_specs, log_spec = pair_specs(rows, pairs)
    return pl.pallas_call(
        attend_kernel,
        grid=(pairs,),
        in_specs=[q_spec] + kv_specs,
        out_specs=[q_spec, log_spec],
        out_shape=[
            jax.ShapeDtypeStruct((rows, width), bf16),
            jax.ShapeDtypeStruct((pairs, 2, rows), f32),
        ],
        compiler_params=pltpu.CompilerParams(vmem_limit_bytes=40 * 2**20),
        cost_estimate=attend_cost(queries, blocks, 2),
        name="attend",
    )(queries, *blocks)


def attend_back(queries, blocks, grad, log_total):
    rows, width = queries.shape
    pairs = width // PAIR
    q_spec, kv_specs, log_spec = pair_specs(rows, pairs)
    return pl.pallas_call(
        attend_back_kernel,
        grid=(pairs,),
        in_specs=[q_spec] + kv_specs + [q_spec, log_spec],
        out_specs=[q_spec] + kv_specs,
        out_shape=[jax.ShapeDtypeStruct((rows, width), bf16)]
        + [jax.ShapeDtypeStruct((rows, 2 * width), bf16)] * 4,
        compiler_params=pltpu.CompilerParams(vmem_limit_bytes=40 * 2**20),
        cost_estimate=attend_cost(queries, blocks, 5),
        name="attend_back",
    )(queries, *blocks, grad, log_total)


def outer(segments, step, add=None, tail=None):
    rows = segments[0][1].shape[0]
    width = segments[0][2]
    counts = [right.shape[1] // step for _, right, _ in segments]
    starts = [sum(counts[:k]) for k in range(len(counts))]
    total = sum(counts)
    grid = total + (tail is not None)
    n = len(segments)

    def kernel(*refs):
        out_ref = refs[-1]
        i = pl.program_id(0)
        for k in range(n):

            @pl.when((i >= starts[k]) & (i < starts[k] + counts[k]))
            def _(k=k):
                value = t_mm(refs[2 * k][...], refs[2 * k + 1][...])
                if add is not None:
                    value = value + refs[2 * n][...].astype(f32)
                out_ref[...] = value.astype(bf16)

        if tail is not None:

            @pl.when(i == total)
            def _():
                out_ref[...] = refs[2 * n + (add is not None)][...]

    in_specs, operands = [], []
    for (left, right, _), start, count in zip(segments, starts, counts):
        array, which = left
        in_specs.append(pl.BlockSpec((rows, width), lambda i, w=which: (0, w)))
        in_specs.append(
            pl.BlockSpec((rows, step), lambda i, s=start, c=count: (0, jnp.clip(i - s, 0, c - 1)))
        )
        operands += [array, right]
    if add is not None:
        in_specs.append(pl.BlockSpec((width, step), lambda i: (0, jnp.minimum(i, total - 1))))
        operands.append(add)
    if tail is not None:
        in_specs.append(pl.BlockSpec((width, step), lambda i: (0, 0)))
        operands.append(tail)
    return pl.pallas_call(
        kernel,
        grid=(grid,),
        in_specs=in_specs,
        out_specs=pl.BlockSpec((width, step), lambda i: (0, i)),
        out_shape=jax.ShapeDtypeStruct((width, grid * step), bf16),
        compiler_params=pltpu.CompilerParams(vmem_limit_bytes=40 * 2**20),
        cost_estimate=pl.CostEstimate(
            flops=2 * rows * width * total * step,
            bytes_accessed=2 * width * grid * step * (1 if add is None else 2),
            transcendentals=0,
        ),
        name="outer",
    )(*operands)


def fc1_part(normed, grad_before, add=None):
    return outer([((normed, 0), grad_before, normed.shape[1])], 512, add=add)


def fc2_part(activated, grad_branch, add=None):
    width = grad_branch.shape[1]
    count = activated.shape[1] // width
    return outer([((activated, i), grad_branch, width) for i in range(count)], 512, add=add)


def join(kernel, core, inputs, shapes):
    vmem = pl.BlockSpec(memory_space=pltpu.VMEM)
    return pl.pallas_call(
        kernel,
        in_specs=[pl.BlockSpec(memory_space=pltpu.SMEM)] + [vmem] * len(inputs),
        out_specs=[vmem] * len(shapes),
        out_shape=[jax.ShapeDtypeStruct(shape, f32) for shape in shapes],
        compiler_params=pltpu.CompilerParams(vmem_limit_bytes=24 * 2**20),
        cost_estimate=pl.CostEstimate(
            flops=0, bytes_accessed=6 * sum(a.size for a in inputs), transcendentals=0
        ),
        name="join",
    )(core.reshape(1), *inputs)


def vector_block(core, sums, width, columns):
    half = width // 2
    whole = [*sums["gain"], *sums["shift"], *sums["out_bias"], *sums["scale"]]
    halves = [*sums["q"], *sums["kv"], *sums["fc1_bias"]]

    def kernel(core_ref, *refs):
        out_ref, rows_ref = refs[-2:]
        flag = core_ref[0]
        order = lambda a, b: (jnp.where(flag == 0, a, b), jnp.where(flag == 0, b, a))
        rows_ref[...] = jnp.zeros(rows_ref.shape, f32)
        for ref, row in zip(refs, (0, 1, 2, 3, 6, 7, 8, 9)):
            rows_ref[row : row + 1, :] = ref[...]
        q_mine, q_other, kv_mine, kv_other, fc_mine, fc_other = (
            r[...] for r in refs[len(whole) : len(whole) + len(halves)]
        )
        for i, value in enumerate(order(q_mine, q_other)):
            rows_ref[4:5, i * half : (i + 1) * half] = value
        for i, value in enumerate(order(kv_mine, kv_other)):
            for g in range(half // PAIR):
                at = i * half + g * PAIR
                rows_ref[5:6, at : at + PAIR] = value[:, (2 * g + 1) * PAIR : (2 * g + 2) * PAIR]
        for i, value in enumerate(order(fc_mine, fc_other)):
            for k in range(2):
                row = 10 + 2 * i + k
                rows_ref[row : row + 1, :] = value[:, k * width : (k + 1) * width]
        out_ref[...] = rows_ref[...].T.astype(bf16)

    vmem = pl.BlockSpec(memory_space=pltpu.VMEM)
    return pl.pallas_call(
        kernel,
        in_specs=[pl.BlockSpec(memory_space=pltpu.SMEM)] + [vmem] * len(whole + halves),
        out_specs=vmem,
        out_shape=jax.ShapeDtypeStruct((width, columns), bf16),
        scratch_shapes=[pltpu.VMEM((columns, width), f32)],
        name="vector_block",
    )(core.reshape(1), *whole, *halves)


def join_qkv(core, mine, other, width):
    rows, half = mine.shape[0], width // 2

    def kernel(core_ref, mine_ref, other_ref, qkv_ref, proj_ref):
        for ref, place in ((mine_ref, core_ref[0]), (other_ref, 1 - core_ref[0])):
            at = place * half
            columns = lambda start, size: pl.ds(pl.multiple_of(at + start, PAIR), size)
            qkv_ref[:, columns(0, half)] = ref[:, :half].astype(f32)
            proj_ref[:, columns(0, half)] = ref[:, half:width].astype(f32)
            for g in range(half // PAIR):
                k = width + 2 * g * PAIR
                for i in range(2):
                    qkv_ref[:, columns((i + 1) * width + g * PAIR, PAIR)] = ref[
                        :, k + i * PAIR : k + (i + 1) * PAIR
                    ].astype(f32)

    return join(kernel, core, [mine, other], [(rows, 3 * width), (rows, width)])


def join_fc(core, mine, other, width, shards):
    rows = mine.shape[0]
    wide = mine.shape[1] - 2 * width
    part = wide // (2 * shards)
    pair = 2 * part

    def kernel(core_ref, mine_ref, other_ref, fc1_ref, fc2_ref):
        for ref, place in ((mine_ref, core_ref[0]), (other_ref, 1 - core_ref[0])):
            for f in range(shards):
                at = pl.multiple_of(2 * pair * f + place * pair, pair)
                value = [
                    ref[:, i * shards * part + f * part : i * shards * part + (f + 1) * part]
                    for i in range(2)
                ]
                fc1_ref[:, pl.ds(at, pair)] = jnp.concatenate(value, axis=1).astype(f32)
            for i in range(2):
                at = pl.multiple_of(place * 2 * rows + i * rows, rows)
                fc2_ref[pl.ds(at, rows)] = ref[
                    :, wide + i * width : wide + (i + 1) * width
                ].astype(f32)

    return join(kernel, core, [mine, other], [(rows, 2 * wide), (4 * rows, width)])


FLIP = [(0, 0), (1, 2), (2, 1), (3, 3)]


def flip(tokens):
    return lax.ppermute(tokens, ("yh", "core"), FLIP)


def trade(tokens):
    return lax.all_to_all(tokens, "z", split_axis=0, concat_axis=0, tiled=True)


def as_image(tokens):
    return tokens.reshape(-1, tokens.shape[-1])


RING_Z, RING_Y = "z", ("yh", "yl")
AHEAD = [(i, (i + 1) % 4) for i in range(4)]
BACK = [(i, (i - 1) % 4) for i in range(4)]


ACROSS = [(i, (i + 2) % 4) for i in range(4)]


def first_hop(value, axis):
    return lax.ppermute(value, axis, AHEAD), lax.ppermute(value, axis, BACK)


def second_hop(ahead, back, axis):
    half = ahead.shape[0] // 2
    return (
        lax.ppermute(ahead[:half], axis, AHEAD),
        lax.ppermute(back[half:], axis, BACK),
    )


def ring_place(value, axis, hops, out_shapes, views):
    pieces = [(value, 0, 0), (hops[0], 3, 0), (hops[1], 1, 0), (hops[2], 2, 0)]
    if len(hops) > 3:
        pieces.append((hops[3], 2, hops[2].shape[0]))
    n_outs = len(out_shapes)

    def kernel(index_ref, *refs):
        sources, outs = refs[: len(pieces)], refs[len(pieces) :]
        for source, (_, step, start) in zip(sources, pieces):
            place = lax.rem(index_ref[0] + step, 4)
            views(outs, source, place, start)

    vmem = pl.BlockSpec(memory_space=pltpu.VMEM)
    return pl.pallas_call(
        kernel,
        in_specs=[pl.BlockSpec(memory_space=pltpu.SMEM)] + [vmem] * len(pieces),
        out_specs=[vmem] * n_outs,
        out_shape=[jax.ShapeDtypeStruct(shape, value.dtype) for shape in out_shapes],
        compiler_params=pltpu.CompilerParams(vmem_limit_bytes=24 * 2**20),
        cost_estimate=pl.CostEstimate(
            flops=0, bytes_accessed=16 * value.size, transcendentals=0
        ),
        name="ring_place",
    )(lax.axis_index(axis).reshape(1), *(p[0] for p in pieces))


def in_order(outs, piece, place, start):
    outs[0][place, pl.ds(start, piece.shape[0])] = piece[...]


def add(*parts):
    return sum(p.astype(f32) for p in parts).astype(bf16)


def ring_blocks(blocks, axis, dim):
    index = lax.axis_index(axis)
    return [
        lax.dynamic_index_in_dim(blocks, (index + k) % 4, dim, keepdims=False) for k in range(4)
    ]


def ring_sums(items, beside, tokens):
    blocks = [ring_blocks(*item) for item in items]
    hops = []
    for (_, axis, _), (_, _, far, _) in zip(items, blocks):
        half = far.shape[0] // 2
        hops.append(
            (lax.ppermute(far[:half], axis, AHEAD), lax.ppermute(far[half:], axis, BACK))
        )
    hops, beside, tokens = lax.optimization_barrier((hops, beside, tokens))
    ends = []
    for (_, axis, _), (own, after, _, before), (low, high) in zip(items, blocks, hops):
        half = low.shape[0]
        after = jnp.concatenate([add(after[:half], low), after[half:]])
        before = jnp.concatenate([before[:half], add(before[half:], high)])
        ends.append((own, lax.ppermute(after, axis, AHEAD), lax.ppermute(before, axis, BACK)))
    ends, traded = lax.optimization_barrier((ends, trade(tokens)))
    return [add(*e) for e in ends], beside, traded


def direct_sums(items):
    ways = [(1, AHEAD), (3, BACK), (2, ACROSS)]
    parts = []
    for blocks, axis, dim in items:
        block = ring_blocks(blocks, axis, dim)
        parts.append([block[0]] + [lax.ppermute(block[k], axis, way) for k, way in ways])
    return [add(*p) for p in lax.optimization_barrier(parts)]


def group_parts(own, mate, near, far):
    mate, far = swap(mate, "core"), swap(far, "core")
    sent = (near.astype(f32) + far.astype(f32)).astype(bf16)
    return own.astype(f32) + mate.astype(f32), sent


def normal_part(values):
    mean = jnp.mean(values, axis=-1, keepdims=True)
    centred = values - mean
    factor = lax.rsqrt(jnp.mean(centred * centred, axis=-1, keepdims=True) + EPSILON)
    return centred * factor, factor


def norm_back(grad, normal, factor, gain):
    e = grad * gain
    inner = jnp.mean(e * normal, axis=-1, keepdims=True)
    return factor * (e - jnp.mean(e, axis=-1, keepdims=True) - normal * inner)


def flip_halves(core, value):
    half = value.shape[-1] // 2
    turned = jnp.concatenate([value[..., half:], value[..., :half]], axis=-1)
    return jnp.where(core == 0, value, turned)


CHUNKS = 2


def chunked(halves):
    size = halves[0].shape[1] // CHUNKS
    cut = lambda h, i: h[:, i * size : (i + 1) * size]
    return [jnp.concatenate([cut(h, i) for h in halves], axis=1) for i in range(CHUNKS)]


def unchunked(chunks):
    size = chunks[0].shape[1] // 2
    return [
        jnp.concatenate([c[:, i * size : (i + 1) * size] for c in chunks], axis=1)
        for i in range(2)
    ]


def forward(tokens, w, late=None):
    inputs = tokens.astype(f32)
    normed_one = (normal_part(inputs)[0] * w["gain"][0] + w["shift"][0]).astype(bf16)
    project = lambda name: [
        (mm(normed_one, part) + bias).astype(bf16) for part, bias in zip(w[name], w[name + "_bias"])
    ]
    key_value = chunked(project("kv"))
    queries = chunked(project("q"))
    mate, near = swap(key_value[0], "core"), swap(key_value[0], "yl")
    blocks, results, traded = [], [], None
    for i, own in enumerate(key_value):
        blocks.append((own, mate, near, swap(near, "core")))
        if i + 1 < CHUNKS:
            following, near = lax.optimization_barrier((key_value[i + 1], near))
            if late is not None:
                traded = trade(late[2])
            mate, near = swap(following, "core"), swap(following, "yl")
            result = attend(queries[i], blocks[i])
            result, near, mate, traded = lax.optimization_barrier((result, near, mate, traded))
        else:
            if late is not None:
                blocks[i], gathered = lax.optimization_barrier((blocks[i], late[0]))
                w.update(late[1](gathered))
            result = attend(queries[i], blocks[i])
        results.append(result)
    attended, log_total = zip(*results)
    attended = jnp.concatenate(unchunked(attended), axis=1)
    attended = flip_halves(w["core"], attended)
    branch = flip_halves(w["core"], jnp.concatenate([mm(attended, p) for p in w["proj"]], axis=1))
    branch = branch + w["out_bias"][0]
    middle = inputs + w["scale"][0] * branch
    normed_two = (normal_part(middle)[0] * w["gain"][1] + w["shift"][1]).astype(bf16)
    activated, slope, branch_two = [], [], w["out_bias"][1]
    for up, bias, down in zip(w["fc1"], w["fc1_bias"], w["fc2"]):
        before = mm(normed_two, up) + bias
        phi = 0.5 * (1.0 + lax.erf(before * (0.5**0.5)))
        density = jnp.exp(-0.5 * before * before) * 0.3989422804014327
        active = (before * phi).astype(bf16)
        activated.append(active)
        slope.append((phi + before * density).astype(bf16))
        for i, part in enumerate(down):
            rows = part.shape[0]
            branch_two = branch_two + mm(active[:, i * rows : (i + 1) * rows], part)
    result = (middle + w["scale"][1] * branch_two).astype(bf16)
    kept = dict(
        inputs=inputs,
        normed_one=normed_one,
        queries=queries,
        blocks=blocks,
        traded=traded,
        attended=attended,
        log_total=log_total,
        branch=branch,
        middle=middle,
        normed_two=normed_two,
        activated=activated,
        slope=slope,
        branch_two=branch_two,
    )
    return result, kept


def backward(grad_out, kept, w, last=False, result=None):
    grad_branch_two = (w["scale"][1] * grad_out).astype(bf16)
    grad_before = []
    grad_normed_two = 0.0
    if last:
        fc2_sent = swap(fc2_part(kept["activated"][1], grad_branch_two), "core")
    for up, down, slope in zip(w["fc1"], w["fc2"], kept["slope"]):
        part = jnp.concatenate([mm_t(grad_branch_two, d) for d in down], axis=1)
        part = (part * slope.astype(f32)).astype(bf16)
        grad_before.append(part)
        grad_normed_two = grad_normed_two + mm_t(part, up)
    if last:
        fc2 = fc2_part(kept["activated"][0], grad_branch_two, fc2_sent)
        fc2, grad_normed_two = lax.optimization_barrier((fc2, grad_normed_two))
        fc2 = lax.psum_scatter(fc2, RING_Z, scatter_dimension=0, tiled=True)
    normal_two, factor_two = normal_part(kept["middle"])
    grad_middle = grad_out + norm_back(grad_normed_two, normal_two, factor_two, w["gain"][1])
    grad_branch = (w["scale"][0] * grad_middle).astype(bf16)
    width = grad_branch.shape[1]
    half = width // 2
    grad_halves = flip_halves(w["core"], grad_branch)
    grad_halves = [grad_halves[:, :half], grad_halves[:, half:]]
    grad_attended = sum(mm_t(g, p) for g, p in zip(grad_halves, w["proj"])).astype(bf16)
    grad_attended = flip_halves(w["core"], grad_attended)
    fc_grad = None
    if last:
        fc1_sent = fc1_part(kept["normed_two"], grad_before[1])
        fc1_sent, grad_attended = lax.optimization_barrier((fc1_sent, grad_attended))
        fc1_sent = swap(fc1_sent, "core")
    grad_chunks = chunked([grad_attended[:, :half], grad_attended[:, half:]])
    q_chunks, kv_chunks = [], []
    ready = None
    for i in range(CHUNKS):
        g = grad_chunks[i]
        if ready is not None:
            own, sent = ready
            if last and fc_grad is None:
                fc1 = fc1_part(kept["normed_two"], grad_before[0], fc1_sent)
                sent, g, fc1 = lax.optimization_barrier((sent, g, fc1))
                fc1 = lax.psum_scatter(fc1, RING_Z, scatter_dimension=0, tiled=True)
                fc_grad = [fc1, fc2]
            else:
                sent, g = lax.optimization_barrier((sent, g))
            came = swap(sent, "yl")
        parts = attend_back(kept["queries"][i], kept["blocks"][i], g, kept["log_total"][i])
        if ready is not None:
            parts, came = lax.optimization_barrier((parts, came))
            kv_chunks.append((own + came.astype(f32)).astype(bf16))
        q_chunks.append(parts[0])
        ready = group_parts(*parts[1:])
    own, sent = ready
    traded = None
    if result is not None:
        sent, result = lax.optimization_barrier((sent, result))
        traded = trade(result)
    a_full = None
    if last:
        grad_q = unchunked(q_chunks)
        make = lambda i, add=None: outer(
            [
                ((kept["normed_one"], 0), grad_q[i], width),
                ((kept["attended"], 0), grad_halves[i], width),
            ],
            half // 2,
            add=add,
        )
        a_full = make(0, swap(make(1), "core"))
    came, traded, a_full = lax.optimization_barrier((swap(sent, "yl"), traded, a_full))
    kv_chunks.append((own + came.astype(f32)).astype(bf16))
    grad_q, grad_kv = unchunked(q_chunks), unchunked(kv_chunks)
    grad_normed_one = sum(
        mm_t(g, part) for g, part in zip(grad_q + grad_kv, w["q"] + w["kv"])
    )
    normal_one, factor_one = normal_part(kept["inputs"])
    grad_inputs = grad_middle + norm_back(grad_normed_one, normal_one, factor_one, w["gain"][0])
    total = lambda a: jnp.sum(a.astype(f32), axis=0, keepdims=True)
    vectors = dict(
        gain=(total(grad_normed_one * normal_one), total(grad_normed_two * normal_two)),
        shift=(total(grad_normed_one), total(grad_normed_two)),
        out_bias=(total(grad_branch), total(grad_branch_two)),
        scale=(total(grad_middle * kept["branch"]), total(grad_out * kept["branch_two"])),
        q=[total(g) for g in grad_q],
        kv=[total(g) for g in grad_kv],
        fc1_bias=[total(g) for g in grad_before],
    )
    products = dict(
        a=a_full,
        kv=(kept["normed_one"], grad_kv),
        fc=fc_grad,
        traded=traded,
    )
    return grad_inputs.astype(bf16), vectors, products


def ordered(core, mine, other):
    return jnp.where(core == 0, mine, other), jnp.where(core == 0, other, mine)


def per_device(
    patch_tokens,
    out_grad,
    batch_counts,
    norm_gain,
    norm_bias,
    qkv_weight,
    qv_bias,
    proj_weight,
    fc1_weight,
    fc1_bias,
    fc2_weight,
    out_bias,
    layer_scale,
):
    section = lax.axis_index("section")
    core = lax.axis_index("core")
    shards = lax.axis_size(FSDP)
    images, rows, width = patch_tokens.shape
    half = width // 2
    own = width // shards
    hidden = fc2_weight.shape[1]
    mid = hidden // 2
    groups = half // PAIR
    pick = lambda a, i, axis: lax.dynamic_index_in_dim(a, i, axis, keepdims=False)

    part = mid // 2
    q, k, v = (qkv_weight[0][:, i * width : (i + 1) * width] for i in range(3))
    q_mine = pick(q.reshape(own, 2, half), core, 1)
    kv = jnp.stack([k.reshape(own, 2, groups, PAIR), v.reshape(own, 2, groups, PAIR)], axis=3)
    kv_mine = pick(kv, core, 1).reshape(own, width)
    proj_mine = pick(proj_weight[0].reshape(own, 2, half), core, 1)
    vectors = jnp.concatenate(
        [a[0] for a in (norm_gain, norm_bias, qv_bias, out_bias, layer_scale)]
        + [fc1_bias[0].reshape(hidden // own, own)],
        axis=0,
    ).T
    count = vectors.shape[1]
    vectors = jnp.pad(vectors, ((0, 0), (0, 128 - count)))
    fc1_mine = pick(fc1_weight[0].reshape(own, shards, 2, 2, part), core, 2)
    fc1_mine = jnp.swapaxes(fc1_mine, 1, 2).reshape(own, shards * mid)
    fc2_mine = pick(fc2_weight[0].reshape(2, 2, part, width), core, 0)
    fc_mine = jnp.concatenate([fc1_mine, fc2_mine[0], fc2_mine[1]], axis=1)
    fc_row = lax.all_gather(fc_mine, RING_Y, axis=0, tiled=True)

    mine = jnp.concatenate([kv_mine, vectors, q_mine, proj_mine], axis=1)
    live = (
        jnp.arange(images) % IMG_MB < jnp.repeat(batch_counts[0], IMG_MB)
    ).astype(bf16)
    live_grad = out_grad * live[:, None, None]
    hops = (*first_hop(mine, RING_Z), lax.ppermute(mine, RING_Z, ACROSS))
    hops, live_grad, first_tokens = lax.optimization_barrier(
        (hops, live_grad, as_image(trade(flip(patch_tokens))))
    )

    def row_views(outs, piece, place, start):
        at = 0
        for out in outs:
            size = out.shape[-1]
            out[place] = piece[:, at : at + size]
            at += size

    early, later = ring_place(
        mine, RING_Z, hops, [(4, own, width + 128), (4, own, width)], row_views
    )
    early_hops = first_hop(early, RING_Y)
    later, fc_row = lax.optimization_barrier((later, fc_row))
    fc_half = lax.all_gather(fc_row, RING_Z, axis=0, tiled=True)
    later_hops = first_hop(later, RING_Y)

    def views(outs, piece, place, start):
        for i in range(piece.shape[0]):
            at = 0
            for out in outs:
                size = out.shape[-1]
                out[start + i, place] = piece[i, :, at : at + size]
                at += size

    def spread(row, hops, sizes):
        hops = lax.optimization_barrier(hops)
        more = lax.optimization_barrier(second_hop(*hops, RING_Y))
        shapes = [(4, 4, own, size) for size in sizes]
        return [o.reshape(width, -1) for o in ring_place(row, RING_Y, hops + more, shapes, views)]

    kv_half, vectors = spread(early, early_hops, (width, 128))
    q_half, proj_half = spread(later, later_hops, (half, half))
    vectors = vectors[:, :16].T.astype(f32)

    def halves(row):
        return ordered(core, row[:, :half], row[:, half:])

    def fc1_bias_of(which):
        rows = jnp.where(which == 0, vectors[10:12], vectors[12:14])
        return jnp.concatenate([rows[0:1], rows[1:2]], axis=1)

    def kv_bias(v_half):
        zeros = jnp.zeros((1, PAIR), f32)
        cuts = [v_half[:, i * PAIR : (i + 1) * PAIR] for i in range(groups)]
        return jnp.concatenate([x for c in cuts for x in (zeros, c)], axis=1)

    wide = shards * mid
    w = dict(
        core=core,
        gain=(vectors[0:1], vectors[1:2]),
        shift=(vectors[2:3], vectors[3:4]),
        out_bias=(vectors[6:7], vectors[7:8]),
        scale=(vectors[8:9], vectors[9:10]),
        q=[q_half, swap(q_half, "core")],
        q_bias=halves(vectors[4:5]),
        kv=[kv_half, swap(kv_half, "core")],
        kv_bias=[kv_bias(b) for b in halves(vectors[5:6])],
        proj=(proj_half, swap(proj_half, "core")),
        fc1_bias=[fc1_bias_of(c) for c in (core, 1 - core)],
    )

    def fc_weights(gathered):
        pair = (gathered, swap(gathered, "core"))
        return dict(
            fc1=[f[:, :wide] for f in pair],
            fc2=[(f[:, wide : wide + width], f[:, wide + width :]) for f in pair],
        )


    sent, first = forward(first_tokens, w, late=(fc_half, fc_weights, live_grad))
    sent, traded = lax.optimization_barrier((sent, first["traded"]))
    passed = lax.ppermute(sent, "section", [(0, 1)])
    last_grad = as_image(flip(traded))
    tokens = jnp.where(section == 0, first_tokens, passed)
    result, kept = forward(tokens, w)

    slots = (images, result.shape[0] // images, width)
    sent, _, early = backward(last_grad.astype(f32), kept, w, result=result.reshape(slots))
    sent, traded = lax.optimization_barrier((sent, early["traded"]))
    passed, block_out = lax.optimization_barrier(
        (lax.ppermute(sent, "section", [(1, 0)]), flip(traded))
    )
    grad_out = jnp.where(section == 1, last_grad, passed).astype(f32)
    grad_inputs, sums, products = backward(grad_out, kept, w, last=True)

    vector_grads = vector_block(core, sums, width, PAIR)

    a1, dkv = products["kv"]
    make = lambda i, add=None: outer([((a1, 0), dkv[i], width)], half // 2, add=add)
    b_full = make(0, swap(make(1), "core"))
    a_full = products["a"]
    a_full = jnp.concatenate([a_full, vector_grads], axis=1).reshape(4, 4, own, width + PAIR)
    (a_sum, b_sum), rows, traded = ring_sums(
        [(a_full, RING_Y, 1), (b_full.reshape(4, 4, own, width), RING_Z, 0)],
        products["fc"],
        grad_inputs.reshape(slots),
    )
    fc_grad = lax.psum_scatter(
        jnp.concatenate(rows, axis=1), RING_Y, scatter_dimension=0, tiled=True
    )
    ab = direct_sums([(a_sum, RING_Z, 0), (b_sum, RING_Y, 0)])
    in_grad = flip(traded)
    ab = jnp.concatenate([ab[0][:, :width], ab[1], ab[0][:, width:]], axis=1)

    def chips_sum(a):
        return (a.astype(f32) + swap(a, "xhi").astype(f32)).astype(bf16)

    ab = chips_sum(ab)
    ab_other = swap(ab, "core")
    qkv_out, proj_out = join_qkv(core, ab, ab_other, width)
    vec_grad = sum(p[:, 2 * width : 2 * width + count].astype(f32) for p in (ab, ab_other)).T
    fc_grad = chips_sum(fc_grad)
    fc1_out, fc2_out = join_fc(core, fc_grad, swap(fc_grad, "core"), width, shards)
    return (
        block_out[None],
        in_grad[None],
        vec_grad[0:2][None],
        vec_grad[2:4][None],
        qkv_out[None],
        vec_grad[4:6][None],
        proj_out[None],
        fc1_out[None],
        vec_grad[10:].reshape(1, hidden),
        fc2_out[None],
        vec_grad[6:8][None],
        vec_grad[8:10][None],
    )


def solution(mesh):
    sections, fsdp, rep = mesh.devices.shape
    inner = Mesh(
        mesh.devices.reshape(sections, fsdp // 4, 2, 2, rep // 2, 2),
        ("section",) + FSDP + REP,
    )
    weight = P("section", FSDP, None)
    vector = P("section", None, FSDP)
    tokens = P(REP, FSDP, None)
    both = P("section", REP, FSDP, None)
    return jax.shard_map(
        per_device,
        mesh=inner,
        in_specs=(
            tokens,
            tokens,
            P(REP, None),
            vector,
            vector,
            weight,
            vector,
            weight,
            weight,
            P("section", FSDP),
            weight,
            vector,
            vector,
        ),
        out_specs=(
            both,
            both,
            vector,
            vector,
            weight,
            vector,
            weight,
            weight,
            P("section", FSDP),
            weight,
            vector,
            vector,
        ),
        check_vma=False,
    )
```

```python
import jax
import jax.numpy as jnp
from jax import lax
from jax.experimental import pallas as pl
from jax.experimental.pallas import tpu as pltpu
from jax.sharding import Mesh, PartitionSpec as P

HEAD_DIM = 64
IMG_MB = 2
PAIR = 2 * HEAD_DIM
EPSILON = 1e-06

FSDP = ("z", "yh", "yl")
REP = ("xhi", "core")
bf16 = jnp.bfloat16
f32 = jnp.float32


def dot(a, b, dims):
    return lax.dot_general(a, b, (dims, ((), ())), preferred_element_type=f32)


def mm(a, b):
    return dot(a, b, ((1,), (0,)))


def mm_t(a, b):
    return dot(a, b, ((1,), (1,)))


def t_mm(a, b):
    return dot(a, b, ((0,), (0,)))


def swap(value, axis):
    return lax.ppermute(value, axis, [(0, 1), (1, 0)])


def attend_kernel(q_ref, own_ref, mate_ref, near_ref, far_ref, out_ref, log_ref):
    rows = q_ref.shape[0]
    both = [r[...] for r in (own_ref, mate_ref, near_ref, far_ref)]
    keys = jnp.concatenate([b[:, :PAIR] for b in both], axis=0)
    values = jnp.concatenate([b[:, PAIR:] for b in both], axis=0)
    queries = q_ref[...] * jnp.asarray(HEAD_DIM**-0.5, bf16)
    lane = lax.broadcasted_iota(jnp.int32, (rows, PAIR), 1)
    outs = []
    for head in range(2):
        mine = (lane >= head * HEAD_DIM) & (lane < (head + 1) * HEAD_DIM)
        picked = jnp.where(mine, queries, jnp.zeros_like(queries))
        scores = mm_t(keys, picked)
        top = jnp.max(scores, axis=0, keepdims=True)
        raised = jnp.exp(scores - top)
        total = jnp.sum(raised, axis=0, keepdims=True)
        out = t_mm(values, raised.astype(bf16))
        outs.append(out * (1.0 / total))
        log_ref[0, head : head + 1, :] = top + jnp.log(total)
    row = lax.broadcasted_iota(jnp.int32, (PAIR, rows), 0)
    joined = jnp.where(row < HEAD_DIM, outs[0], outs[1])
    out_ref[...] = joined.T.astype(bf16)


def attend_back_kernel(
    q_ref, own_ref, mate_ref, near_ref, far_ref, grad_ref, log_ref, dq_ref, *dkv_refs
):
    rows = q_ref.shape[0]
    both = [r[...] for r in (own_ref, mate_ref, near_ref, far_ref)]
    keys = jnp.concatenate([b[:, :PAIR] for b in both], axis=0)
    values = jnp.concatenate([b[:, PAIR:] for b in both], axis=0)
    queries = q_ref[...] * jnp.asarray(HEAD_DIM**-0.5, bf16)
    grads = grad_ref[...]
    lane = lax.broadcasted_iota(jnp.int32, (rows, PAIR), 1)
    dqs, dk, dv = [], None, None
    for head in range(2):
        mine = (lane >= head * HEAD_DIM) & (lane < (head + 1) * HEAD_DIM)
        picked = jnp.where(mine, queries, jnp.zeros_like(queries))
        grad = jnp.where(mine, grads, jnp.zeros_like(grads))
        scores = mm_t(keys, picked)
        weighting = jnp.exp(scores - log_ref[0, head : head + 1, :])
        grad_weighting = mm_t(values, grad)
        row_term = jnp.sum(grad_weighting * weighting, axis=0, keepdims=True)
        grad_scores = (weighting * (grad_weighting - row_term)).astype(bf16)
        dqs.append(t_mm(keys, grad_scores))
        k_part = mm(grad_scores, picked)
        v_part = mm(weighting.astype(bf16), grad)
        dk = k_part if dk is None else dk + k_part
        dv = v_part if dv is None else dv + v_part
    row = lax.broadcasted_iota(jnp.int32, (PAIR, rows), 0)
    joined = jnp.where(row < HEAD_DIM, dqs[0], dqs[1]) * (HEAD_DIM**-0.5)
    dq_ref[...] = joined.T.astype(bf16)
    for i, ref in enumerate(dkv_refs):
        ref[:, :PAIR] = dk[i * rows : (i + 1) * rows].astype(bf16)
        ref[:, PAIR:] = dv[i * rows : (i + 1) * rows].astype(bf16)


def pair_specs(rows, pairs):
    half = pairs // 2
    q_spec = pl.BlockSpec((rows, PAIR), lambda i: (0, i))
    kv_spec = pl.BlockSpec((rows, 2 * PAIR), lambda i: (0, i))
    kv_swapped = pl.BlockSpec((rows, 2 * PAIR), lambda i: (0, (i + half) % pairs))
    log_spec = pl.BlockSpec((1, 2, rows), lambda i: (i, 0, 0))
    return q_spec, [kv_spec, kv_swapped, kv_spec, kv_swapped], log_spec


def attend_cost(queries, blocks, products):
    rows, width = queries.shape
    scores = rows * rows * len(blocks) * width // HEAD_DIM
    return pl.CostEstimate(
        flops=products * scores * 2 * 256,
        bytes_accessed=2 * 2 * len(blocks) * rows * width * 2,
        transcendentals=scores,
    )


def attend(queries, blocks):
    rows, width = queries.shape
    pairs = width // PAIR
    q_spec, kv_specs, log_spec = pair_specs(rows, pairs)
    return pl.pallas_call(
        attend_kernel,
        grid=(pairs,),
        in_specs=[q_spec] + kv_specs,
        out_specs=[q_spec, log_spec],
        out_shape=[
            jax.ShapeDtypeStruct((rows, width), bf16),
            jax.ShapeDtypeStruct((pairs, 2, rows), f32),
        ],
        compiler_params=pltpu.CompilerParams(vmem_limit_bytes=40 * 2**20),
        cost_estimate=attend_cost(queries, blocks, 2),
        name="attend",
    )(queries, *blocks)


def attend_back(queries, blocks, grad, log_total):
    rows, width = queries.shape
    pairs = width // PAIR
    q_spec, kv_specs, log_spec = pair_specs(rows, pairs)
    return pl.pallas_call(
        attend_back_kernel,
        grid=(pairs,),
        in_specs=[q_spec] + kv_specs + [q_spec, log_spec],
        out_specs=[q_spec] + kv_specs,
        out_shape=[jax.ShapeDtypeStruct((rows, width), bf16)]
        + [jax.ShapeDtypeStruct((rows, 2 * width), bf16)] * 4,
        compiler_params=pltpu.CompilerParams(vmem_limit_bytes=40 * 2**20),
        cost_estimate=attend_cost(queries, blocks, 5),
        name="attend_back",
    )(queries, *blocks, grad, log_total)


def outer(segments, step, add=None, tail=None):
    rows = segments[0][1].shape[0]
    width = segments[0][2]
    counts = [right.shape[1] // step for _, right, _ in segments]
    starts = [sum(counts[:k]) for k in range(len(counts))]
    total = sum(counts)
    grid = total + (tail is not None)
    n = len(segments)

    def kernel(*refs):
        out_ref = refs[-1]
        i = pl.program_id(0)
        for k in range(n):

            @pl.when((i >= starts[k]) & (i < starts[k] + counts[k]))
            def _(k=k):
                value = t_mm(refs[2 * k][...], refs[2 * k + 1][...])
                if add is not None:
                    value = value + refs[2 * n][...].astype(f32)
                out_ref[...] = value.astype(bf16)

        if tail is not None:

            @pl.when(i == total)
            def _():
                out_ref[...] = refs[2 * n + (add is not None)][...]

    in_specs, operands = [], []
    for (left, right, _), start, count in zip(segments, starts, counts):
        array, which = left
        in_specs.append(pl.BlockSpec((rows, width), lambda i, w=which: (0, w)))
        in_specs.append(
            pl.BlockSpec((rows, step), lambda i, s=start, c=count: (0, jnp.clip(i - s, 0, c - 1)))
        )
        operands += [array, right]
    if add is not None:
        in_specs.append(pl.BlockSpec((width, step), lambda i: (0, jnp.minimum(i, total - 1))))
        operands.append(add)
    if tail is not None:
        in_specs.append(pl.BlockSpec((width, step), lambda i: (0, 0)))
        operands.append(tail)
    return pl.pallas_call(
        kernel,
        grid=(grid,),
        in_specs=in_specs,
        out_specs=pl.BlockSpec((width, step), lambda i: (0, i)),
        out_shape=jax.ShapeDtypeStruct((width, grid * step), bf16),
        compiler_params=pltpu.CompilerParams(vmem_limit_bytes=40 * 2**20),
        cost_estimate=pl.CostEstimate(
            flops=2 * rows * width * total * step,
            bytes_accessed=2 * width * grid * step * (1 if add is None else 2),
            transcendentals=0,
        ),
        name="outer",
    )(*operands)


def fc1_part(normed, grad_before, add=None):
    return outer([((normed, 0), grad_before, normed.shape[1])], 512, add=add)


def fc2_part(activated, grad_branch, add=None):
    width = grad_branch.shape[1]
    count = activated.shape[1] // width
    return outer([((activated, i), grad_branch, width) for i in range(count)], 512, add=add)


def join(kernel, core, inputs, shapes):
    vmem = pl.BlockSpec(memory_space=pltpu.VMEM)
    return pl.pallas_call(
        kernel,
        in_specs=[pl.BlockSpec(memory_space=pltpu.SMEM)] + [vmem] * len(inputs),
        out_specs=[vmem] * len(shapes),
        out_shape=[jax.ShapeDtypeStruct(shape, f32) for shape in shapes],
        compiler_params=pltpu.CompilerParams(vmem_limit_bytes=24 * 2**20),
        cost_estimate=pl.CostEstimate(
            flops=0, bytes_accessed=6 * sum(a.size for a in inputs), transcendentals=0
        ),
        name="join",
    )(core.reshape(1), *inputs)


def vector_block(core, sums, width, columns):
    half = width // 2
    whole = [*sums["gain"], *sums["shift"], *sums["out_bias"], *sums["scale"]]
    halves = [*sums["q"], *sums["kv"], *sums["fc1_bias"]]

    def kernel(core_ref, *refs):
        out_ref, rows_ref = refs[-2:]
        flag = core_ref[0]
        order = lambda a, b: (jnp.where(flag == 0, a, b), jnp.where(flag == 0, b, a))
        rows_ref[...] = jnp.zeros(rows_ref.shape, f32)
        for ref, row in zip(refs, (0, 1, 2, 3, 6, 7, 8, 9)):
            rows_ref[row : row + 1, :] = ref[...]
        q_mine, q_other, kv_mine, kv_other, fc_mine, fc_other = (
            r[...] for r in refs[len(whole) : len(whole) + len(halves)]
        )
        for i, value in enumerate(order(q_mine, q_other)):
            rows_ref[4:5, i * half : (i + 1) * half] = value
        for i, value in enumerate(order(kv_mine, kv_other)):
            for g in range(half // PAIR):
                at = i * half + g * PAIR
                rows_ref[5:6, at : at + PAIR] = value[:, (2 * g + 1) * PAIR : (2 * g + 2) * PAIR]
        for i, value in enumerate(order(fc_mine, fc_other)):
            for k in range(2):
                row = 10 + 2 * i + k
                rows_ref[row : row + 1, :] = value[:, k * width : (k + 1) * width]
        out_ref[...] = rows_ref[...].T.astype(bf16)

    vmem = pl.BlockSpec(memory_space=pltpu.VMEM)
    return pl.pallas_call(
        kernel,
        in_specs=[pl.BlockSpec(memory_space=pltpu.SMEM)] + [vmem] * len(whole + halves),
        out_specs=vmem,
        out_shape=jax.ShapeDtypeStruct((width, columns), bf16),
        scratch_shapes=[pltpu.VMEM((columns, width), f32)],
        name="vector_block",
    )(core.reshape(1), *whole, *halves)


def join_qkv(core, mine, other, width):
    rows, half = mine.shape[0], width // 2

    def kernel(core_ref, mine_ref, other_ref, qkv_ref, proj_ref):
        for ref, place in ((mine_ref, core_ref[0]), (other_ref, 1 - core_ref[0])):
            at = place * half
            columns = lambda start, size: pl.ds(pl.multiple_of(at + start, PAIR), size)
            qkv_ref[:, columns(0, half)] = ref[:, :half].astype(f32)
            proj_ref[:, columns(0, half)] = ref[:, half:width].astype(f32)
            for g in range(half // PAIR):
                k = width + 2 * g * PAIR
                for i in range(2):
                    qkv_ref[:, columns((i + 1) * width + g * PAIR, PAIR)] = ref[
                        :, k + i * PAIR : k + (i + 1) * PAIR
                    ].astype(f32)

    return join(kernel, core, [mine, other], [(rows, 3 * width), (rows, width)])


def join_fc(core, mine, other, width, shards):
    rows = mine.shape[0]
    wide = mine.shape[1] - 2 * width
    part = wide // (2 * shards)
    pair = 2 * part

    def kernel(core_ref, mine_ref, other_ref, fc1_ref, fc2_ref):
        for ref, place in ((mine_ref, core_ref[0]), (other_ref, 1 - core_ref[0])):
            for f in range(shards):
                at = pl.multiple_of(2 * pair * f + place * pair, pair)
                value = [
                    ref[:, i * shards * part + f * part : i * shards * part + (f + 1) * part]
                    for i in range(2)
                ]
                fc1_ref[:, pl.ds(at, pair)] = jnp.concatenate(value, axis=1).astype(f32)
            for i in range(2):
                at = pl.multiple_of(place * 2 * rows + i * rows, rows)
                fc2_ref[pl.ds(at, rows)] = ref[
                    :, wide + i * width : wide + (i + 1) * width
                ].astype(f32)

    return join(kernel, core, [mine, other], [(rows, 2 * wide), (4 * rows, width)])


FLIP = [(0, 0), (1, 2), (2, 1), (3, 3)]


def flip(tokens):
    return lax.ppermute(tokens, ("yh", "core"), FLIP)


def trade(tokens):
    return lax.all_to_all(tokens, "z", split_axis=0, concat_axis=0, tiled=True)


def as_image(tokens):
    return tokens.reshape(-1, tokens.shape[-1])


RING_Z, RING_Y = "z", ("yh", "yl")
AHEAD = [(i, (i + 1) % 4) for i in range(4)]
BACK = [(i, (i - 1) % 4) for i in range(4)]


ACROSS = [(i, (i + 2) % 4) for i in range(4)]


def first_hop(value, axis):
    return lax.ppermute(value, axis, AHEAD), lax.ppermute(value, axis, BACK)


def second_hop(ahead, back, axis):
    half = ahead.shape[0] // 2
    return (
        lax.ppermute(ahead[:half], axis, AHEAD),
        lax.ppermute(back[half:], axis, BACK),
    )


def ring_place(value, axis, hops, out_shapes, views):
    pieces = [(value, 0, 0), (hops[0], 3, 0), (hops[1], 1, 0), (hops[2], 2, 0)]
    if len(hops) > 3:
        pieces.append((hops[3], 2, hops[2].shape[0]))
    n_outs = len(out_shapes)

    def kernel(index_ref, *refs):
        sources, outs = refs[: len(pieces)], refs[len(pieces) :]
        for source, (_, step, start) in zip(sources, pieces):
            place = lax.rem(index_ref[0] + step, 4)
            views(outs, source, place, start)

    vmem = pl.BlockSpec(memory_space=pltpu.VMEM)
    return pl.pallas_call(
        kernel,
        in_specs=[pl.BlockSpec(memory_space=pltpu.SMEM)] + [vmem] * len(pieces),
        out_specs=[vmem] * n_outs,
        out_shape=[jax.ShapeDtypeStruct(shape, value.dtype) for shape in out_shapes],
        compiler_params=pltpu.CompilerParams(vmem_limit_bytes=24 * 2**20),
        cost_estimate=pl.CostEstimate(
            flops=0, bytes_accessed=16 * value.size, transcendentals=0
        ),
        name="ring_place",
    )(lax.axis_index(axis).reshape(1), *(p[0] for p in pieces))


def in_order(outs, piece, place, start):
    outs[0][place, pl.ds(start, piece.shape[0])] = piece[...]


def add(*parts):
    return sum(p.astype(f32) for p in parts).astype(bf16)


def ring_blocks(blocks, axis, dim):
    index = lax.axis_index(axis)
    return [
        lax.dynamic_index_in_dim(blocks, (index + k) % 4, dim, keepdims=False) for k in range(4)
    ]


def ring_sums(items, beside, tokens):
    blocks = [ring_blocks(*item) for item in items]
    hops = []
    for (_, axis, _), (_, _, far, _) in zip(items, blocks):
        half = far.shape[0] // 2
        hops.append(
            (lax.ppermute(far[:half], axis, AHEAD), lax.ppermute(far[half:], axis, BACK))
        )
    hops, beside, tokens = lax.optimization_barrier((hops, beside, tokens))
    ends = []
    for (_, axis, _), (own, after, _, before), (low, high) in zip(items, blocks, hops):
        half = low.shape[0]
        after = jnp.concatenate([add(after[:half], low), after[half:]])
        before = jnp.concatenate([before[:half], add(before[half:], high)])
        ends.append((own, lax.ppermute(after, axis, AHEAD), lax.ppermute(before, axis, BACK)))
    ends, traded = lax.optimization_barrier((ends, trade(tokens)))
    return [add(*e) for e in ends], beside, traded


def direct_sums(items):
    ways = [(1, AHEAD), (3, BACK), (2, ACROSS)]
    parts = []
    for blocks, axis, dim in items:
        block = ring_blocks(blocks, axis, dim)
        parts.append([block[0]] + [lax.ppermute(block[k], axis, way) for k, way in ways])
    return [add(*p) for p in lax.optimization_barrier(parts)]


def group_parts(own, mate, near, far):
    mate, far = swap(mate, "core"), swap(far, "core")
    sent = (near.astype(f32) + far.astype(f32)).astype(bf16)
    return own.astype(f32) + mate.astype(f32), sent


def normal_part(values):
    mean = jnp.mean(values, axis=-1, keepdims=True)
    centred = values - mean
    factor = lax.rsqrt(jnp.mean(centred * centred, axis=-1, keepdims=True) + EPSILON)
    return centred * factor, factor


def norm_back(grad, normal, factor, gain):
    e = grad * gain
    inner = jnp.mean(e * normal, axis=-1, keepdims=True)
    return factor * (e - jnp.mean(e, axis=-1, keepdims=True) - normal * inner)


def flip_halves(core, value):
    half = value.shape[-1] // 2
    turned = jnp.concatenate([value[..., half:], value[..., :half]], axis=-1)
    return jnp.where(core == 0, value, turned)


CHUNKS = 2


def chunked(halves):
    size = halves[0].shape[1] // CHUNKS
    cut = lambda h, i: h[:, i * size : (i + 1) * size]
    return [jnp.concatenate([cut(h, i) for h in halves], axis=1) for i in range(CHUNKS)]


def unchunked(chunks):
    size = chunks[0].shape[1] // 2
    return [
        jnp.concatenate([c[:, i * size : (i + 1) * size] for c in chunks], axis=1)
        for i in range(2)
    ]


def forward(tokens, w, late=None):
    inputs = tokens.astype(f32)
    normed_one = (normal_part(inputs)[0] * w["gain"][0] + w["shift"][0]).astype(bf16)
    project = lambda name: [
        (mm(normed_one, part) + bias).astype(bf16) for part, bias in zip(w[name], w[name + "_bias"])
    ]
    key_value = chunked(project("kv"))
    queries = chunked(project("q"))
    mate, near = swap(key_value[0], "core"), swap(key_value[0], "yl")
    blocks, results, traded = [], [], None
    for i, own in enumerate(key_value):
        blocks.append((own, mate, near, swap(near, "core")))
        if i + 1 < CHUNKS:
            following, near = lax.optimization_barrier((key_value[i + 1], near))
            if late is not None:
                traded = trade(late[2])
            mate, near = swap(following, "core"), swap(following, "yl")
            result = attend(queries[i], blocks[i])
            result, near, mate, traded = lax.optimization_barrier((result, near, mate, traded))
        else:
            if late is not None:
                blocks[i], gathered = lax.optimization_barrier((blocks[i], late[0]))
                w.update(late[1](gathered))
            result = attend(queries[i], blocks[i])
        results.append(result)
    attended, log_total = zip(*results)
    attended = jnp.concatenate(unchunked(attended), axis=1)
    attended = flip_halves(w["core"], attended)
    branch = flip_halves(w["core"], jnp.concatenate([mm(attended, p) for p in w["proj"]], axis=1))
    branch = branch + w["out_bias"][0]
    middle = inputs + w["scale"][0] * branch
    normed_two = (normal_part(middle)[0] * w["gain"][1] + w["shift"][1]).astype(bf16)
    activated, slope, branch_two = [], [], w["out_bias"][1]
    for up, bias, down in zip(w["fc1"], w["fc1_bias"], w["fc2"]):
        before = mm(normed_two, up) + bias
        phi = 0.5 * (1.0 + lax.erf(before * (0.5**0.5)))
        density = jnp.exp(-0.5 * before * before) * 0.3989422804014327
        active = (before * phi).astype(bf16)
        activated.append(active)
        slope.append((phi + before * density).astype(bf16))
        for i, part in enumerate(down):
            rows = part.shape[0]
            branch_two = branch_two + mm(active[:, i * rows : (i + 1) * rows], part)
    result = (middle + w["scale"][1] * branch_two).astype(bf16)
    kept = dict(
        inputs=inputs,
        normed_one=normed_one,
        queries=queries,
        blocks=blocks,
        traded=traded,
        attended=attended,
        log_total=log_total,
        branch=branch,
        middle=middle,
        normed_two=normed_two,
        activated=activated,
        slope=slope,
        branch_two=branch_two,
    )
    return result, kept


def backward(grad_out, kept, w, last=False, result=None):
    grad_branch_two = (w["scale"][1] * grad_out).astype(bf16)
    grad_before = []
    grad_normed_two = 0.0
    if last:
        fc2_sent = swap(fc2_part(kept["activated"][1], grad_branch_two), "core")
    for up, down, slope in zip(w["fc1"], w["fc2"], kept["slope"]):
        part = jnp.concatenate([mm_t(grad_branch_two, d) for d in down], axis=1)
        part = (part * slope.astype(f32)).astype(bf16)
        grad_before.append(part)
        grad_normed_two = grad_normed_two + mm_t(part, up)
    if last:
        fc2 = fc2_part(kept["activated"][0], grad_branch_two, fc2_sent)
        fc2, grad_normed_two = lax.optimization_barrier((fc2, grad_normed_two))
        fc2 = lax.psum_scatter(fc2, RING_Z, scatter_dimension=0, tiled=True)
    normal_two, factor_two = normal_part(kept["middle"])
    grad_middle = grad_out + norm_back(grad_normed_two, normal_two, factor_two, w["gain"][1])
    grad_branch = (w["scale"][0] * grad_middle).astype(bf16)
    width = grad_branch.shape[1]
    half = width // 2
    grad_halves = flip_halves(w["core"], grad_branch)
    grad_halves = [grad_halves[:, :half], grad_halves[:, half:]]
    grad_attended = sum(mm_t(g, p) for g, p in zip(grad_halves, w["proj"])).astype(bf16)
    grad_attended = flip_halves(w["core"], grad_attended)
    fc_grad = None
    if last:
        fc1_sent = fc1_part(kept["normed_two"], grad_before[1])
        fc1_sent, grad_attended = lax.optimization_barrier((fc1_sent, grad_attended))
        fc1_sent = swap(fc1_sent, "core")
    grad_chunks = chunked([grad_attended[:, :half], grad_attended[:, half:]])
    q_chunks, kv_chunks = [], []
    ready = None
    for i in range(CHUNKS):
        g = grad_chunks[i]
        if ready is not None:
            own, sent = ready
            if last and fc_grad is None:
                fc1 = fc1_part(kept["normed_two"], grad_before[0], fc1_sent)
                sent, g, fc1 = lax.optimization_barrier((sent, g, fc1))
                fc1 = lax.psum_scatter(fc1, RING_Z, scatter_dimension=0, tiled=True)
                fc_grad = [fc1, fc2]
            else:
                sent, g = lax.optimization_barrier((sent, g))
            came = swap(sent, "yl")
        parts = attend_back(kept["queries"][i], kept["blocks"][i], g, kept["log_total"][i])
        if ready is not None:
            parts, came = lax.optimization_barrier((parts, came))
            kv_chunks.append((own + came.astype(f32)).astype(bf16))
        q_chunks.append(parts[0])
        ready = group_parts(*parts[1:])
    own, sent = ready
    traded = None
    if result is not None:
        sent, result = lax.optimization_barrier((sent, result))
        traded = trade(result)
    came, traded = lax.optimization_barrier((swap(sent, "yl"), traded))
    kv_chunks.append((own + came.astype(f32)).astype(bf16))
    grad_q, grad_kv = unchunked(q_chunks), unchunked(kv_chunks)
    grad_normed_one = sum(
        mm_t(g, part) for g, part in zip(grad_q + grad_kv, w["q"] + w["kv"])
    )
    normal_one, factor_one = normal_part(kept["inputs"])
    grad_inputs = grad_middle + norm_back(grad_normed_one, normal_one, factor_one, w["gain"][0])
    total = lambda a: jnp.sum(a.astype(f32), axis=0, keepdims=True)
    vectors = dict(
        gain=(total(grad_normed_one * normal_one), total(grad_normed_two * normal_two)),
        shift=(total(grad_normed_one), total(grad_normed_two)),
        out_bias=(total(grad_branch), total(grad_branch_two)),
        scale=(total(grad_middle * kept["branch"]), total(grad_out * kept["branch_two"])),
        q=[total(g) for g in grad_q],
        kv=[total(g) for g in grad_kv],
        fc1_bias=[total(g) for g in grad_before],
    )
    products = dict(
        q=(kept["normed_one"], grad_q),
        kv=(kept["normed_one"], grad_kv),
        proj=(kept["attended"], grad_halves),
        fc=fc_grad,
        traded=traded,
    )
    return grad_inputs.astype(bf16), vectors, products


def ordered(core, mine, other):
    return jnp.where(core == 0, mine, other), jnp.where(core == 0, other, mine)


def per_device(
    patch_tokens,
    out_grad,
    batch_counts,
    norm_gain,
    norm_bias,
    qkv_weight,
    qv_bias,
    proj_weight,
    fc1_weight,
    fc1_bias,
    fc2_weight,
    out_bias,
    layer_scale,
):
    section = lax.axis_index("section")
    core = lax.axis_index("core")
    shards = lax.axis_size(FSDP)
    images, rows, width = patch_tokens.shape
    half = width // 2
    own = width // shards
    hidden = fc2_weight.shape[1]
    mid = hidden // 2
    groups = half // PAIR
    pick = lambda a, i, axis: lax.dynamic_index_in_dim(a, i, axis, keepdims=False)

    part = mid // 2
    q, k, v = (qkv_weight[0][:, i * width : (i + 1) * width] for i in range(3))
    q_mine = pick(q.reshape(own, 2, half), core, 1)
    kv = jnp.stack([k.reshape(own, 2, groups, PAIR), v.reshape(own, 2, groups, PAIR)], axis=3)
    kv_mine = pick(kv, core, 1).reshape(own, width)
    proj_mine = pick(proj_weight[0].reshape(own, 2, half), core, 1)
    vectors = jnp.concatenate(
        [a[0] for a in (norm_gain, norm_bias, qv_bias, out_bias, layer_scale)]
        + [fc1_bias[0].reshape(hidden // own, own)],
        axis=0,
    ).T
    count = vectors.shape[1]
    vectors = jnp.pad(vectors, ((0, 0), (0, 128 - count)))
    fc1_mine = pick(fc1_weight[0].reshape(own, shards, 2, 2, part), core, 2)
    fc1_mine = jnp.swapaxes(fc1_mine, 1, 2).reshape(own, shards * mid)
    fc2_mine = pick(fc2_weight[0].reshape(2, 2, part, width), core, 0)
    fc_mine = jnp.concatenate([fc1_mine, fc2_mine[0], fc2_mine[1]], axis=1)
    fc_row = lax.all_gather(fc_mine, RING_Y, axis=0, tiled=True)

    mine = jnp.concatenate([kv_mine, q_mine, proj_mine, vectors], axis=1)
    live = (
        jnp.arange(images) % IMG_MB < jnp.repeat(batch_counts[0], IMG_MB)
    ).astype(bf16)
    live_grad = out_grad * live[:, None, None]
    hops = (*first_hop(mine, RING_Z), lax.ppermute(mine, RING_Z, ACROSS))
    hops, fc_row, live_grad, first_tokens = lax.optimization_barrier(
        (hops, fc_row, live_grad, as_image(trade(flip(patch_tokens))))
    )
    fc_half = lax.all_gather(fc_row, RING_Z, axis=0, tiled=True)
    row = ring_place(mine, RING_Z, hops, [(4, *mine.shape)], in_order)[0]
    hops = lax.optimization_barrier(first_hop(row, RING_Y))
    more = lax.optimization_barrier(second_hop(*hops, RING_Y))

    def views(outs, piece, place, start):
        for i in range(piece.shape[0]):
            at = 0
            for out in outs:
                size = out.shape[-1]
                out[start + i, place] = piece[i, :, at : at + size]
                at += size

    sizes = (width, half, half, 128)
    kv_half, q_half, proj_half, vectors = (
        o.reshape(width, -1)
        for o in ring_place(
            row, RING_Y, hops + more, [(4, 4, own, size) for size in sizes], views
        )
    )
    vectors = vectors[:, :16].T.astype(f32)

    def halves(row):
        return ordered(core, row[:, :half], row[:, half:])

    def fc1_bias_of(which):
        rows = jnp.where(which == 0, vectors[10:12], vectors[12:14])
        return jnp.concatenate([rows[0:1], rows[1:2]], axis=1)

    def kv_bias(v_half):
        zeros = jnp.zeros((1, PAIR), f32)
        cuts = [v_half[:, i * PAIR : (i + 1) * PAIR] for i in range(groups)]
        return jnp.concatenate([x for c in cuts for x in (zeros, c)], axis=1)

    wide = shards * mid
    w = dict(
        core=core,
        gain=(vectors[0:1], vectors[1:2]),
        shift=(vectors[2:3], vectors[3:4]),
        out_bias=(vectors[6:7], vectors[7:8]),
        scale=(vectors[8:9], vectors[9:10]),
        q=[q_half, swap(q_half, "core")],
        q_bias=halves(vectors[4:5]),
        kv=[kv_half, swap(kv_half, "core")],
        kv_bias=[kv_bias(b) for b in halves(vectors[5:6])],
        proj=(proj_half, swap(proj_half, "core")),
        fc1_bias=[fc1_bias_of(c) for c in (core, 1 - core)],
    )

    def fc_weights(gathered):
        pair = (gathered, swap(gathered, "core"))
        return dict(
            fc1=[f[:, :wide] for f in pair],
            fc2=[(f[:, wide : wide + width], f[:, wide + width :]) for f in pair],
        )


    sent, first = forward(first_tokens, w, late=(fc_half, fc_weights, live_grad))
    sent, traded = lax.optimization_barrier((sent, first["traded"]))
    passed = lax.ppermute(sent, "section", [(0, 1)])
    last_grad = as_image(flip(traded))
    tokens = jnp.where(section == 0, first_tokens, passed)
    result, kept = forward(tokens, w)

    slots = (images, result.shape[0] // images, width)
    sent, _, early = backward(last_grad.astype(f32), kept, w, result=result.reshape(slots))
    sent, traded = lax.optimization_barrier((sent, early["traded"]))
    passed, block_out = lax.optimization_barrier(
        (lax.ppermute(sent, "section", [(1, 0)]), flip(traded))
    )
    grad_out = jnp.where(section == 1, last_grad, passed).astype(f32)
    grad_inputs, sums, products = backward(grad_out, kept, w, last=True)

    vector_grads = vector_block(core, sums, width, PAIR)

    a1, dq = products["q"]
    dkv = products["kv"][1]
    o, e1 = products["proj"]
    make_a = lambda i, add=None: outer(
        [((a1, 0), dq[i], width), ((o, 0), e1[i], width)], half // 2, add=add
    )
    make_b = lambda i, add=None: outer([((a1, 0), dkv[i], width)], half // 2, add=add)
    a_full, b_full = (make(0, swap(make(1), "core")) for make in (make_a, make_b))
    a_full = jnp.concatenate([a_full, vector_grads], axis=1).reshape(4, 4, own, width + PAIR)
    (a_sum, b_sum), rows, traded = ring_sums(
        [(a_full, RING_Y, 1), (b_full.reshape(4, 4, own, width), RING_Z, 0)],
        products["fc"],
        grad_inputs.reshape(slots),
    )
    fc_grad = lax.psum_scatter(
        jnp.concatenate(rows, axis=1), RING_Y, scatter_dimension=0, tiled=True
    )
    ab = direct_sums([(a_sum, RING_Z, 0), (b_sum, RING_Y, 0)])
    in_grad = flip(traded)
    ab = jnp.concatenate([ab[0][:, :width], ab[1], ab[0][:, width:]], axis=1)

    def chips_sum(a):
        return (a.astype(f32) + swap(a, "xhi").astype(f32)).astype(bf16)

    ab = chips_sum(ab)
    ab_other = swap(ab, "core")
    qkv_out, proj_out = join_qkv(core, ab, ab_other, width)
    vec_grad = sum(p[:, 2 * width : 2 * width + count].astype(f32) for p in (ab, ab_other)).T
    fc_grad = chips_sum(fc_grad)
    fc1_out, fc2_out = join_fc(core, fc_grad, swap(fc_grad, "core"), width, shards)
    return (
        block_out[None],
        in_grad[None],
        vec_grad[0:2][None],
        vec_grad[2:4][None],
        qkv_out[None],
        vec_grad[4:6][None],
        proj_out[None],
        fc1_out[None],
        vec_grad[10:].reshape(1, hidden),
        fc2_out[None],
        vec_grad[6:8][None],
        vec_grad[8:10][None],
    )


def solution(mesh):
    sections, fsdp, rep = mesh.devices.shape
    inner = Mesh(
        mesh.devices.reshape(sections, fsdp // 4, 2, 2, rep // 2, 2),
        ("section",) + FSDP + REP,
    )
    weight = P("section", FSDP, None)
    vector = P("section", None, FSDP)
    tokens = P(REP, FSDP, None)
    both = P("section", REP, FSDP, None)
    return jax.shard_map(
        per_device,
        mesh=inner,
        in_specs=(
            tokens,
            tokens,
            P(REP, None),
            vector,
            vector,
            weight,
            vector,
            weight,
            weight,
            P("section", FSDP),
            weight,
            vector,
            vector,
        ),
        out_specs=(
            both,
            both,
            vector,
            vector,
            weight,
            vector,
            weight,
            weight,
            P("section", FSDP),
            weight,
            vector,
            vector,
        ),
        check_vma=False,
    )
```
